32 devices in a mesh: fsdp: 4 (over z), ctx: 4 (over x, core), tp: 2 (over y).
Axes of the slice: x: 2, y: 2, z: 4, core: 2. Of those that a mesh axis runs over, the one named last changes fastest.
Arguments:
- hidden_in: bfloat16 [4096, 2048], P(('fsdp', 'ctx')), may hold values from -6 to 6
- cotangent: bfloat16 [4096, 2048], P(('fsdp', 'ctx')), may hold values from -6 to 6
- routes: int32 [4096, 6], P(('fsdp', 'ctx')), may hold values from 0 to 15, all different within a row; in each aligned block of 256 rows (0 to 255, 256 to 511, ...) at most 128 rows name the same one
- gate_weights: float32 [4096, 6], P(('fsdp', 'ctx')), may hold values from 0.05 to 0.35
- gain_attn: bfloat16 [2048], P('fsdp'), may hold values from 0.5 to 1.5
- gain_latent: bfloat16 [512], P('fsdp'), may hold values from 0.5 to 1.5
- w_query: bfloat16 [2048, 3072], P('fsdp', 'tp'), may hold values from -0.1875 to 0.1875
- w_latent: bfloat16 [2048, 576], P('fsdp'), may hold values from -0.125 to 0.125
- w_expand: bfloat16 [512, 4096], P('fsdp', 'tp'), may hold values from -0.25 to 0.25
- w_out: bfloat16 [2048, 2048], P('tp', 'fsdp'), may hold values from -1.5 to 1.5
- gain_moe: bfloat16 [2048], P('fsdp'), may hold values from 0.5 to 1.5
- expert_gate: bfloat16 [16, 2048, 1408], P(None, 'fsdp', 'tp'), may hold values from -0.125 to 0.125
- expert_up: bfloat16 [16, 2048, 1408], P(None, 'fsdp', 'tp'), may hold values from -0.125 to 0.125
- expert_down: bfloat16 [16, 1408, 2048], P(None, 'tp', 'fsdp'), may hold values from -0.4375 to 0.4375
- shared_gate: bfloat16 [2048, 2816], P('fsdp', 'tp'), may hold values from -0.125 to 0.125
- shared_up: bfloat16 [2048, 2816], P('fsdp', 'tp'), may hold values from -0.125 to 0.125
- shared_down: bfloat16 [2816, 2048], P('tp', 'fsdp'), may hold values from -0.15625 to 0.15625
Outputs:
- layer_out: bfloat16 [4096, 2048], P(('fsdp', 'ctx'))
- input_grad: float32 [4096, 2048], P(('fsdp', 'ctx'))
- gates_grad: float32 [4096, 6], P(('fsdp', 'ctx'))
- gain_attn_grad: float32 [2048], P('fsdp')
- gain_latent_grad: float32 [512], P('fsdp')
- w_query_grad: float32 [2048, 3072], P('fsdp', 'tp')
- w_latent_grad: float32 [2048, 576], P('fsdp')
- w_expand_grad: float32 [512, 4096], P('fsdp', 'tp')
- w_out_grad: float32 [2048, 2048], P('tp', 'fsdp')
- gain_moe_grad: float32 [2048], P('fsdp')
- expert_gate_grad: float32 [16, 2048, 1408], P(None, 'fsdp', 'tp')
- expert_up_grad: float32 [16, 2048, 1408], P(None, 'fsdp', 'tp')
- expert_down_grad: float32 [16, 1408, 2048], P(None, 'tp', 'fsdp')
- shared_gate_grad: float32 [2048, 2816], P('fsdp', 'tp')
- shared_up_grad: float32 [2048, 2816], P('fsdp', 'tp')
- shared_down_grad: float32 [2816, 2048], P('tp', 'fsdp')
The draws below stay inside these ranges and needn't reach their ends.
Inputs may be any that keep to these rules, and one draw needn't show every extreme that they name: `routes`: each row names 6 different experts; in each aligned block of 256 rows (the rows of one device) no expert is named by more than 128 rows, a bound that some block reaches.
All inputs are finite; a program needn't handle non-finite values.
Results may differ from the reference program's by a relative error of at most 0.025.
Values may be sent and summed in bfloat16 or wider, within the bound.
No kernel may reach another device: no remote copies, remote signals or barrier semaphores. Data moves between devices by JAX's collectives and lax.ppermute only.
A program may use at most 512 MiB of HBM per device.

```python
import math
import jax
import jax.numpy as jnp
import numpy as np
from jax import lax

D = 2048
HEADS = 16
NOPE = 128
ROPE = 64
LATENT = 512
VHEAD = 128
FFN = 1408
EXPERTS = 16
TOPK = 6
TOK_DEV = 256
SHARED = 2816
CAPACITY = 128
SEQ_LEN = 1024
TOKENS = 4096
N_FSDP = 4


def steps_of(own_key, shape, cuts, low, high):
    loudness, own = 1.0, jax.random.fold_in(own_key, 6)
    for axis_at, parts in cuts:
        draws = jnp.exp(jax.random.uniform(jax.random.fold_in(own, axis_at), (parts,), jnp.float32, low / len(cuts), high / len(cuts)))
        loudness = loudness * jnp.repeat(draws, shape[axis_at] // parts).reshape([-1 if axis == axis_at else 1 for axis in range(len(shape))])
    return loudness


def routed_block(stream_key, own, number, rows, count, top, most, slope):
    ranking = jax.random.permutation(stream_key, count)
    heavy_load, common = portions_of(count, rows * top, most, slope, True), portions_of(count, rows * top, most, slope, False)
    places = jnp.arange(count)

    def named(lengths, turn):
        used = int((lengths > 0).sum())
        fixed = max(1, used // 4)
        moved = fixed + (places - fixed + turn * (used - fixed)) % max(1, count - fixed)
        return jnp.zeros((count,), jnp.int32).at[ranking[jnp.where(places < fixed, places, moved)]].set(jnp.asarray(lengths, jnp.int32))

    lengths = jnp.where(number % 4 == 0, named(heavy_load, number // 4), named(common, number - number // 4 - 1))
    mixed = jax.random.permutation(jax.random.fold_in(own, 3), count)
    source_of, taker = mixed[0:count // 2 * 2:2], mixed[1:count // 2 * 2:2]
    margin = jnp.minimum(lengths[source_of] - 1, most - lengths[taker]) // 2
    margin = jnp.where((source_of == ranking[0]) | (taker == ranking[0]) | (lengths[taker] == 0), 0, jnp.maximum(margin, 0))
    moved = jax.random.randint(jax.random.fold_in(own, 4), (count // 2,), 0, 1 << 20) % (margin + 1)
    lengths = lengths.at[source_of].add(-moved).at[taker].add(moved)
    members = jnp.searchsorted(jnp.cumsum(lengths), jnp.arange(rows * top), side="right").astype(jnp.int32)
    grid = members.reshape(top, rows).T
    grid = grid[jax.random.permutation(jax.random.fold_in(own, 1), rows)]
    turn = jax.random.randint(jax.random.fold_in(own, 2), (rows, 1), 0, top)
    return jnp.take_along_axis(grid, (jnp.arange(top)[None, :] + turn) % top, axis=1)


def portions_of(amount, total, bound, skew, full):
    weights = [(1 << 20) // math.isqrt(rank ** skew) + 1 for rank in range(1, amount + 1)]
    largest = bound if full else min(bound, max(-(-total // amount), total * weights[0] // sum(weights)))
    least = 1 if total - largest >= amount - 1 else 0
    given, rest = [largest] + [least] * (amount - 1), total - largest - least * (amount - 1)
    while rest > 0:
        free = [i for i in range(1, amount) if given[i] < largest] or [i for i in range(1, amount) if given[i] < bound]
        mass, budget = sum([weights[i] for i in free]), rest
        for i in free:
            more = min(bound - given[i], max(1, budget * weights[i] // mass), rest)
            given[i] = given[i] + more
            rest = rest - more
    return np.array(given)


def gaussian(own_key, dims, scale, most, cuts=(), held_as=jnp.bfloat16):
    entries = scale * jax.random.normal(own_key, dims, jnp.float32)
    if cuts:
        entries = entries * steps_of(own_key, dims, cuts, -0.22, 0.18)
    return jnp.clip(entries, -most, most).astype(held_as)


def setup_inputs(seed: int = 0) -> dict:
    streams_of = jax.random.split(jax.random.key(seed), 18)
    hidden_in = gaussian(streams_of[0], (TOKENS, D), 1.0, 6.0, ((0, 16),))
    cotangent = gaussian(streams_of[1], (TOKENS, D), 1.0, 6.0, ((0, 16),))
    routes_keys = jax.random.split(jax.random.fold_in(streams_of[2], 1), TOKENS // TOK_DEV)
    routes_turns = jax.random.permutation(jax.random.fold_in(streams_of[2], 3), TOKENS // TOK_DEV)
    routes = jax.vmap(lambda own, number: routed_block(jax.random.fold_in(streams_of[2], 2), own, number, TOK_DEV, EXPERTS, TOPK, CAPACITY, 1))(routes_keys, routes_turns).reshape((TOKENS, TOPK))
    gate_weights = jnp.clip(0.05 + 0.29999999 * jax.random.uniform(streams_of[3], (TOKENS, TOPK), jnp.float32) ** steps_of(streams_of[3], (TOKENS, TOPK), ((0, 16),), -0.2, 0.2), 0.05, 0.35)
    gain_attn = jnp.clip(1.0 + 0.1 * jax.random.normal(streams_of[4], (D,), jnp.float32), 0.5, 1.5).astype(jnp.bfloat16)
    gain_latent = jnp.clip(1.0 + 0.1 * jax.random.normal(streams_of[5], (LATENT,), jnp.float32), 0.5, 1.5).astype(jnp.bfloat16)
    w_query = gaussian(streams_of[6], (D, HEADS * (NOPE + ROPE)), (D // 2) ** -0.5, 0.1875, ((0, 4), (1, 2)))
    w_latent = gaussian(streams_of[7], (D, LATENT + ROPE), D ** -0.5, 0.125, ((0, 4),))
    w_expand = gaussian(streams_of[8], (LATENT, HEADS * (NOPE + VHEAD)), LATENT ** -0.5, 0.25, ((0, 4), (1, 2)))
    w_out = gaussian(streams_of[9], (HEADS * VHEAD, D), (max(HEADS * VHEAD // 128, 1)) ** -0.5, 1.5, ((0, 2), (1, 4)))
    gain_moe = jnp.clip(1.0 + 0.1 * jax.random.normal(streams_of[10], (D,), jnp.float32), 0.5, 1.5).astype(jnp.bfloat16)
    expert_gate = gaussian(streams_of[11], (EXPERTS, D, FFN), D ** -0.5, 0.125, ((1, 4), (2, 2)))
    expert_up = gaussian(streams_of[12], (EXPERTS, D, FFN), D ** -0.5, 0.125, ((1, 4), (2, 2)))
    expert_down = gaussian(streams_of[13], (EXPERTS, FFN, D), (FFN // 8) ** -0.5, 0.4375, ((1, 2), (2, 4)))
    shared_gate = gaussian(streams_of[14], (D, SHARED), D ** -0.5, 0.125, ((0, 4), (1, 2)))
    shared_up = gaussian(streams_of[15], (D, SHARED), D ** -0.5, 0.125, ((0, 4), (1, 2)))
    shared_down = gaussian(streams_of[16], (SHARED, D), (SHARED // 2) ** -0.5, 0.15625, ((0, 2), (1, 4)))
    return dict(hidden_in=hidden_in, cotangent=cotangent, routes=routes, gate_weights=gate_weights, gain_attn=gain_attn, gain_latent=gain_latent, w_query=w_query, w_latent=w_latent, w_expand=w_expand, w_out=w_out, gain_moe=gain_moe, expert_gate=expert_gate, expert_up=expert_up, expert_down=expert_down, shared_gate=shared_gate, shared_up=shared_up, shared_down=shared_down)


@jax.custom_vjp
def low(v):
    return lax.optimization_barrier(v.astype(jnp.bfloat16)).astype(jnp.float32)

@jax.custom_vjp
def low_back(v):
    return v

def low_keep(v):
    return (low(v), None)

def low_pass(kept, grad):
    return (grad,)

def back_keep(v):
    return (v, None)

def back_low(kept, grad):
    return (low(grad),)
low.defvjp(low_keep, low_pass)
low_back.defvjp(back_keep, back_low)
EPSILON = 1e-06
HIGHEST = lax.Precision.HIGHEST

def norm_rows(values, gain_vec):
    return values * lax.rsqrt(lax.optimization_barrier(jnp.mean(values * values, axis=-1, keepdims=True)) + EPSILON) * gain_vec

def angle_tables(position, width):
    half_width = width // 2
    frequency = jnp.exp(jnp.arange(half_width, dtype=jnp.float32) * (-2.0 * math.log(10000.0) / width))
    angles = position.astype(jnp.float32)[:, None] * frequency[None, :]
    return (jnp.cos(angles), jnp.sin(angles))

def rotate(values, cosine, sine_tab):
    half_width = values.shape[-1] // 2
    front_half = values[..., :half_width]
    back_half = values[..., half_width:]
    return jnp.concatenate([front_half * cosine - back_half * sine_tab, back_half * cosine + front_half * sine_tab], axis=-1)

def product(left_mat, right_mat):
    return jnp.dot(left_mat, right_mat, precision=HIGHEST)

def swiglu(gate_act, up_act):
    return gate_act * jax.nn.sigmoid(gate_act) * up_act

def sequence(hidden_in, routes, gate_weights, params):
    gain_attn, gain_latent, w_query, w_latent, w_expand, w_out, gain_moe, expert_gate, expert_up, expert_down, shared_gate, shared_up, shared_down = params
    length = hidden_in.shape[0]
    position = jnp.arange(length, dtype=jnp.int32)
    cosine, sine_tab = angle_tables(position, ROPE)
    normed = low(norm_rows(hidden_in, gain_attn))
    queries = low_back(product(normed, w_query)).reshape(length, HEADS, NOPE + ROPE)
    queries = low(jnp.concatenate([queries[..., :NOPE], rotate(queries[..., NOPE:], cosine[:, None, :], sine_tab[:, None, :])], axis=-1))
    latent_raw = low_back(product(normed, w_latent))
    latent = low(jnp.concatenate([norm_rows(latent_raw[:, :LATENT], gain_latent), rotate(latent_raw[:, LATENT:], cosine, sine_tab)], axis=1))
    expanded = low_back(low(product(latent[:, :LATENT], w_expand))).reshape(length, HEADS, NOPE + VHEAD)
    key_all = jnp.concatenate([expanded[..., :NOPE], jnp.broadcast_to(latent[:, None, LATENT:], (length, HEADS, ROPE))], axis=-1)
    values_all = expanded[..., NOPE:]
    block_rows = min(512, length)
    blocks = length // block_rows
    scaling = (NOPE + ROPE) ** (-0.5)

    def attend(element):
        query_blk, offset = element
        scores = jnp.einsum('qhd,khd->hqk', query_blk, key_all, precision=HIGHEST) * scaling
        scores = low_back(scores)
        row_pos = offset + jnp.arange(block_rows, dtype=jnp.int32)
        scores = jnp.where(position[None, None, :] <= row_pos[None, :, None], scores, -1e+30)
        exponent = jnp.exp(scores - lax.optimization_barrier(jnp.max(scores, axis=-1, keepdims=True)))
        attn_prob = exponent / lax.optimization_barrier(jnp.sum(exponent, axis=-1, keepdims=True))
        return jnp.einsum('hqk,khd->qhd', low(attn_prob), values_all, precision=HIGHEST)
    offsets = jnp.arange(blocks, dtype=jnp.int32) * block_rows
    heads_out = lax.map(jax.checkpoint(attend), (queries.reshape(blocks, block_rows, HEADS, NOPE + ROPE), offsets))
    heads_out = low_back(low(heads_out.reshape(length, HEADS * VHEAD)))
    middle = hidden_in + low_back(product(heads_out, w_out))
    normed_moe = low(norm_rows(middle, gain_moe))
    flat_expert = routes.reshape(-1).astype(jnp.int32)
    pieces = length // TOK_DEV
    onehot = (flat_expert[:, None] == jnp.arange(EXPERTS, dtype=jnp.int32)[None, :]).astype(jnp.int32)
    onehot = onehot.reshape(pieces, TOK_DEV * TOPK, EXPERTS)
    earlier = (jnp.cumsum(onehot, axis=1) - onehot).astype(jnp.int32)
    slot_in = lax.optimization_barrier(jnp.sum(earlier * onehot, axis=2)).reshape(-1).astype(jnp.int32)
    slot_idx = jnp.arange(length * TOPK, dtype=jnp.int32) // (TOK_DEV * TOPK) * CAPACITY + slot_in
    repeated = jnp.repeat(normed_moe, TOPK, axis=0)
    dispatch = jnp.zeros((EXPERTS, pieces * CAPACITY, D), normed_moe.dtype).at[flat_expert, slot_idx].add(repeated)
    gate_act = low_back(jnp.einsum('erd,edf->erf', dispatch, expert_gate, precision=HIGHEST))
    up_act = low_back(jnp.einsum('erd,edf->erf', dispatch, expert_up, precision=HIGHEST))
    hidden_e = low(swiglu(gate_act, up_act))
    expert_out = low_back(jnp.einsum('erf,efd->erd', hidden_e, expert_down, precision=HIGHEST))
    picked = expert_out[flat_expert, slot_idx].reshape(length, TOPK, D)
    routed = lax.optimization_barrier(jnp.sum(picked * gate_weights[:, :, None], axis=1))
    shared_g = low_back(product(normed_moe, shared_gate))
    shared_u = low_back(product(normed_moe, shared_up))
    shared_out = low_back(product(low(swiglu(shared_g, shared_u)), shared_down))
    return middle + routed + shared_out

def reference(hidden_in, cotangent, routes, gate_weights, gain_attn, gain_latent, w_query, w_latent, w_expand, w_out, gain_moe, expert_gate, expert_up, expert_down, shared_gate, shared_up, shared_down):
    params = tuple((weight_arr.astype(jnp.float32) for weight_arr in (gain_attn, gain_latent, w_query, w_latent, w_expand, w_out, gain_moe, expert_gate, expert_up, expert_down, shared_gate, shared_up, shared_down)))
    seq_routes = routes.reshape(N_FSDP, SEQ_LEN, TOPK)

    def forward(inputs, gates_in, weights):

        def one_sequence(element):
            return sequence(element[0], element[1], element[2], weights)
        outputs = lax.map(jax.checkpoint(one_sequence), (inputs.reshape(N_FSDP, SEQ_LEN, D), seq_routes, gates_in.reshape(N_FSDP, SEQ_LEN, TOPK)))
        return outputs.reshape(TOKENS, D)
    outputs, pullback = jax.vjp(forward, hidden_in.astype(jnp.float32), gate_weights.astype(jnp.float32), params)
    grad_in, grad_gates, grads = pullback(cotangent.astype(jnp.float32))
    return (outputs.astype(jnp.bfloat16), grad_in, grad_gates, grads[0], grads[1], grads[2], grads[3], grads[4], grads[5], grads[6], grads[7], grads[8], grads[9], grads[10], grads[11], grads[12])
```

```python
import math

import jax
import jax.numpy as jnp
from jax import lax
from jax.experimental import pallas as pl
from jax.experimental.pallas import tpu as pltpu
from jax.sharding import PartitionSpec as P

NOPE = 128
ROPE = 64
LATENT = 512
VHEAD = 128
EXPERTS = 16
TOPK = 6
CAPACITY = 128
EPSILON = 1e-06

f32 = jnp.float32
bf16 = jnp.bfloat16


def norm_rows(values, gain_vec):
    scales = lax.rsqrt(jnp.mean(values * values, axis=-1, keepdims=True) + EPSILON)
    return (values * scales * gain_vec, scales)


def norm_back(values, scales, gain_vec, gradient):
    weighted = gradient * gain_vec
    inner = jnp.mean(weighted * values, axis=-1, keepdims=True)
    return (
        scales * weighted - values * scales**3 * inner,
        jnp.sum(gradient * values * scales, axis=0),
    )


def angle_tables(position, width):
    half_width = width // 2
    frequency = jnp.exp(
        jnp.arange(half_width, dtype=f32) * (-2.0 * math.log(10000.0) / width)
    )
    angles = position.astype(f32)[:, None] * frequency[None, :]
    return (jnp.cos(angles), jnp.sin(angles))


def rotate(values, cosine, sine_tab):
    half_width = values.shape[-1] // 2
    front_half = values[..., :half_width]
    back_half = values[..., half_width:]
    return jnp.concatenate(
        [front_half * cosine - back_half * sine_tab, back_half * cosine + front_half * sine_tab],
        axis=-1,
    )


def rotate_back(gradient, cosine, sine_tab):
    return rotate(gradient, cosine, -sine_tab)


def swiglu_back(gate_act, up_act, grad_hidden):
    sigmoid_g = jax.nn.sigmoid(gate_act)
    grad_up = (grad_hidden * gate_act * sigmoid_g).astype(bf16)
    grad_gate = (grad_hidden * up_act * sigmoid_g * (1.0 + gate_act * (1.0 - sigmoid_g))).astype(
        bf16
    )
    return (grad_gate, grad_up)


def mm(left, right):
    return jnp.dot(left, right, preferred_element_type=f32)


def mm_nt(left, right):
    return lax.dot_general(left, right, (((1,), (1,)), ((), ())), preferred_element_type=f32)


def mm_tn(left, right):
    return lax.dot_general(left, right, (((0,), (0,)), ((), ())), preferred_element_type=f32)


def after(value, *earlier):
    return lax.optimization_barrier((value,) + earlier)[0]


def exchange(value, axis, bit):
    size = lax.axis_size(axis)
    return lax.ppermute(value, axis, [(a, a ^ bit) for a in range(size)])


def high_bits(size):
    bit = size // 2
    while bit >= 2:
        yield bit
        bit //= 2


def low_bits(size):
    bit = 1
    while bit < size:
        yield bit
        bit *= 2


def place(shape, dtype, parts, starts, axis):
    buffer = jnp.zeros(shape, dtype)
    for part, start in zip(parts, starts):
        buffer = lax.dynamic_update_slice_in_dim(buffer, part.astype(dtype), start, axis)
    return buffer


def slot_masks(row_ref, pieces, tokens):
    iota = lax.broadcasted_iota(jnp.int32, (CAPACITY, tokens), 0)
    return [iota == row_ref[a] for a in range(pieces)]


def one_hot(mask):
    return jnp.where(mask, 1.0, 0.0).astype(bf16)


def rows_kernel(pieces, fs, steps, groups, *refs):
    row_ref, ws_ref = refs[:2]
    xs, dys = refs[2 : 2 + 2 * groups], refs[2 + 2 * groups : 2 + 4 * groups]
    wg, wu = refs[2 + 4 * groups : 4 + 4 * groups]
    slots_ref, sdy_ref, gate_ref, up_ref, ds_ref, dsh_ref, xbuf, dybuf, sems = refs[
        4 + 4 * groups :
    ]
    ffn = gate_ref.shape[1]
    step = pl.program_id(0)
    slot = lax.rem(step, 2)
    width = xbuf.shape[4]
    tokens = xbuf.shape[2] * xbuf.shape[3]
    dpart = wg.shape[2]
    shp = ws_ref.shape[0] // 3
    per = steps // (2 * groups)

    def begin(at, into):
        for q in range(steps):

            @pl.when(at == q)
            def _(q=q):
                chunk, other = q // 2, q % 2
                which, c = 2 * (chunk // per) + other, chunk % per
                pltpu.make_async_copy(xs[which].at[:, :, c], xbuf.at[into], sems.at[into, 0]).start()
                pltpu.make_async_copy(
                    dys[which].at[:, :, c], dybuf.at[into], sems.at[into, 1]
                ).start()

    @pl.when(step == 0)
    def _():
        begin(step, 0)

    @pl.when(step + 1 < steps)
    def _():
        begin(step + 1, 1 - slot)

    pltpu.make_async_copy(xs[0].at[:, :, 0], xbuf.at[slot], sems.at[slot, 0]).wait()
    pltpu.make_async_copy(dys[0].at[:, :, 0], dybuf.at[slot], sems.at[slot, 1]).wait()
    masks = slot_masks(row_ref, pieces, tokens)
    for a in range(pieces):
        pick = one_hot(masks[a])
        of = slice(a * CAPACITY, (a + 1) * CAPACITY)
        slots_ref[of, :] = mm(pick, xbuf[slot, a].reshape(tokens, width)).astype(bf16)
        sdy_ref[of, :] = mm(pick, dybuf[slot, a].reshape(tokens, width)).astype(bf16)
    gate_act = up_act = None
    for s in range(fs):
        part = slots_ref[:, s * dpart : (s + 1) * dpart]
        g, u = mm_nt(part, wg[s, :ffn]), mm_nt(part, wu[s])
        gate_act = g if s == 0 else gate_act + g
        up_act = u if s == 0 else up_act + u
    gate_ref[...] = gate_act
    up_ref[...] = up_act
    flat = xbuf[slot].reshape(pieces * tokens, width)
    dflat = dybuf[slot].reshape(pieces * tokens, width)
    both = mm_nt(flat, ws_ref[: 2 * shp])
    sg, su = both[:, :shp], both[:, shp:]
    sd = mm_nt(dflat, ws_ref[2 * shp :])
    sig = 1.0 / (1.0 + jnp.exp(-sg))
    silu = sg * sig
    s_hid = (silu * su).astype(bf16)
    ds_up = (sd * silu).astype(bf16)
    ds_gate = (sd * su * sig * (1.0 + sg * (1.0 - sig))).astype(bf16)
    ds_ref[:, :shp] = ds_gate
    ds_ref[:, shp : 2 * shp] = ds_up
    ds_ref[:, 2 * shp :] = s_hid
    first = mm_tn(ds_ref[:, : 2 * shp], flat)
    second = mm_tn(s_hid, dflat)

    @pl.when(step == 0)
    def _():
        dsh_ref[: 2 * shp] = first
        dsh_ref[2 * shp :] = second

    @pl.when(step > 0)
    def _():
        dsh_ref[: 2 * shp] += first
        dsh_ref[2 * shp :] += second


def moe_rows(fs, ffn, xs, dys, slot_row, shared, gate_w, up_w):
    pieces, tp, per, n, width = xs[0].shape
    groups = len(xs) // 2
    tokens = tp * n
    steps = 2 * groups * per
    shp = shared.shape[0] // 3
    slots = pieces * CAPACITY
    once = pl.Buffered(buffer_count=1)

    def by_step(shape):
        return pl.BlockSpec(shape, lambda q: (q,) + (0,) * (len(shape) - 1))

    def fixed(shape):
        return pl.BlockSpec(shape, lambda q: (0,) * len(shape), pipeline_mode=once)

    total = steps * slots
    return pl.pallas_call(
        lambda *refs: rows_kernel(pieces, fs, steps, groups, *refs),
        grid=(steps,),
        in_specs=[by_step((pieces, 1, tokens)), fixed((3 * shp, width))]
        + [pl.BlockSpec(memory_space=pl.ANY)] * (4 * groups)
        + [fixed(gate_w.shape), fixed(up_w.shape)],
        out_specs=[
            by_step((slots, width)),
            by_step((slots, width)),
            by_step((slots, ffn)),
            by_step((slots, ffn)),
            by_step((pieces * tokens, 3 * shp)),
            fixed((3 * shp, width)),
        ],
        scratch_shapes=[
            pltpu.VMEM((2, pieces, tp, n, width), bf16),
            pltpu.VMEM((2, pieces, tp, n, width), bf16),
            pltpu.SemaphoreType.DMA((2, 2)),
        ],
        out_shape=[
            jax.ShapeDtypeStruct((total, width), bf16),
            jax.ShapeDtypeStruct((total, width), bf16),
            jax.ShapeDtypeStruct((total, ffn), f32),
            jax.ShapeDtypeStruct((total, ffn), f32),
            jax.ShapeDtypeStruct((steps * pieces * tokens, 3 * shp), bf16),
            jax.ShapeDtypeStruct((3 * shp, width), f32),
        ],
        compiler_params=pltpu.CompilerParams(vmem_limit_bytes=60 * 1024 * 1024),
        cost_estimate=pl.CostEstimate(flops=0, bytes_accessed=1_000_000, transcendentals=0),
        name="moe_rows",
    )(slot_row, shared, *xs, *dys, gate_w, up_w)


def back_kernel(pieces, fs, extra, tp_first, me_ref, *refs):
    sdy_ref, gate_ref, up_ref, row_ref, col_ref, wt_ref, ds_ref, ws_ref, wg, wu, wd = refs[:11]
    name_ref = refs[11]
    dg_ref, du_ref, hw_ref, keep_ref, send_ref = refs[12 + extra :]
    ffn = gate_ref.shape[1]
    n, width = keep_ref.shape[3], ws_ref.shape[1]
    half = lax.rem(pl.program_id(0), 2)
    tokens = row_ref.shape[2]
    dpart = wg.shape[2]
    shp = ws_ref.shape[0] // 3
    masks = slot_masks(row_ref, pieces, tokens)
    weight = jnp.concatenate(
        [
            jnp.sum(jnp.where(masks[a], wt_ref[a], 0.0), axis=1, keepdims=True)
            for a in range(pieces)
        ],
        axis=0,
    )
    dy_down = None
    for s in range(fs):
        d = mm_nt(sdy_ref[:, s * dpart : (s + 1) * dpart], wd[s])
        dy_down = d if s == 0 else dy_down + d
    gate_act, up_act = gate_ref[...], up_ref[...]
    sig = 1.0 / (1.0 + jnp.exp(-gate_act))
    silu = gate_act * sig
    hidden = (silu * up_act).astype(bf16).astype(f32)
    slot_grad = jnp.sum(hidden * dy_down, axis=1, keepdims=True)
    hw_ref[...] = (weight * hidden).astype(bf16)
    d_hidden = weight * dy_down
    du_ref[...] = (d_hidden * silu).astype(bf16)
    dg_ref[...] = (d_hidden * up_act * sig * (1.0 + gate_act * (1.0 - sig))).astype(bf16)
    across = lax.broadcasted_iota(jnp.int32, (tokens, CAPACITY), 1)
    picks = [one_hot(across == col_ref[a]) for a in range(pieces)]

    def write(a, at, value):
        for t in range(tokens // n):
            rows = value[t * n : (t + 1) * n]
            at_t = me_ref[0] ^ t
            index = (at_t, a) if tp_first else (a, at_t)

            @pl.when(half == 0)
            def _():
                keep_ref[index[0], index[1], 0, :, at] = rows

            @pl.when(half == 1)
            def _():
                send_ref[index[0], index[1], 0, :, at] = rows

    for s in range(fs):
        at = slice(s * dpart, (s + 1) * dpart)
        back = (
            mm(dg_ref[...], wg[s, :ffn]) + mm(du_ref[...], wu[s])
        ).astype(bf16)
        s_back = mm(ds_ref[:, : 2 * shp], ws_ref[: 2 * shp, at])
        for a in range(pieces):
            part = mm(picks[a], back[a * CAPACITY : (a + 1) * CAPACITY])
            write(a, at, (part + s_back[a * tokens : (a + 1) * tokens]).astype(bf16))
    spread = (slot_grad * name_ref[...]).astype(bf16)
    for a in range(pieces):
        part = mm(picks[a], spread[a * CAPACITY : (a + 1) * CAPACITY])
        write(a, slice(width, width + 128), part.astype(bf16))


def moe_back(
    first, chunks, tp, fs, tp_first, me, sdy, gate, up, slot_row, slot_col, weight, ds, shared, gate_w, up_w, down_w, name, big
):
    width = sdy.shape[1]
    all_pieces, _, tokens = slot_row.shape
    pieces = all_pieces // (2 * fs)
    ffn, dpart = down_w.shape[1:]
    shp = shared.shape[0] // 3
    slots = pieces * CAPACITY
    once = pl.Buffered(buffer_count=1)

    def by_step(shape):
        return pl.BlockSpec(shape, lambda q, me: (2 * first + q,) + (0,) * (len(shape) - 1))

    def fixed(shape):
        return pl.BlockSpec(shape, lambda q, me: (0,) * len(shape), pipeline_mode=once)

    n = tokens // tp
    outer = (tp, pieces) if tp_first else (pieces, tp)
    half_spec = pl.BlockSpec(outer + (1, n, width + 128), lambda q, me: (0, 0, q // 2, 0, 0))
    total = sdy.shape[0]
    half = jax.ShapeDtypeStruct(outer + (chunks, n, width + 128), bf16)
    return pl.pallas_call(
        lambda *refs: back_kernel(pieces, fs, len(big), tp_first, *refs),
        grid_spec=pltpu.PrefetchScalarGridSpec(
            num_scalar_prefetch=1,
            grid=(2 * chunks,),
            in_specs=[
                by_step((slots, width)),
                by_step((slots, ffn)),
                by_step((slots, ffn)),
                by_step((pieces, 1, tokens)),
                by_step((pieces, tokens, 1)),
                by_step((pieces, 1, tokens)),
                by_step((pieces * tokens, 3 * shp)),
                fixed((3 * shp, width)),
            ]
            + [fixed(gate_w.shape), fixed(up_w.shape), fixed((fs, ffn, dpart))]
            + [fixed((1, 128))]
            + [pl.BlockSpec(memory_space=pl.ANY)] * len(big),
            out_specs=[
                by_step((slots, ffn)),
                by_step((slots, ffn)),
                by_step((slots, ffn)),
                half_spec,
                half_spec,
            ],
        ),
        out_shape=[
            jax.ShapeDtypeStruct((total, ffn), bf16),
            jax.ShapeDtypeStruct((total, ffn), bf16),
            jax.ShapeDtypeStruct((total, ffn), bf16),
            half,
            half,
        ],
        input_output_aliases={13 + b: b for b in range(len(big))},
        compiler_params=pltpu.CompilerParams(vmem_limit_bytes=60 * 1024 * 1024),
        cost_estimate=pl.CostEstimate(flops=0, bytes_accessed=1_000_000, transcendentals=0),
        name="moe_back",
    )(me, sdy, gate, up, slot_row, slot_col, weight, ds, shared, gate_w, up_w, down_w, name, *big)


def out_kernel(pieces, fs, ctx_first, me_ref, hw_ref, col_ref, ds_ref, ws_ref, wd, keep_ref, send_ref):
    tokens = col_ref.shape[1]
    n = keep_ref.shape[3]
    half = lax.rem(pl.program_id(0), 2)
    dpart = wd.shape[2]
    across = lax.broadcasted_iota(jnp.int32, (tokens, CAPACITY), 1)
    picks = [one_hot(across == col_ref[a]) for a in range(pieces)]
    for s in range(fs):
        at = slice(s * dpart, (s + 1) * dpart)
        out = mm(hw_ref[...], wd[s]).astype(bf16)
        shared = mm(ds_ref[...], ws_ref[:, at])
        for a in range(pieces):
            part = mm(picks[a], out[a * CAPACITY : (a + 1) * CAPACITY])
            value = (part + shared[a * tokens : (a + 1) * tokens]).astype(bf16)
            for t in range(tokens // n):
                rows = value[t * n : (t + 1) * n]
                at_t = me_ref[0] ^ t
                index = (a, at_t) if ctx_first else (at_t, a)

                @pl.when(half == 0)
                def _():
                    keep_ref[index[0], index[1], 0, :, at] = rows

                @pl.when(half == 1)
                def _():
                    send_ref[index[0], index[1], 0, :, at] = rows


def moe_out(first, chunks, tp, fs, ctx_first, me, hw, slot_col, ds, shared, down_w):
    all_pieces, tokens, _ = slot_col.shape
    ffn, dpart = down_w.shape[1:]
    width = shared.shape[1]
    shp = shared.shape[0] // 3
    pieces = all_pieces // (2 * fs)
    n = tokens // tp
    once = pl.Buffered(buffer_count=1)
    slots = 2 * chunks * pieces * CAPACITY
    outer = (pieces, tp) if ctx_first else (tp, pieces)
    half_spec = pl.BlockSpec(outer + (1, n, width), lambda q, me: (0, 0, q // 2, 0, 0))
    return pl.pallas_call(
        lambda *refs: out_kernel(pieces, fs, ctx_first, *refs),
        grid_spec=pltpu.PrefetchScalarGridSpec(
            num_scalar_prefetch=1,
            grid=(2 * chunks,),
            in_specs=[
                pl.BlockSpec((pieces * CAPACITY, ffn), lambda q, me: (2 * first + q, 0)),
                pl.BlockSpec((pieces, tokens, 1), lambda q, me: (2 * first + q, 0, 0)),
                pl.BlockSpec((pieces * tokens, shp), lambda q, me: (2 * first + q, 2)),
                pl.BlockSpec((shp, width), lambda q, me: (2, 0), pipeline_mode=once),
                pl.BlockSpec((fs, ffn, dpart), lambda q, me: (0, 0, 0), pipeline_mode=once),
            ],
            out_specs=[half_spec, half_spec],
        ),
        out_shape=[jax.ShapeDtypeStruct(outer + (chunks, n, width), bf16)] * 2,
        compiler_params=pltpu.CompilerParams(vmem_limit_bytes=40 * 1024 * 1024),
        cost_estimate=pl.CostEstimate(flops=0, bytes_accessed=1_000_000, transcendentals=0),
        name="moe_out",
    )(me, hw, slot_col, ds, shared, down_w)


def turned(front, back, cosine, sine):
    return front * cosine - back * sine, back * cosine + front * sine


def attend_kernel(hd, normed, query, latent, expand, out_w, gain, cos, sin, posq, posk, *outs):
    keep_ref, send_ref, raw_ref, low_ref, q_ref, ex_ref, prob_ref, heads_ref = outs
    length = normed.shape[0]
    q_width, kv_width, turn = NOPE + ROPE, NOPE + VHEAD, ROPE // 2
    scaling = q_width ** (-0.5)
    q_raw = mm_nt(normed[...], query[...])
    for h in range(hd):
        at = h * q_width
        q_ref[:, at : at + NOPE] = q_raw[:, at : at + NOPE].astype(bf16)
        front, back = q_raw[:, at + NOPE : at + NOPE + turn], q_raw[:, at + NOPE + turn : at + q_width]
        front, back = turned(front, back, cos[...], sin[...])
        q_ref[:, at + NOPE : at + NOPE + turn] = front.astype(bf16)
        q_ref[:, at + NOPE + turn : at + q_width] = back.astype(bf16)
    raw = mm_nt(normed[...], latent[...])
    raw_ref[...] = raw
    body = raw[:, :LATENT]
    scales = lax.rsqrt(jnp.mean(body * body, axis=-1, keepdims=True) + EPSILON)
    low_ref[:, :LATENT] = (body * scales * gain[...]).astype(bf16)
    front, back = turned(raw[:, LATENT : LATENT + turn], raw[:, LATENT + turn :], cos[...], sin[...])
    low_ref[:, LATENT : LATENT + turn] = front.astype(bf16)
    low_ref[:, LATENT + turn :] = back.astype(bf16)
    ex_ref[...] = mm(low_ref[:, :LATENT], expand[...]).astype(bf16)
    rope = low_ref[:, LATENT:]
    block = min(256, length)
    for h in range(hd):
        at, kv = h * q_width, h * kv_width
        keys, vals = ex_ref[:, kv : kv + NOPE], ex_ref[:, kv + NOPE : kv + kv_width]
        for r in range(0, length, block):
            rows = slice(r, r + block)
            scores = mm_nt(q_ref[rows, at : at + NOPE], keys)
            scores = (scores + mm_nt(q_ref[rows, at + NOPE : at + q_width], rope)) * scaling
            scores = jnp.where(posk[...] <= posq[rows, :], scores, -1e30)
            exponent = jnp.exp(scores - jnp.max(scores, axis=-1, keepdims=True))
            total = jnp.sum(exponent, axis=-1, keepdims=True)
            prob = (exponent / total).astype(bf16)
            prob_ref[h, rows, :] = prob
            heads_ref[rows, h * VHEAD : (h + 1) * VHEAD] = mm(prob, vals).astype(bf16)
    keep_ref[...] = mm(heads_ref[: length // 2], out_w[...]).astype(bf16)
    send_ref[...] = mm(heads_ref[length // 2 :], out_w[...]).astype(bf16)


def whole_call(body, operands, out_shape, name):
    return pl.pallas_call(
        body,
        in_specs=[pl.BlockSpec(memory_space=pltpu.VMEM)] * len(operands),
        out_specs=[pl.BlockSpec(memory_space=pltpu.VMEM)] * len(out_shape),
        out_shape=[jax.ShapeDtypeStruct(shape, dtype) for shape, dtype in out_shape],
        compiler_params=pltpu.CompilerParams(vmem_limit_bytes=60 * 1024 * 1024),
        cost_estimate=pl.CostEstimate(flops=0, bytes_accessed=1_000_000, transcendentals=0),
        name=name,
    )(*operands)


def attend(hd, normed, query, latent, expand, out_w, gain, cos, sin, position):
    length, width = normed.shape
    half = length // 2
    operands = (
        normed,
        query,
        latent,
        expand,
        out_w,
        gain[None],
        cos,
        sin,
        position[:, None],
        position[None],
    )
    out_shape = [
        ((half, width), bf16),
        ((half, width), bf16),
        ((length, LATENT + ROPE), f32),
        ((length, LATENT + ROPE), bf16),
        ((length, hd * (NOPE + ROPE)), bf16),
        ((length, hd * (NOPE + VHEAD)), bf16),
        ((hd, length, length), bf16),
        ((length, hd * VHEAD), bf16),
    ]
    return whole_call(lambda *refs: attend_kernel(hd, *refs), operands, out_shape, "attend")


def attend_back_kernel(hd, grad, out_w, prob, heads, ex, low, q, cos, sin, query, expand, *outs):
    keep_ref, send_ref, dq_ref, dex_ref = outs
    length, width = grad.shape
    half = length // 2
    q_width, kv_width, turn = NOPE + ROPE, NOPE + VHEAD, ROPE // 2
    scaling = q_width ** (-0.5)
    d_heads = mm_nt(grad[...], out_w[...]).astype(bf16)
    rope = low[:, LATENT:]
    block = min(256, length)
    d_rope = None
    for h in range(hd):
        at, kv = h * q_width, h * kv_width
        of = slice(h * VHEAD, (h + 1) * VHEAD)
        keys, vals = ex[:, kv : kv + NOPE], ex[:, kv + NOPE : kv + kv_width]
        d_key = d_kr = d_val = None
        for r in range(0, length, block):
            rows = slice(r, r + block)
            d_out = d_heads[rows, of]
            inner = jnp.sum(
                d_out.astype(f32) * heads[rows, of].astype(f32), axis=-1, keepdims=True
            )
            p = prob[h, rows, :]
            d_scores = (p.astype(f32) * (mm_nt(d_out, vals) - inner)).astype(bf16)
            dq_ref[rows, at : at + NOPE] = (mm(d_scores, keys) * scaling).astype(bf16)
            d_turn = mm(d_scores, rope) * scaling
            front, back = turned(d_turn[:, :turn], d_turn[:, turn:], cos[rows, :], -sin[rows, :])
            dq_ref[rows, at + NOPE : at + NOPE + turn] = front.astype(bf16)
            dq_ref[rows, at + NOPE + turn : at + q_width] = back.astype(bf16)
            one = mm_tn(d_scores, q[rows, at : at + NOPE])
            two = mm_tn(d_scores, q[rows, at + NOPE : at + q_width])
            three = mm_tn(p, d_out)
            d_key = one if r == 0 else d_key + one
            d_kr = two if r == 0 else d_kr + two
            d_val = three if r == 0 else d_val + three
        dex_ref[:, kv : kv + NOPE] = (d_key * scaling).astype(bf16)
        dex_ref[:, kv + NOPE : kv + kv_width] = d_val.astype(bf16)
        d_rope = d_kr if h == 0 else d_rope + d_kr
    d_rope = (d_rope * scaling).astype(bf16)
    for ref, rows in ((send_ref, slice(half, length)), (keep_ref, slice(0, half))):
        ref[:, :width] = mm(dq_ref[rows, :], query[...]).astype(bf16)
        ref[:, width : width + LATENT] = mm_nt(dex_ref[rows, :], expand[...]).astype(bf16)
        ref[:, width + LATENT :] = d_rope[rows]


def attend_back(hd, grad, out_w, prob, heads, ex, low, q, cos, sin, query, expand):
    length, width = grad.shape
    cols = width + LATENT + ROPE
    operands = (grad, out_w, prob, heads, ex, low, q, cos, sin, query, expand)
    out_shape = [
        ((length // 2, cols), bf16),
        ((length // 2, cols), bf16),
        (q.shape, bf16),
        (ex.shape, bf16),
    ]
    return whole_call(
        lambda *refs: attend_back_kernel(hd, *refs), operands, out_shape, "attend_back"
    )


def attend_weights_kernel(grad, heads, dq, normed, dex, low, dw_ref, de_ref):
    fs, _, dpart = dw_ref.shape
    first = heads.shape[1]
    for z in range(fs):
        at = slice(z * dpart, (z + 1) * dpart)
        dw_ref[z, :first] = mm_tn(heads[...], grad[:, at]).astype(bf16)
        dw_ref[z, first:] = mm_tn(dq[...], normed[:, at]).astype(bf16)
    de_ref[...] = mm_tn(low[:, :LATENT], dex[...]).astype(bf16)


def attend_weights(fs, grad, heads, dq, normed, dex, low):
    rows = heads.shape[1] + dq.shape[1]
    out_shape = [((fs, rows, grad.shape[1] // fs), bf16), ((LATENT, dex.shape[1]), bf16)]
    return whole_call(
        attend_weights_kernel, (grad, heads, dq, normed, dex, low), out_shape, "attend_weights"
    )


def weight_grads(left, right, fs, more=None, sh=0):
    slots, ffn = left.shape
    dpart = right.shape[1] // fs
    extra = 3 * sh if more is not None else 0
    once = pl.Buffered(buffer_count=1)

    def body(left_ref, right_ref, *refs):
        out_ref = refs[-1]
        out_ref[0, :ffn] = mm_tn(left_ref[...], right_ref[...]).astype(bf16)
        if more is not None:
            shp = more.shape[0] // 3
            for b in range(3):
                out_ref[0, ffn + b * sh : ffn + (b + 1) * sh] = refs[0][
                    b * shp : b * shp + sh
                ].astype(bf16)

    in_specs = [
        pl.BlockSpec((slots, ffn), lambda z: (0, 0), pipeline_mode=once),
        pl.BlockSpec((slots, dpart), lambda z: (0, z)),
    ]
    operands = [left, right]
    if more is not None:
        in_specs.append(pl.BlockSpec((more.shape[0], dpart), lambda z: (0, z)))
        operands.append(more)
    return pl.pallas_call(
        body,
        grid=(fs,),
        in_specs=in_specs,
        out_specs=pl.BlockSpec((1, ffn + extra, dpart), lambda z: (z, 0, 0)),
        out_shape=jax.ShapeDtypeStruct((fs, ffn + extra, dpart), bf16),
        compiler_params=pltpu.CompilerParams(vmem_limit_bytes=50 * 1024 * 1024),
        cost_estimate=pl.CostEstimate(flops=0, bytes_accessed=1_000_000, transcendentals=0),
        name="weight_grads",
    )(*operands)


def assemble(blocks, dest, count, rows):
    each, _, cols = blocks[0].shape
    parts = len(blocks)

    def body(dest_ref, *refs):
        step = pl.program_id(0)
        for q in range(parts):

            @pl.when(step // each == q)
            def _(q=q):
                refs[parts][...] = refs[q][...].astype(f32)

    def source(q):
        return pl.BlockSpec(
            (1, rows, cols), lambda g, dest: (jnp.clip(g - q * each, 0, each - 1), 0, 0)
        )

    return pl.pallas_call(
        body,
        grid_spec=pltpu.PrefetchScalarGridSpec(
            num_scalar_prefetch=1,
            grid=(parts * each,),
            in_specs=[source(q) for q in range(parts)],
            out_specs=pl.BlockSpec((1, rows, cols), lambda g, dest: (dest[g], 0, 0)),
        ),
        out_shape=jax.ShapeDtypeStruct((count, rows, cols), f32),
        compiler_params=pltpu.CompilerParams(vmem_limit_bytes=40 * 1024 * 1024),
        cost_estimate=pl.CostEstimate(flops=0, bytes_accessed=1_000_000, transcendentals=0),
        name="assemble",
    )(dest, *blocks)


def local(
    hidden_in,
    cotangent,
    routes,
    gate_weights,
    gain_attn,
    gain_latent,
    w_query,
    w_latent,
    w_expand,
    w_out,
    gain_moe,
    expert_gate,
    expert_up,
    expert_down,
    shared_gate,
    shared_up,
    shared_down,
):
    fs, cx, tp = lax.axis_size("fsdp"), lax.axis_size("ctx"), lax.axis_size("tp")
    i, j, k = lax.axis_index("fsdp"), lax.axis_index("ctx"), lax.axis_index("tp")
    rows_dev, width = hidden_in.shape
    n = rows_dev // tp
    length = rows_dev * cx
    dpart = width // fs
    q_width = NOPE + ROPE
    kv_width = NOPE + VHEAD
    heads_dev = w_out.shape[0] // VHEAD
    groups = min(cx, heads_dev)
    share = cx // groups
    hd = heads_dev // groups
    group = j // share
    lead = j % share == 0
    scaling = q_width ** (-0.5)
    assert EXPERTS == fs * cx

    members = [0]
    for bit in list(high_bits(cx)) + [1]:
        members = members + [m ^ bit for m in members]
    place_of = [members.index(m) for m in range(cx)]

    def spot(m):
        return jnp.asarray(place_of, jnp.int32)[m]

    def spread_ctx(cur):
        for bit in high_bits(cx):
            cur = jnp.concatenate([cur, exchange(cur, "ctx", bit)], axis=0)
        return cur

    def spread_core(cur):
        return jnp.concatenate([cur, exchange(cur, "ctx", 1)], axis=0)

    def spread_tp(cur):
        for bit in low_bits(tp):
            cur = jnp.concatenate([cur, exchange(cur, "tp", bit)], axis=1)
        return cur

    def gather_halves(own, ctx_first):
        cur = own[None, None]
        cur = spread_tp(spread_ctx(cur)) if ctx_first else spread_ctx(spread_tp(cur))
        return cur, exchange(cur, "ctx", 1)

    def gather_plane(own, ctx_first=True):
        return jnp.concatenate(gather_halves(own, ctx_first), axis=0)

    def gather_ctx(own):
        return spread_core(spread_ctx(own[None]))

    def over_ctx(stack):
        blocks = [stack]
        for bit in list(high_bits(cx)) + [1]:
            blocks = blocks + [exchange(block, "ctx", bit) for block in blocks]
        return blocks

    def reduce_core(keep, send):
        return (keep.astype(f32) + exchange(send, "ctx", 1).astype(f32)).astype(bf16)

    def reduce_lead(cur, axis):
        bits = low_bits(tp) if axis == "tp" else high_bits(cx)
        for bit in sorted(bits, reverse=True):
            at = cur.shape[0] // 2
            other = exchange(cur[at:], axis, bit)
            cur = (cur[:at].astype(f32) + other.astype(f32)).astype(bf16)
        return cur[0]

    def reduce_plane(keep, send, *pins):
        cols = keep.shape[-1]

        def lead_tp(v):
            return v.astype(bf16).reshape(cx // 2, tp, n, cols).transpose(1, 0, 2, 3)

        cur = reduce_core(lead_tp(keep), lead_tp(send))
        cur = after(cur, *pins) if pins else cur
        return reduce_lead(reduce_lead(cur, "tp"), "ctx").astype(f32)

    def rel_tp(value):
        blocks = value.reshape((tp, n) + value.shape[1:])
        return jnp.concatenate(
            [lax.dynamic_index_in_dim(blocks, k ^ t, 0, keepdims=False) for t in range(tp)], axis=0
        )

    def own_rows(value):
        return lax.dynamic_slice_in_dim(value, k * n, n, 0)

    def home_sum(value):
        cur, bit = value, 1
        while bit < fs:
            cur = cur.reshape((cur.shape[0] // 2, 2) + cur.shape[1:])
            mine = (i // bit) % 2
            send = lax.dynamic_index_in_dim(cur, 1 - mine, 1, keepdims=False).astype(bf16)
            keep = lax.dynamic_index_in_dim(cur, mine, 1, keepdims=False)
            cur = keep.astype(f32) + exchange(send, "fsdp", bit).astype(f32)
            bit *= 2
        return cur[0]

    def turn(value):
        return lax.all_to_all(value, "fsdp", 0, 0)

    hid_rel = rel_tp(hidden_in)
    x_rel = hid_rel[:n].astype(f32)
    hid_all = gather_ctx(hid_rel).reshape(length, width)
    row = jnp.arange(n, dtype=jnp.int32)
    pos_rel = jnp.concatenate(
        [(j ^ m) * rows_dev + (k ^ t) * n + row for m in members for t in range(tp)]
    )
    cos_rel, sin_rel = angle_tables(pos_rel, ROPE)
    hid_all = after(hid_all, cos_rel, sin_rel)

    lat_cols = w_latent.shape[1] // cx
    query_own = lax.dynamic_slice_in_dim(w_query, group * hd * q_width, hd * q_width, 1)
    latent_own = lax.dynamic_slice_in_dim(w_latent.T, j * lat_cols, lat_cols, 0)
    expand_own = lax.dynamic_slice_in_dim(w_expand, group * hd * kv_width, hd * kv_width, 1)
    out_own = lax.dynamic_slice_in_dim(w_out, group * hd * VHEAD, hd * VHEAD, 0)
    lat_part = gain_latent.shape[0]
    gate_high = lax.reduce_precision(gate_weights, 8, 7)
    gate_low = (gate_weights - gate_high).astype(bf16)
    small = jnp.concatenate(
        [routes.T.astype(bf16), gate_high.T.astype(bf16), gate_low.T], axis=0
    )
    small_rows = -(-small.size // dpart)
    small = rel_tp(small.T).T.reshape(-1)
    small = jnp.pad(small, (0, small_rows * dpart - small.shape[0])).reshape(small_rows, dpart)
    extra = jnp.concatenate(
        [
            gain_attn[None],
            gain_moe[None],
            jnp.pad(gain_latent, (0, dpart - lat_part))[None],
            small,
        ],
        axis=0,
    )
    extra = jnp.pad(extra, ((0, -extra.shape[0] % 16), (0, 0)))
    first_pack = jnp.concatenate([query_own.T, latent_own, extra], axis=0)
    first_pack = after(lax.all_gather(first_pack, "fsdp", axis=0), hid_all)
    q_cols = hd * q_width
    query_t = first_pack[:, :q_cols].transpose(1, 0, 2).reshape(q_cols, width)
    latent_t = first_pack[:, q_cols : q_cols + lat_cols].transpose(1, 0, 2)
    latent_t = gather_ctx(latent_t.reshape(lat_cols, width))
    latent_t = place(
        (cx * lat_cols, width), bf16, list(latent_t), [(j ^ m) * lat_cols for m in members], 0
    )
    extra = first_pack[:, q_cols + lat_cols :]
    gain_norm = extra[:, 0].reshape(-1).astype(f32)
    gain_mix = extra[:, 1].reshape(-1).astype(f32)
    gain_lat = extra[:, 2, :lat_part].reshape(-1).astype(f32)
    small = extra[:, 3 : 3 + small_rows].reshape(fs, -1)[:, : 3 * TOPK * rows_dev]
    small = gather_ctx(small.reshape(fs, 3 * TOPK, rows_dev))
    small = small.transpose(1, 0, 2, 3).reshape(fs * cx, 3 * TOPK, rows_dev).astype(f32)
    ex_rows = expand_own.size // dpart
    second_pack = lax.all_gather(
        after(
            jnp.concatenate([expand_own.reshape(ex_rows, dpart), out_own], axis=0), first_pack
        ),
        "fsdp",
        axis=0,
    )
    second_pack = after(second_pack, latent_t)
    expand_w = second_pack[:, :ex_rows].reshape(-1, hd * kv_width)
    output_w = second_pack[:, ex_rows:].transpose(1, 0, 2).reshape(hd * VHEAD, width)

    dy_own = own_rows(cotangent)
    dy_seqs = lax.all_gather(after(dy_own, second_pack), "fsdp", axis=0)

    sh = shared_gate.shape[1] // (cx * fs)
    shp = -(-sh // 128) * 128
    ffn = expert_down.shape[1]
    cut = j * fs * sh
    gate_w = jnp.concatenate(
        [
            lax.dynamic_slice_in_dim(expert_gate.transpose(0, 2, 1), j * fs, fs, 0),
            lax.dynamic_slice_in_dim(shared_gate, cut, fs * sh, 1).T.reshape(fs, sh, dpart),
            lax.dynamic_slice_in_dim(shared_up, cut, fs * sh, 1).T.reshape(fs, sh, dpart),
            lax.dynamic_slice_in_dim(shared_down, cut, fs * sh, 0).reshape(fs, sh, dpart),
        ],
        axis=1,
    )
    gate_w = turn(after(gate_w, second_pack))
    shared_w = gate_w[:, ffn:].reshape(fs, 3, sh, dpart).transpose(1, 2, 0, 3)
    shared_w = jnp.pad(shared_w.reshape(3, sh, width), ((0, 0), (0, shp - sh), (0, 0)))
    shared_w = shared_w.reshape(3 * shp, width)

    normed, attn_scale = norm_rows(hid_all.astype(f32), gain_norm)
    normed_all = normed.astype(bf16)
    keep, send, latent_raw, latent_low, queries, expanded, attn_prob, heads_out = attend(
        hd, normed_all, query_t, latent_t, expand_w, output_w, gain_lat, cos_rel, sin_rel, pos_rel
    )
    half = length // 2

    def leading(value):
        return value if share == 1 else jnp.where(lead, value, jnp.zeros((), value.dtype))

    attn_sum = reduce_plane(leading(keep), leading(send))
    middle = x_rel + attn_sum
    normed_moe, moe_scale = norm_rows(middle, gain_mix)
    moe_low = normed_moe.astype(bf16)

    per = fs // 2 if fs > 1 else 1
    row_seqs = lax.all_gather(moe_low, "fsdp", axis=0)

    def to_all(seqs, *pins):
        halves = []
        for g in range(fs // per):
            cur = seqs[g * per : (g + 1) * per][None, None]
            if g % 2 == 0:
                cur = spread_ctx(cur)
                cur = spread_tp(after(cur, *pins) if pins else cur)
            else:
                cur = spread_tp(cur)
                cur = spread_ctx(after(cur, *pins) if pins else cur)
            halves += [cur, exchange(cur, "ctx", 1)]
        return halves

    dy_halves = to_all(after(dy_seqs, middle), gate_w, moe_low)
    up_w = turn(
        after(lax.dynamic_slice_in_dim(expert_up.transpose(0, 2, 1), j * fs, fs, 0), row_seqs)
    )
    row_halves = to_all(after(row_seqs, *dy_halves[::2]))
    down_w = turn(after(lax.dynamic_slice_in_dim(expert_down, j * fs, fs, 0), up_w))

    expert = (j * fs + i).astype(f32)
    named = small[:, :TOPK] == expert
    chosen = jnp.any(named, axis=1).astype(f32)
    gates_all = small[:, TOPK : 2 * TOPK] + small[:, 2 * TOPK :]
    weight = jnp.sum(jnp.where(named, gates_all, 0.0), axis=1)
    ahead = (
        jnp.arange(rows_dev, dtype=jnp.int32)[:, None]
        < jnp.arange(rows_dev, dtype=jnp.int32)[None, :]
    ).astype(bf16)
    earlier = mm(chosen.astype(bf16), ahead).astype(jnp.int32)
    slot_of = jnp.where(chosen > 0.5, earlier, -1).reshape(fs * cx, 1, rows_dev)
    weight = weight.reshape(fs * cx, 1, rows_dev)
    slot_col = slot_of.reshape(fs * cx, rows_dev, 1)

    all_slots, all_dy, gate_act, up_act, shared_ds, d_shared = moe_rows(
        fs, ffn, row_halves, dy_halves, slot_of, shared_w, gate_w, up_w
    )
    me = jnp.zeros((1,), jnp.int32)

    name = (jnp.arange(128, dtype=jnp.int32) == j * fs + i).astype(f32)[None]
    big, flows = [], []
    dy_in = all_dy
    for g in range(fs // per):
        results = moe_back(
            g * per,
            per,
            tp,
            fs,
            g % 2 == 0,
            me,
            dy_in,
            gate_act,
            up_act,
            slot_of,
            slot_col,
            weight,
            shared_ds,
            shared_w,
            gate_w,
            up_w,
            down_w,
            name,
            big,
        )
        big = list(results[:3])
        dy_in = after(all_dy, results[4])
        flows.append(reduce_core(results[3], results[4]))
    all_dg, all_du, all_hw = big

    def split_cols(value):
        return value.reshape(value.shape[0], fs, dpart).transpose(1, 0, 2)

    d_gate_w = weight_grads(after(all_dg, *flows), all_slots, fs)
    gate_back = turn(d_gate_w)
    firsts = [reduce_lead(flow, "ctx" if g % 2 else "tp") for g, flow in enumerate(flows)]
    d_up_w = weight_grads(after(all_du, d_gate_w), all_slots, fs)
    out_args = (slot_col, shared_ds, shared_w, down_w)
    outs = [moe_out(0, per, tp, fs, False, me, after(all_hw, d_up_w), *out_args)]
    firsts = [after(flow, d_up_w, *outs[0]) for flow in firsts]
    seconds = [reduce_lead(flow, "tp" if g % 2 else "ctx") for g, flow in enumerate(firsts)]
    d_down_w = weight_grads(after(all_hw, *firsts), all_dy, fs, d_shared, sh)
    for g in range(1, fs // per):
        outs.append(
            moe_out(g * per, per, tp, fs, g % 2 == 1, me, after(all_hw, d_down_w), *out_args)
        )
    home = jnp.concatenate([after(flow, *outs[-1]) for flow in seconds], axis=0)
    gate_back = after(gate_back, home)
    gate_blocks = lax.all_gather(gate_back, "ctx", axis=0)
    out_flows = [
        reduce_lead(after(reduce_core(keep, send), home), "ctx" if g % 2 else "tp")
        for g, (keep, send) in enumerate(outs)
    ]
    up_back = turn(after(d_up_w, gate_back))
    home_own = after(home_sum(after(home, gate_back)), *out_flows)
    grad_total, gate_cols = home_own[:, :width], home_own[:, width:]
    in_order = jnp.arange(EXPERTS, dtype=jnp.int32)

    def lay_out(blocks):
        return assemble([blocks.reshape(EXPERTS, -1, dpart)], in_order, EXPERTS, ffn)

    grad_mid_norm, d_gain_moe = norm_back(middle, moe_scale, gain_mix, grad_total)
    grad_mid = dy_own.astype(f32) + grad_mid_norm
    grad_low = grad_mid.astype(bf16)
    grad_all = gather_plane(grad_low).reshape(length, width)

    grad_all = after(grad_all, up_back)
    up_blocks = lax.all_gather(after(up_back, grad_all), "ctx", axis=0)
    down_back = turn(after(d_down_w, grad_all))
    out_flows = [
        reduce_lead(after(flow, grad_all), "tp" if g % 2 else "ctx")
        for g, flow in enumerate(out_flows)
    ]
    out_home = jnp.concatenate(out_flows, axis=0)
    gate_shards = lay_out(gate_blocks)
    keep, send, grad_q, grad_expanded = attend_back(
        hd,
        grad_all,
        output_w,
        attn_prob,
        heads_out,
        expanded,
        latent_low,
        queries,
        cos_rel,
        sin_rel,
        query_t,
        expand_w,
    )
    summed = after(reduce_plane(leading(keep), leading(send)), down_back, gate_shards, out_home)
    grad_latent_own = summed[:, width:]
    d_attn, d_w_expand = attend_weights(
        fs, grad_all, heads_out, after(grad_q, send), normed_all, grad_expanded, latent_low
    )
    up_shards = lay_out(up_blocks)
    latent_scale = lax.rsqrt(
        jnp.mean(latent_raw[:n, :LATENT] ** 2, axis=-1, keepdims=True) + EPSILON
    )
    grad_lat_raw, d_gain_latent = norm_back(
        latent_raw[:n, :LATENT], latent_scale, gain_lat, grad_latent_own[:, :LATENT]
    )
    grad_kv_raw = jnp.concatenate(
        [grad_lat_raw, rotate_back(grad_latent_own[:, LATENT:], cos_rel[:n], sin_rel[:n])], axis=1
    ).astype(bf16)
    grad_normed = summed[:, :width] + mm(grad_kv_raw, latent_t)
    out_total = home_sum(after(out_home, summed))
    down_blocks = lax.all_gather(after(down_back, summed), "ctx", axis=0)
    grad_x_norm, d_gain_attn = norm_back(x_rel, attn_scale[:n], gain_norm, grad_normed)
    input_own = after((grad_mid + grad_x_norm).astype(bf16), up_shards)
    input_grad = rel_tp(spread_tp(input_own[None, None]).reshape(rows_dev, width)).astype(f32)

    out_own_rows = (middle + out_total).astype(bf16)
    layer_out = rel_tp(spread_tp(out_own_rows[None, None]).reshape(rows_dev, width))

    gate_cols = spread_tp(gate_cols[:, :EXPERTS][None, None]).reshape(rows_dev, EXPERTS)
    gate_cols = rel_tp(gate_cols)
    experts = jnp.arange(EXPERTS, dtype=jnp.int32)
    gates_grad = jnp.sum(
        jnp.where(routes[:, :, None] == experts, gate_cols[:, None, :], 0.0), axis=-1
    )

    kv_all = gather_plane(grad_kv_raw).reshape(length, -1)
    d_w_latent = mm_tn(
        lax.dynamic_slice_in_dim(kv_all, j * lat_cols, lat_cols, 1), normed_all
    ).astype(bf16)

    def attn_shards(parts):
        return over_ctx(home_sum(after(jnp.concatenate(parts, axis=1), down_back)).astype(bf16))

    ex_part = d_w_expand.size // (fs * dpart)
    blocks = attn_shards(
        [d_attn, d_w_expand.reshape(fs, ex_part, dpart)]
    )
    at_q, at_e = hd * VHEAD, hd * VHEAD + q_cols
    by_group = [(j ^ m) // share for m in members]
    w_out_grad = place(
        w_out.shape, f32, [v[:at_q] for v in blocks], [g * hd * VHEAD for g in by_group], 0
    )
    w_query_grad = place(
        w_query.shape[::-1], f32, [v[at_q:at_e] for v in blocks], [g * q_cols for g in by_group], 0
    ).T
    w_expand_grad = place(
        w_expand.shape,
        f32,
        [v[at_e:].reshape(w_expand.shape[0], hd * kv_width) for v in blocks],
        [g * hd * kv_width for g in by_group],
        1,
    )
    blocks = attn_shards([split_cols(d_w_latent)])
    w_latent_grad = place(
        w_latent.shape[::-1], f32, blocks, [(j ^ m) * lat_cols for m in members], 0
    ).T

    gain_parts = jnp.concatenate(
        [
            d_gain_attn.reshape(fs, -1),
            d_gain_moe.reshape(fs, -1),
            d_gain_latent.reshape(fs, -1),
        ],
        axis=1,
    )
    gain_sum = jnp.sum(turn(gain_parts[:, None, :]), axis=0)
    for bit in low_bits(tp):
        gain_sum = gain_sum + exchange(gain_sum, "tp", bit)
    for bit in low_bits(cx):
        gain_sum = gain_sum + exchange(gain_sum, "ctx", bit)
    gain_sum = gain_sum[0]
    cut_a, cut_b = gain_attn.shape[0], gain_attn.shape[0] + gain_moe.shape[0]

    expert_gate_grad = gate_shards.transpose(0, 2, 1)
    expert_up_grad = up_shards.transpose(0, 2, 1)
    expert_down_grad = lay_out(down_blocks)
    shared_grads = down_blocks[:, :, ffn:].reshape(cx, fs, 3, sh, dpart).transpose(2, 0, 1, 3, 4)
    shared_grads = shared_grads.reshape(3, cx * fs * sh, dpart).astype(f32)
    shared_gate_grad = shared_grads[0].T
    shared_up_grad = shared_grads[1].T
    shared_down_grad = shared_grads[2]

    return (
        layer_out,
        input_grad,
        gates_grad,
        gain_sum[:cut_a],
        gain_sum[cut_b:],
        w_query_grad,
        w_latent_grad,
        w_expand_grad,
        w_out_grad,
        gain_sum[cut_a:cut_b],
        expert_gate_grad,
        expert_up_grad,
        expert_down_grad,
        shared_gate_grad,
        shared_up_grad,
        shared_down_grad,
    )


def solution(mesh):
    placed = (
        P(("fsdp", "ctx"), None),
        P(("fsdp", "ctx"), None),
        P(("fsdp", "ctx"), None),
        P(("fsdp", "ctx"), None),
        P("fsdp"),
        P("fsdp"),
        P("fsdp", "tp"),
        P("fsdp", None),
        P("fsdp", "tp"),
        P("tp", "fsdp"),
        P("fsdp"),
        P(None, "fsdp", "tp"),
        P(None, "fsdp", "tp"),
        P(None, "tp", "fsdp"),
        P("fsdp", "tp"),
        P("fsdp", "tp"),
        P("tp", "fsdp"),
    )
    return jax.shard_map(
        local,
        mesh=mesh,
        in_specs=placed,
        out_specs=(
            P(("fsdp", "ctx"), None),
            P(("fsdp", "ctx"), None),
            P(("fsdp", "ctx"), None),
            P("fsdp"),
            P("fsdp"),
            P("fsdp", "tp"),
            P("fsdp", None),
            P("fsdp", "tp"),
            P("tp", "fsdp"),
            P("fsdp"),
            P(None, "fsdp", "tp"),
            P(None, "fsdp", "tp"),
            P(None, "tp", "fsdp"),
            P("fsdp", "tp"),
            P("fsdp", "tp"),
            P("tp", "fsdp"),
        ),
        check_vma=False,
    )
```

```python
import math

import jax
import jax.numpy as jnp
from jax import lax
from jax.experimental import pallas as pl
from jax.experimental.pallas import tpu as pltpu
from jax.sharding import PartitionSpec as P

NOPE = 128
ROPE = 64
LATENT = 512
VHEAD = 128
EXPERTS = 16
TOPK = 6
CAPACITY = 128
EPSILON = 1e-06

f32 = jnp.float32
bf16 = jnp.bfloat16


def norm_rows(values, gain_vec):
    scales = lax.rsqrt(jnp.mean(values * values, axis=-1, keepdims=True) + EPSILON)
    return (values * scales * gain_vec, scales)


def norm_back(values, scales, gain_vec, gradient):
    weighted = gradient * gain_vec
    inner = jnp.mean(weighted * values, axis=-1, keepdims=True)
    return (
        scales * weighted - values * scales**3 * inner,
        jnp.sum(gradient * values * scales, axis=0),
    )


def angle_tables(position, width):
    half_width = width // 2
    frequency = jnp.exp(
        jnp.arange(half_width, dtype=f32) * (-2.0 * math.log(10000.0) / width)
    )
    angles = position.astype(f32)[:, None] * frequency[None, :]
    return (jnp.cos(angles), jnp.sin(angles))


def rotate(values, cosine, sine_tab):
    half_width = values.shape[-1] // 2
    front_half = values[..., :half_width]
    back_half = values[..., half_width:]
    return jnp.concatenate(
        [front_half * cosine - back_half * sine_tab, back_half * cosine + front_half * sine_tab],
        axis=-1,
    )


def rotate_back(gradient, cosine, sine_tab):
    return rotate(gradient, cosine, -sine_tab)


def swiglu_back(gate_act, up_act, grad_hidden):
    sigmoid_g = jax.nn.sigmoid(gate_act)
    grad_up = (grad_hidden * gate_act * sigmoid_g).astype(bf16)
    grad_gate = (grad_hidden * up_act * sigmoid_g * (1.0 + gate_act * (1.0 - sigmoid_g))).astype(
        bf16
    )
    return (grad_gate, grad_up)


def mm(left, right):
    return jnp.dot(left, right, preferred_element_type=f32)


def mm_nt(left, right):
    return lax.dot_general(left, right, (((1,), (1,)), ((), ())), preferred_element_type=f32)


def mm_tn(left, right):
    return lax.dot_general(left, right, (((0,), (0,)), ((), ())), preferred_element_type=f32)


def after(value, *earlier):
    return lax.optimization_barrier((value,) + earlier)[0]


def exchange(value, axis, bit):
    size = lax.axis_size(axis)
    return lax.ppermute(value, axis, [(a, a ^ bit) for a in range(size)])


def high_bits(size):
    bit = size // 2
    while bit >= 2:
        yield bit
        bit //= 2


def low_bits(size):
    bit = 1
    while bit < size:
        yield bit
        bit *= 2


def place(shape, dtype, parts, starts, axis):
    buffer = jnp.zeros(shape, dtype)
    for part, start in zip(parts, starts):
        buffer = lax.dynamic_update_slice_in_dim(buffer, part.astype(dtype), start, axis)
    return buffer


def slot_masks(row_ref, pieces, tokens):
    iota = lax.broadcasted_iota(jnp.int32, (CAPACITY, tokens), 0)
    return [iota == row_ref[a] for a in range(pieces)]


def one_hot(mask):
    return jnp.where(mask, 1.0, 0.0).astype(bf16)


def rows_kernel(pieces, fs, steps, groups, *refs):
    row_ref, ws_ref = refs[:2]
    xs, dys = refs[2 : 2 + 2 * groups], refs[2 + 2 * groups : 2 + 4 * groups]
    wg, wu = refs[2 + 4 * groups : 4 + 4 * groups]
    slots_ref, sdy_ref, gate_ref, up_ref, ds_ref, dsh_ref, xbuf, dybuf, sems = refs[
        4 + 4 * groups :
    ]
    ffn = gate_ref.shape[1]
    step = pl.program_id(0)
    slot = lax.rem(step, 2)
    width = xbuf.shape[4]
    tokens = xbuf.shape[2] * xbuf.shape[3]
    dpart = wg.shape[2]
    shp = ws_ref.shape[0] // 3
    per = steps // (2 * groups)

    def begin(at, into):
        for q in range(steps):

            @pl.when(at == q)
            def _(q=q):
                chunk, other = q // 2, q % 2
                which, c = 2 * (chunk // per) + other, chunk % per
                pltpu.make_async_copy(xs[which].at[:, :, c], xbuf.at[into], sems.at[into, 0]).start()
                pltpu.make_async_copy(
                    dys[which].at[:, :, c], dybuf.at[into], sems.at[into, 1]
                ).start()

    @pl.when(step == 0)
    def _():
        begin(step, 0)

    @pl.when(step + 1 < steps)
    def _():
        begin(step + 1, 1 - slot)

    pltpu.make_async_copy(xs[0].at[:, :, 0], xbuf.at[slot], sems.at[slot, 0]).wait()
    pltpu.make_async_copy(dys[0].at[:, :, 0], dybuf.at[slot], sems.at[slot, 1]).wait()
    masks = slot_masks(row_ref, pieces, tokens)
    for a in range(pieces):
        pick = one_hot(masks[a])
        of = slice(a * CAPACITY, (a + 1) * CAPACITY)
        slots_ref[of, :] = mm(pick, xbuf[slot, a].reshape(tokens, width)).astype(bf16)
        sdy_ref[of, :] = mm(pick, dybuf[slot, a].reshape(tokens, width)).astype(bf16)
    gate_act = up_act = None
    for s in range(fs):
        part = slots_ref[:, s * dpart : (s + 1) * dpart]
        g, u = mm_nt(part, wg[s]), mm_nt(part, wu[s])
        gate_act = g if s == 0 else gate_act + g
        up_act = u if s == 0 else up_act + u
    gate_ref[...] = gate_act
    up_ref[...] = up_act
    flat = xbuf[slot].reshape(pieces * tokens, width)
    dflat = dybuf[slot].reshape(pieces * tokens, width)
    both = mm_nt(flat, ws_ref[: 2 * shp])
    sg, su = both[:, :shp], both[:, shp:]
    sd = mm_nt(dflat, ws_ref[2 * shp :])
    sig = 1.0 / (1.0 + jnp.exp(-sg))
    silu = sg * sig
    s_hid = (silu * su).astype(bf16)
    ds_up = (sd * silu).astype(bf16)
    ds_gate = (sd * su * sig * (1.0 + sg * (1.0 - sig))).astype(bf16)
    ds_ref[:, :shp] = ds_gate
    ds_ref[:, shp : 2 * shp] = ds_up
    ds_ref[:, 2 * shp :] = s_hid
    first = mm_tn(ds_ref[:, : 2 * shp], flat)
    second = mm_tn(s_hid, dflat)

    @pl.when(step == 0)
    def _():
        dsh_ref[: 2 * shp] = first
        dsh_ref[2 * shp :] = second

    @pl.when(step > 0)
    def _():
        dsh_ref[: 2 * shp] += first
        dsh_ref[2 * shp :] += second


def moe_rows(fs, ffn, xs, dys, slot_row, shared, gate_w, up_w):
    pieces, tp, per, n, width = xs[0].shape
    groups = len(xs) // 2
    tokens = tp * n
    steps = 2 * groups * per
    shp = shared.shape[0] // 3
    slots = pieces * CAPACITY
    once = pl.Buffered(buffer_count=1)

    def by_step(shape):
        return pl.BlockSpec(shape, lambda q: (q,) + (0,) * (len(shape) - 1))

    def fixed(shape):
        return pl.BlockSpec(shape, lambda q: (0,) * len(shape), pipeline_mode=once)

    total = steps * slots
    return pl.pallas_call(
        lambda *refs: rows_kernel(pieces, fs, steps, groups, *refs),
        grid=(steps,),
        in_specs=[by_step((pieces, 1, tokens)), fixed((3 * shp, width))]
        + [pl.BlockSpec(memory_space=pl.ANY)] * (4 * groups)
        + [fixed(gate_w.shape), fixed(up_w.shape)],
        out_specs=[
            by_step((slots, width)),
            by_step((slots, width)),
            by_step((slots, ffn)),
            by_step((slots, ffn)),
            by_step((pieces * tokens, 3 * shp)),
            fixed((3 * shp, width)),
        ],
        scratch_shapes=[
            pltpu.VMEM((2, pieces, tp, n, width), bf16),
            pltpu.VMEM((2, pieces, tp, n, width), bf16),
            pltpu.SemaphoreType.DMA((2, 2)),
        ],
        out_shape=[
            jax.ShapeDtypeStruct((total, width), bf16),
            jax.ShapeDtypeStruct((total, width), bf16),
            jax.ShapeDtypeStruct((total, ffn), f32),
            jax.ShapeDtypeStruct((total, ffn), f32),
            jax.ShapeDtypeStruct((steps * pieces * tokens, 3 * shp), bf16),
            jax.ShapeDtypeStruct((3 * shp, width), f32),
        ],
        compiler_params=pltpu.CompilerParams(vmem_limit_bytes=60 * 1024 * 1024),
        cost_estimate=pl.CostEstimate(flops=0, bytes_accessed=1_000_000, transcendentals=0),
        name="moe_rows",
    )(slot_row, shared, *xs, *dys, gate_w, up_w)


def back_kernel(pieces, fs, extra, tp_first, me_ref, *refs):
    sdy_ref, gate_ref, up_ref, row_ref, col_ref, wt_ref, ds_ref, ws_ref, wg, wu, wd = refs[:11]
    name_ref = refs[11]
    dg_ref, du_ref, hw_ref, keep_ref, send_ref = refs[12 + extra :]
    ffn = gate_ref.shape[1]
    n, width = keep_ref.shape[3], ws_ref.shape[1]
    half = lax.rem(pl.program_id(0), 2)
    tokens = row_ref.shape[2]
    dpart = wg.shape[2]
    shp = ws_ref.shape[0] // 3
    masks = slot_masks(row_ref, pieces, tokens)
    weight = jnp.concatenate(
        [
            jnp.sum(jnp.where(masks[a], wt_ref[a], 0.0), axis=1, keepdims=True)
            for a in range(pieces)
        ],
        axis=0,
    )
    dy_down = None
    for s in range(fs):
        d = mm_nt(sdy_ref[:, s * dpart : (s + 1) * dpart], wd[s])
        dy_down = d if s == 0 else dy_down + d
    gate_act, up_act = gate_ref[...], up_ref[...]
    sig = 1.0 / (1.0 + jnp.exp(-gate_act))
    silu = gate_act * sig
    hidden = (silu * up_act).astype(bf16).astype(f32)
    slot_grad = jnp.sum(hidden * dy_down, axis=1, keepdims=True)
    hw_ref[...] = (weight * hidden).astype(bf16)
    d_hidden = weight * dy_down
    du_ref[...] = (d_hidden * silu).astype(bf16)
    dg_ref[...] = (d_hidden * up_act * sig * (1.0 + gate_act * (1.0 - sig))).astype(bf16)
    across = lax.broadcasted_iota(jnp.int32, (tokens, CAPACITY), 1)
    picks = [one_hot(across == col_ref[a]) for a in range(pieces)]

    def write(a, at, value):
        for t in range(tokens // n):
            rows = value[t * n : (t + 1) * n]
            at_t = me_ref[0] ^ t
            index = (at_t, a) if tp_first else (a, at_t)

            @pl.when(half == 0)
            def _():
                keep_ref[index[0], index[1], 0, :, at] = rows

            @pl.when(half == 1)
            def _():
                send_ref[index[0], index[1], 0, :, at] = rows

    for s in range(fs):
        at = slice(s * dpart, (s + 1) * dpart)
        back = (
            mm(dg_ref[...], wg[s]) + mm(du_ref[...], wu[s])
        ).astype(bf16)
        s_back = mm(ds_ref[:, : 2 * shp], ws_ref[: 2 * shp, at])
        for a in range(pieces):
            part = mm(picks[a], back[a * CAPACITY : (a + 1) * CAPACITY])
            write(a, at, (part + s_back[a * tokens : (a + 1) * tokens]).astype(bf16))
    spread = (slot_grad * name_ref[...]).astype(bf16)
    for a in range(pieces):
        part = mm(picks[a], spread[a * CAPACITY : (a + 1) * CAPACITY])
        write(a, slice(width, width + 128), part.astype(bf16))


def moe_back(
    first, chunks, tp, fs, tp_first, me, sdy, gate, up, slot_row, slot_col, weight, ds, shared, gate_w, up_w, down_w, name, big
):
    width = sdy.shape[1]
    all_pieces, _, tokens = slot_row.shape
    pieces = all_pieces // (2 * fs)
    ffn, dpart = down_w.shape[1:]
    shp = shared.shape[0] // 3
    slots = pieces * CAPACITY
    once = pl.Buffered(buffer_count=1)

    def by_step(shape):
        return pl.BlockSpec(shape, lambda q, me: (2 * first + q,) + (0,) * (len(shape) - 1))

    def fixed(shape):
        return pl.BlockSpec(shape, lambda q, me: (0,) * len(shape), pipeline_mode=once)

    n = tokens // tp
    outer = (tp, pieces) if tp_first else (pieces, tp)
    half_spec = pl.BlockSpec(outer + (1, n, width + 128), lambda q, me: (0, 0, q // 2, 0, 0))
    total = sdy.shape[0]
    half = jax.ShapeDtypeStruct(outer + (chunks, n, width + 128), bf16)
    return pl.pallas_call(
        lambda *refs: back_kernel(pieces, fs, len(big), tp_first, *refs),
        grid_spec=pltpu.PrefetchScalarGridSpec(
            num_scalar_prefetch=1,
            grid=(2 * chunks,),
            in_specs=[
                by_step((slots, width)),
                by_step((slots, ffn)),
                by_step((slots, ffn)),
                by_step((pieces, 1, tokens)),
                by_step((pieces, tokens, 1)),
                by_step((pieces, 1, tokens)),
                by_step((pieces * tokens, 3 * shp)),
                fixed((3 * shp, width)),
            ]
            + [fixed(gate_w.shape), fixed(up_w.shape), fixed((fs, ffn, dpart))]
            + [fixed((1, 128))]
            + [pl.BlockSpec(memory_space=pl.ANY)] * len(big),
            out_specs=[
                by_step((slots, ffn)),
                by_step((slots, ffn)),
                by_step((slots, ffn)),
                half_spec,
                half_spec,
            ],
        ),
        out_shape=[
            jax.ShapeDtypeStruct((total, ffn), bf16),
            jax.ShapeDtypeStruct((total, ffn), bf16),
            jax.ShapeDtypeStruct((total, ffn), bf16),
            half,
            half,
        ],
        input_output_aliases={13 + b: b for b in range(len(big))},
        compiler_params=pltpu.CompilerParams(vmem_limit_bytes=60 * 1024 * 1024),
        cost_estimate=pl.CostEstimate(flops=0, bytes_accessed=1_000_000, transcendentals=0),
        name="moe_back",
    )(me, sdy, gate, up, slot_row, slot_col, weight, ds, shared, gate_w, up_w, down_w, name, *big)


def out_kernel(pieces, fs, ctx_first, me_ref, hw_ref, col_ref, ds_ref, ws_ref, wd, keep_ref, send_ref):
    tokens = col_ref.shape[1]
    n = keep_ref.shape[3]
    half = lax.rem(pl.program_id(0), 2)
    dpart = wd.shape[2]
    across = lax.broadcasted_iota(jnp.int32, (tokens, CAPACITY), 1)
    picks = [one_hot(across == col_ref[a]) for a in range(pieces)]
    for s in range(fs):
        at = slice(s * dpart, (s + 1) * dpart)
        out = mm(hw_ref[...], wd[s]).astype(bf16)
        shared = mm(ds_ref[...], ws_ref[:, at])
        for a in range(pieces):
            part = mm(picks[a], out[a * CAPACITY : (a + 1) * CAPACITY])
            value = (part + shared[a * tokens : (a + 1) * tokens]).astype(bf16)
            for t in range(tokens // n):
                rows = value[t * n : (t + 1) * n]
                at_t = me_ref[0] ^ t
                index = (a, at_t) if ctx_first else (at_t, a)

                @pl.when(half == 0)
                def _():
                    keep_ref[index[0], index[1], 0, :, at] = rows

                @pl.when(half == 1)
                def _():
                    send_ref[index[0], index[1], 0, :, at] = rows


def moe_out(first, chunks, tp, fs, ctx_first, me, hw, slot_col, ds, shared, down_w):
    all_pieces, tokens, _ = slot_col.shape
    ffn, dpart = down_w.shape[1:]
    width = shared.shape[1]
    shp = shared.shape[0] // 3
    pieces = all_pieces // (2 * fs)
    n = tokens // tp
    once = pl.Buffered(buffer_count=1)
    slots = 2 * chunks * pieces * CAPACITY
    outer = (pieces, tp) if ctx_first else (tp, pieces)
    half_spec = pl.BlockSpec(outer + (1, n, width), lambda q, me: (0, 0, q // 2, 0, 0))
    return pl.pallas_call(
        lambda *refs: out_kernel(pieces, fs, ctx_first, *refs),
        grid_spec=pltpu.PrefetchScalarGridSpec(
            num_scalar_prefetch=1,
            grid=(2 * chunks,),
            in_specs=[
                pl.BlockSpec((pieces * CAPACITY, ffn), lambda q, me: (2 * first + q, 0)),
                pl.BlockSpec((pieces, tokens, 1), lambda q, me: (2 * first + q, 0, 0)),
                pl.BlockSpec((pieces * tokens, shp), lambda q, me: (2 * first + q, 2)),
                pl.BlockSpec((shp, width), lambda q, me: (2, 0), pipeline_mode=once),
                pl.BlockSpec((fs, ffn, dpart), lambda q, me: (0, 0, 0), pipeline_mode=once),
            ],
            out_specs=[half_spec, half_spec],
        ),
        out_shape=[jax.ShapeDtypeStruct(outer + (chunks, n, width), bf16)] * 2,
        compiler_params=pltpu.CompilerParams(vmem_limit_bytes=40 * 1024 * 1024),
        cost_estimate=pl.CostEstimate(flops=0, bytes_accessed=1_000_000, transcendentals=0),
        name="moe_out",
    )(me, hw, slot_col, ds, shared, down_w)


def turned(front, back, cosine, sine):
    return front * cosine - back * sine, back * cosine + front * sine


def attend_kernel(hd, normed, query, latent, expand, out_w, gain, cos, sin, posq, posk, *outs):
    keep_ref, send_ref, raw_ref, low_ref, q_ref, ex_ref, prob_ref, heads_ref = outs
    length = normed.shape[0]
    q_width, kv_width, turn = NOPE + ROPE, NOPE + VHEAD, ROPE // 2
    scaling = q_width ** (-0.5)
    q_raw = mm_nt(normed[...], query[...])
    for h in range(hd):
        at = h * q_width
        q_ref[:, at : at + NOPE] = q_raw[:, at : at + NOPE].astype(bf16)
        front, back = q_raw[:, at + NOPE : at + NOPE + turn], q_raw[:, at + NOPE + turn : at + q_width]
        front, back = turned(front, back, cos[...], sin[...])
        q_ref[:, at + NOPE : at + NOPE + turn] = front.astype(bf16)
        q_ref[:, at + NOPE + turn : at + q_width] = back.astype(bf16)
    raw = mm_nt(normed[...], latent[...])
    raw_ref[...] = raw
    body = raw[:, :LATENT]
    scales = lax.rsqrt(jnp.mean(body * body, axis=-1, keepdims=True) + EPSILON)
    low_ref[:, :LATENT] = (body * scales * gain[...]).astype(bf16)
    front, back = turned(raw[:, LATENT : LATENT + turn], raw[:, LATENT + turn :], cos[...], sin[...])
    low_ref[:, LATENT : LATENT + turn] = front.astype(bf16)
    low_ref[:, LATENT + turn :] = back.astype(bf16)
    ex_ref[...] = mm(low_ref[:, :LATENT], expand[...]).astype(bf16)
    rope = low_ref[:, LATENT:]
    block = min(256, length)
    for h in range(hd):
        at, kv = h * q_width, h * kv_width
        keys, vals = ex_ref[:, kv : kv + NOPE], ex_ref[:, kv + NOPE : kv + kv_width]
        for r in range(0, length, block):
            rows = slice(r, r + block)
            scores = mm_nt(q_ref[rows, at : at + NOPE], keys)
            scores = (scores + mm_nt(q_ref[rows, at + NOPE : at + q_width], rope)) * scaling
            scores = jnp.where(posk[...] <= posq[rows, :], scores, -1e30)
            exponent = jnp.exp(scores - jnp.max(scores, axis=-1, keepdims=True))
            total = jnp.sum(exponent, axis=-1, keepdims=True)
            prob = (exponent / total).astype(bf16)
            prob_ref[h, rows, :] = prob
            heads_ref[rows, h * VHEAD : (h + 1) * VHEAD] = mm(prob, vals).astype(bf16)
    tp, pairs, n, _ = keep_ref.shape
    for ref, start in ((send_ref, length // 2), (keep_ref, 0)):
        for p in range(pairs):
            for t in range(tp):
                at = start + (p * tp + t) * n
                ref[t, p] = mm(heads_ref[at : at + n], out_w[...]).astype(bf16)


def whole_call(body, operands, out_shape, name, declared=1_000_000):
    return pl.pallas_call(
        body,
        in_specs=[pl.BlockSpec(memory_space=pltpu.VMEM)] * len(operands),
        out_specs=[pl.BlockSpec(memory_space=pltpu.VMEM)] * len(out_shape),
        out_shape=[jax.ShapeDtypeStruct(shape, dtype) for shape, dtype in out_shape],
        compiler_params=pltpu.CompilerParams(vmem_limit_bytes=60 * 1024 * 1024),
        cost_estimate=pl.CostEstimate(flops=0, bytes_accessed=declared, transcendentals=0),
        name=name,
    )(*operands)


def attend(hd, lead, normed, query, latent, expand, out_w, gain, cos, sin, position):
    length, width = normed.shape
    operands = (
        normed,
        query,
        latent,
        expand,
        out_w,
        gain[None],
        cos,
        sin,
        position[:, None],
        position[None],
    )
    out_shape = [
        (lead + (width,), bf16),
        (lead + (width,), bf16),
        ((length, LATENT + ROPE), f32),
        ((length, LATENT + ROPE), bf16),
        ((length, hd * (NOPE + ROPE)), bf16),
        ((length, hd * (NOPE + VHEAD)), bf16),
        ((hd, length, length), bf16),
        ((length, hd * VHEAD), bf16),
    ]
    return whole_call(lambda *refs: attend_kernel(hd, *refs), operands, out_shape, "attend")


def attend_back_kernel(hd, grad, out_w, prob, heads, ex, low, q, cos, sin, query, expand, *outs):
    keep_ref, send_ref, dq_ref, dex_ref = outs
    length, width = grad.shape
    half = length // 2
    q_width, kv_width, turn = NOPE + ROPE, NOPE + VHEAD, ROPE // 2
    scaling = q_width ** (-0.5)
    d_heads = mm_nt(grad[...], out_w[...]).astype(bf16)
    rope = low[:, LATENT:]
    block = min(256, length)
    d_rope = None
    for h in range(hd):
        at, kv = h * q_width, h * kv_width
        of = slice(h * VHEAD, (h + 1) * VHEAD)
        keys, vals = ex[:, kv : kv + NOPE], ex[:, kv + NOPE : kv + kv_width]
        d_key = d_kr = d_val = None
        for r in range(0, length, block):
            rows = slice(r, r + block)
            d_out = d_heads[rows, of]
            inner = jnp.sum(
                d_out.astype(f32) * heads[rows, of].astype(f32), axis=-1, keepdims=True
            )
            p = prob[h, rows, :]
            d_scores = (p.astype(f32) * (mm_nt(d_out, vals) - inner)).astype(bf16)
            dq_ref[rows, at : at + NOPE] = (mm(d_scores, keys) * scaling).astype(bf16)
            d_turn = mm(d_scores, rope) * scaling
            front, back = turned(d_turn[:, :turn], d_turn[:, turn:], cos[rows, :], -sin[rows, :])
            dq_ref[rows, at + NOPE : at + NOPE + turn] = front.astype(bf16)
            dq_ref[rows, at + NOPE + turn : at + q_width] = back.astype(bf16)
            one = mm_tn(d_scores, q[rows, at : at + NOPE])
            two = mm_tn(d_scores, q[rows, at + NOPE : at + q_width])
            three = mm_tn(p, d_out)
            d_key = one if r == 0 else d_key + one
            d_kr = two if r == 0 else d_kr + two
            d_val = three if r == 0 else d_val + three
        dex_ref[:, kv : kv + NOPE] = (d_key * scaling).astype(bf16)
        dex_ref[:, kv + NOPE : kv + kv_width] = d_val.astype(bf16)
        d_rope = d_kr if h == 0 else d_rope + d_kr
    d_rope = (d_rope * scaling).astype(bf16)
    tp, pairs, n, _ = keep_ref.shape
    for ref, start in ((send_ref, half), (keep_ref, 0)):
        for p in range(pairs):
            for t in range(tp):
                at = start + (p * tp + t) * n
                rows = slice(at, at + n)
                ref[t, p, :, :width] = mm(dq_ref[rows, :], query[...]).astype(bf16)
                ref[t, p, :, width : width + LATENT] = mm_nt(dex_ref[rows, :], expand[...]).astype(
                    bf16
                )
                ref[t, p, :, width + LATENT : width + LATENT + ROPE] = d_rope[rows]
                if ref.shape[3] > width + LATENT + ROPE:
                    ref[t, p, :, width + LATENT + ROPE :] = jnp.zeros(
                        (n, ref.shape[3] - width - LATENT - ROPE), bf16
                    )


def attend_back(hd, lead, grad, out_w, prob, heads, ex, low, q, cos, sin, query, expand):
    cols = -(-(grad.shape[1] + LATENT + ROPE) // 128) * 128
    operands = (grad, out_w, prob, heads, ex, low, q, cos, sin, query, expand)
    out_shape = [
        (lead + (cols,), bf16),
        (lead + (cols,), bf16),
        (q.shape, bf16),
        (ex.shape, bf16),
    ]
    return whole_call(
        lambda *refs: attend_back_kernel(hd, *refs), operands, out_shape, "attend_back"
    )


def attend_weights_kernel(grad, heads, dq, normed, dex, low, dw_ref, de_ref):
    fs, _, dpart = dw_ref.shape
    first = heads.shape[1]
    for z in range(fs):
        at = slice(z * dpart, (z + 1) * dpart)
        dw_ref[z, :first] = mm_tn(heads[...], grad[:, at]).astype(bf16)
        dw_ref[z, first:] = mm_tn(dq[...], normed[:, at]).astype(bf16)
    de_ref[...] = mm_tn(low[:, :LATENT], dex[...]).astype(bf16)


def attend_weights(fs, grad, heads, dq, normed, dex, low):
    rows = heads.shape[1] + dq.shape[1]
    out_shape = [((fs, rows, grad.shape[1] // fs), bf16), ((LATENT, dex.shape[1]), bf16)]
    return whole_call(
        attend_weights_kernel,
        (grad, heads, dq, normed, dex, low),
        out_shape,
        "attend_weights",
        30_000_000,
    )


def weight_grads(left, right, fs, more=None, sh=0):
    slots, ffn = left.shape
    dpart = right.shape[1] // fs
    extra = 3 * sh if more is not None else 0
    once = pl.Buffered(buffer_count=1)

    def body(left_ref, right_ref, *refs):
        out_ref = refs[-1]
        out_ref[0, :ffn] = mm_tn(left_ref[...], right_ref[...]).astype(bf16)
        if more is not None:
            shp = more.shape[0] // 3
            for b in range(3):
                out_ref[0, ffn + b * sh : ffn + (b + 1) * sh] = refs[0][
                    b * shp : b * shp + sh
                ].astype(bf16)

    in_specs = [
        pl.BlockSpec((slots, ffn), lambda z: (0, 0), pipeline_mode=once),
        pl.BlockSpec((slots, dpart), lambda z: (0, z)),
    ]
    operands = [left, right]
    if more is not None:
        in_specs.append(pl.BlockSpec((more.shape[0], dpart), lambda z: (0, z)))
        operands.append(more)
    return pl.pallas_call(
        body,
        grid=(fs,),
        in_specs=in_specs,
        out_specs=pl.BlockSpec((1, ffn + extra, dpart), lambda z: (z, 0, 0)),
        out_shape=jax.ShapeDtypeStruct((fs, ffn + extra, dpart), bf16),
        compiler_params=pltpu.CompilerParams(vmem_limit_bytes=50 * 1024 * 1024),
        cost_estimate=pl.CostEstimate(flops=0, bytes_accessed=1_000_000, transcendentals=0),
        name="weight_grads",
    )(*operands)


def assemble(blocks, dest, count, rows):
    each, _, cols = blocks[0].shape
    parts = len(blocks)

    def body(dest_ref, *refs):
        step = pl.program_id(0)
        for q in range(parts):

            @pl.when(step // each == q)
            def _(q=q):
                refs[parts][...] = refs[q][...].astype(f32)

    def source(q):
        return pl.BlockSpec(
            (1, rows, cols), lambda g, dest: (jnp.clip(g - q * each, 0, each - 1), 0, 0)
        )

    return pl.pallas_call(
        body,
        grid_spec=pltpu.PrefetchScalarGridSpec(
            num_scalar_prefetch=1,
            grid=(parts * each,),
            in_specs=[source(q) for q in range(parts)],
            out_specs=pl.BlockSpec((1, rows, cols), lambda g, dest: (dest[g], 0, 0)),
        ),
        out_shape=jax.ShapeDtypeStruct((count, rows, cols), f32),
        compiler_params=pltpu.CompilerParams(vmem_limit_bytes=40 * 1024 * 1024),
        cost_estimate=pl.CostEstimate(flops=0, bytes_accessed=36_000_000, transcendentals=0),
        name="assemble",
    )(dest, *blocks)


def local(
    hidden_in,
    cotangent,
    routes,
    gate_weights,
    gain_attn,
    gain_latent,
    w_query,
    w_latent,
    w_expand,
    w_out,
    gain_moe,
    expert_gate,
    expert_up,
    expert_down,
    shared_gate,
    shared_up,
    shared_down,
):
    fs, cx, tp = lax.axis_size("fsdp"), lax.axis_size("ctx"), lax.axis_size("tp")
    i, j, k = lax.axis_index("fsdp"), lax.axis_index("ctx"), lax.axis_index("tp")
    rows_dev, width = hidden_in.shape
    n = rows_dev // tp
    length = rows_dev * cx
    dpart = width // fs
    q_width = NOPE + ROPE
    kv_width = NOPE + VHEAD
    heads_dev = w_out.shape[0] // VHEAD
    groups = min(cx, heads_dev)
    share = cx // groups
    hd = heads_dev // groups
    group = j // share
    lead = j % share == 0
    scaling = q_width ** (-0.5)
    assert EXPERTS == fs * cx

    members = [0]
    for bit in list(high_bits(cx)) + [1]:
        members = members + [m ^ bit for m in members]
    place_of = [members.index(m) for m in range(cx)]

    def spot(m):
        return jnp.asarray(place_of, jnp.int32)[m]

    def spread_ctx(cur):
        for bit in high_bits(cx):
            cur = jnp.concatenate([cur, exchange(cur, "ctx", bit)], axis=0)
        return cur

    def spread_core(cur):
        return jnp.concatenate([cur, exchange(cur, "ctx", 1)], axis=0)

    def spread_tp(cur):
        for bit in low_bits(tp):
            cur = jnp.concatenate([cur, exchange(cur, "tp", bit)], axis=1)
        return cur

    def gather_halves(own, ctx_first):
        cur = own[None, None]
        cur = spread_tp(spread_ctx(cur)) if ctx_first else spread_ctx(spread_tp(cur))
        return cur, exchange(cur, "ctx", 1)

    def gather_plane(own, ctx_first=True):
        return jnp.concatenate(gather_halves(own, ctx_first), axis=0)

    def gather_ctx(own):
        return spread_core(spread_ctx(own[None]))

    def over_ctx(stack, *pins):
        blocks = [stack]
        for bit in list(high_bits(cx)) + [1]:
            if bit == 1 and pins:
                blocks = [after(block, *pins) for block in blocks]
            blocks = blocks + [exchange(block, "ctx", bit) for block in blocks]
        return blocks

    def reduce_core(keep, send):
        return (keep.astype(f32) + exchange(send, "ctx", 1).astype(f32)).astype(bf16)

    def reduce_lead(cur, axis):
        bits = low_bits(tp) if axis == "tp" else high_bits(cx)
        for bit in sorted(bits, reverse=True):
            at = cur.shape[0] // 2
            other = exchange(cur[at:], axis, bit)
            cur = (cur[:at].astype(f32) + other.astype(f32)).astype(bf16)
        return cur[0]

    def reduce_plane(keep, send, *pins):
        cur = after(reduce_core(keep, send), *pins[:1])
        cur = after(reduce_lead(cur, "tp"), *pins[1:])
        return reduce_lead(cur, "ctx").astype(f32)

    def rel_tp(value):
        blocks = value.reshape((tp, n) + value.shape[1:])
        return jnp.concatenate(
            [lax.dynamic_index_in_dim(blocks, k ^ t, 0, keepdims=False) for t in range(tp)], axis=0
        )

    def own_rows(value):
        return lax.dynamic_slice_in_dim(value, k * n, n, 0)

    def hop(cur, bit):
        cur = cur.reshape((cur.shape[0] // 2, 2) + cur.shape[1:])
        mine = (i // bit) % 2
        send = lax.dynamic_index_in_dim(cur, 1 - mine, 1, keepdims=False).astype(bf16)
        keep = lax.dynamic_index_in_dim(cur, mine, 1, keepdims=False)
        return keep.astype(f32) + exchange(send, "fsdp", bit).astype(f32)

    def hops(cur, bits):
        for bit in bits:
            cur = hop(cur, bit)
        return cur

    def turn(value):
        return lax.all_to_all(value, "fsdp", 0, 0)

    hid_rel = rel_tp(hidden_in)
    x_rel = hid_rel[:n].astype(f32)
    hid_all = gather_ctx(hid_rel).reshape(length, width)
    row = jnp.arange(n, dtype=jnp.int32)
    pos_rel = jnp.concatenate(
        [(j ^ m) * rows_dev + (k ^ t) * n + row for m in members for t in range(tp)]
    )
    cos_rel, sin_rel = angle_tables(pos_rel, ROPE)
    hid_all = after(hid_all, cos_rel, sin_rel)

    lat_cols = w_latent.shape[1] // cx
    query_own = lax.dynamic_slice_in_dim(w_query, group * hd * q_width, hd * q_width, 1)
    latent_own = lax.dynamic_slice_in_dim(w_latent.T, j * lat_cols, lat_cols, 0)
    expand_own = lax.dynamic_slice_in_dim(w_expand, group * hd * kv_width, hd * kv_width, 1)
    out_own = lax.dynamic_slice_in_dim(w_out, group * hd * VHEAD, hd * VHEAD, 0)
    lat_part = gain_latent.shape[0]
    gate_high = lax.reduce_precision(gate_weights, 8, 7)
    gate_low = (gate_weights - gate_high).astype(bf16)
    small = jnp.concatenate(
        [routes.T.astype(bf16), gate_high.T.astype(bf16), gate_low.T], axis=0
    )
    small_rows = -(-small.size // dpart)
    small = rel_tp(small.T).T.reshape(-1)
    small = jnp.pad(small, (0, small_rows * dpart - small.shape[0])).reshape(small_rows, dpart)
    extra = jnp.concatenate(
        [
            gain_attn[None],
            gain_moe[None],
            jnp.pad(gain_latent, (0, dpart - lat_part))[None],
            small,
        ],
        axis=0,
    )
    extra = jnp.pad(extra, ((0, -extra.shape[0] % 16), (0, 0)))
    first_pack = jnp.concatenate([query_own.T, latent_own, extra], axis=0)
    first_pack = after(lax.all_gather(first_pack, "fsdp", axis=0), hid_all)
    q_cols = hd * q_width
    query_t = first_pack[:, :q_cols].transpose(1, 0, 2).reshape(q_cols, width)
    latent_t = first_pack[:, q_cols : q_cols + lat_cols].transpose(1, 0, 2)
    latent_t = gather_ctx(latent_t.reshape(lat_cols, width))
    latent_t = place(
        (cx * lat_cols, width), bf16, list(latent_t), [(j ^ m) * lat_cols for m in members], 0
    )
    extra = first_pack[:, q_cols + lat_cols :]
    gain_norm = extra[:, 0].reshape(-1).astype(f32)
    gain_mix = extra[:, 1].reshape(-1).astype(f32)
    gain_lat = extra[:, 2, :lat_part].reshape(-1).astype(f32)
    small = extra[:, 3 : 3 + small_rows].reshape(fs, -1)[:, : 3 * TOPK * rows_dev]
    small = gather_ctx(small.reshape(fs, 3 * TOPK, rows_dev))
    small = small.transpose(1, 0, 2, 3).reshape(fs * cx, 3 * TOPK, rows_dev).astype(f32)
    ex_rows = expand_own.size // dpart
    second_pack = lax.all_gather(
        after(
            jnp.concatenate([expand_own.reshape(ex_rows, dpart), out_own], axis=0), first_pack
        ),
        "fsdp",
        axis=0,
    )
    second_pack = after(second_pack, latent_t)
    expand_w = second_pack[:, :ex_rows].reshape(-1, hd * kv_width)
    output_w = second_pack[:, ex_rows:].transpose(1, 0, 2).reshape(hd * VHEAD, width)

    dy_own = own_rows(cotangent)
    dy_seqs = lax.all_gather(after(dy_own, second_pack), "fsdp", axis=0)

    sh = shared_gate.shape[1] // (cx * fs)
    shp = -(-sh // 128) * 128
    ffn = expert_down.shape[1]
    cut = j * fs * sh
    gate_w = turn(
        after(
            lax.dynamic_slice_in_dim(expert_gate.transpose(0, 2, 1), j * fs, fs, 0), second_pack
        )
    )
    shared_own = jnp.stack(
        [
            lax.dynamic_slice_in_dim(shared_gate, cut, fs * sh, 1).T.reshape(fs, sh, dpart),
            lax.dynamic_slice_in_dim(shared_up, cut, fs * sh, 1).T.reshape(fs, sh, dpart),
            lax.dynamic_slice_in_dim(shared_down, cut, fs * sh, 0).reshape(fs, sh, dpart),
        ],
        axis=1,
    )

    normed, attn_scale = norm_rows(hid_all.astype(f32), gain_norm)
    normed_all = normed.astype(bf16)
    expert = (j * fs + i).astype(f32)
    named = small[:, :TOPK] == expert
    chosen = jnp.any(named, axis=1).astype(f32)
    gates_all = small[:, TOPK : 2 * TOPK] + small[:, 2 * TOPK :]
    weight = jnp.sum(jnp.where(named, gates_all, 0.0), axis=1)
    ahead = (
        jnp.arange(rows_dev, dtype=jnp.int32)[:, None]
        < jnp.arange(rows_dev, dtype=jnp.int32)[None, :]
    ).astype(bf16)
    earlier = mm(chosen.astype(bf16), ahead).astype(jnp.int32)
    slot_of = jnp.where(chosen > 0.5, earlier, -1).reshape(fs * cx, 1, rows_dev)
    weight = weight.reshape(fs * cx, 1, rows_dev)
    slot_col = slot_of.reshape(fs * cx, rows_dev, 1)
    expand_w = after(expand_w, slot_of, slot_col, weight)

    keep, send, latent_raw, latent_low, queries, expanded, attn_prob, heads_out = attend(
        hd, (tp, cx // 2, n), normed_all, query_t, latent_t, expand_w, output_w, gain_lat, cos_rel, sin_rel, pos_rel
    )
    half = length // 2

    def leading(value):
        return value if share == 1 else jnp.where(lead, value, jnp.zeros((), value.dtype))

    attn_sum = after(reduce_plane(leading(keep), leading(send), dy_seqs), gate_w)
    middle = x_rel + attn_sum
    normed_moe, moe_scale = norm_rows(middle, gain_mix)
    moe_low = normed_moe.astype(bf16)

    per = fs // 2 if fs > 1 else 1
    row_seqs = lax.all_gather(moe_low, "fsdp", axis=0)

    def to_all(seqs, *pins):
        halves = []
        for g in range(fs // per):
            cur = seqs[g * per : (g + 1) * per][None, None]
            if g % 2 == 0:
                cur = spread_ctx(cur)
                cur = spread_tp(after(cur, *pins) if pins else cur)
            else:
                cur = spread_tp(cur)
                cur = spread_ctx(after(cur, *pins) if pins else cur)
            halves += [cur, exchange(cur, "ctx", 1)]
        return halves

    dy_halves = to_all(after(dy_seqs, middle), moe_low)
    up_w = turn(
        after(lax.dynamic_slice_in_dim(expert_up.transpose(0, 2, 1), j * fs, fs, 0), row_seqs)
    )
    row_halves = to_all(after(row_seqs, *dy_halves[::2]))
    shared_w = turn(after(shared_own, up_w))
    down_w = turn(after(lax.dynamic_slice_in_dim(expert_down, j * fs, fs, 0), shared_w))
    shared_w = shared_w.transpose(1, 2, 0, 3).reshape(3, sh, width)
    shared_w = jnp.pad(shared_w, ((0, 0), (0, shp - sh), (0, 0))).reshape(3 * shp, width)


    all_slots, all_dy, gate_act, up_act, shared_ds, d_shared = moe_rows(
        fs, ffn, row_halves, dy_halves, slot_of, shared_w, gate_w, up_w
    )
    me = jnp.zeros((1,), jnp.int32)

    name = (jnp.arange(128, dtype=jnp.int32) == j * fs + i).astype(f32)[None]
    big, flows = [], []
    dy_in = all_dy
    for g in range(fs // per):
        results = moe_back(
            g * per,
            per,
            tp,
            fs,
            g % 2 == 0,
            me,
            dy_in,
            gate_act,
            up_act,
            slot_of,
            slot_col,
            weight,
            shared_ds,
            shared_w,
            gate_w,
            up_w,
            down_w,
            name,
            big,
        )
        big = list(results[:3])
        dy_in = after(all_dy, results[4])
        flows.append(reduce_core(results[3], results[4]))
    all_dg, all_du, all_hw = big

    def split_cols(value):
        return value.reshape(value.shape[0], fs, dpart).transpose(1, 0, 2)

    d_gate_w = weight_grads(after(all_dg, *flows), all_slots, fs)
    gate_back = turn(d_gate_w)
    firsts = [reduce_lead(flow, "ctx" if g % 2 else "tp") for g, flow in enumerate(flows)]
    out_args = (slot_col, shared_ds, shared_w, down_w)
    outs = [
        moe_out(g * per, per, tp, fs, g % 2 == 1, me, after(all_hw, d_gate_w), *out_args)
        for g in range(fs // per)
    ]
    firsts = [after(flow, *outs[0], *outs[-1]) for flow in firsts]
    seconds = [reduce_lead(flow, "tp" if g % 2 else "ctx") for g, flow in enumerate(firsts)]
    home = after(jnp.concatenate(seconds, axis=0), gate_back)
    d_up_w = weight_grads(after(all_du, home), all_slots, fs)
    d_down_w = weight_grads(after(all_hw, home), all_dy, fs, d_shared, sh)
    out_flows = [
        reduce_lead(after(reduce_core(keep, send), home), "ctx" if g % 2 else "tp")
        for g, (keep, send) in enumerate(outs)
    ]
    home_own = jnp.sum(turn(home).astype(f32), axis=0)
    home_own = after(home_own, d_up_w, d_down_w, *out_flows)
    up_back = turn(after(d_up_w, home_own))
    grad_total, gate_cols = home_own[:, :width], home_own[:, width:]
    in_order = jnp.arange(EXPERTS, dtype=jnp.int32)

    def lay_out(blocks):
        return assemble([blocks.reshape(EXPERTS, -1, dpart)], in_order, EXPERTS, ffn)

    grad_mid_norm, d_gain_moe = norm_back(middle, moe_scale, gain_mix, grad_total)
    grad_mid = dy_own.astype(f32) + grad_mid_norm
    grad_low = grad_mid.astype(bf16)
    grad_cur = spread_ctx(grad_low[None, None])
    gate_blocks = lax.all_gather(after(gate_back, grad_cur), "ctx", axis=0)
    grad_all = spread_core(spread_tp(grad_cur)).reshape(length, width)

    down_back = turn(after(d_down_w, up_back))
    gate_shards = lay_out(gate_blocks)
    keep, send, grad_q, grad_expanded = attend_back(
        hd,
        (tp, cx // 2, n),
        grad_all,
        output_w,
        attn_prob,
        heads_out,
        expanded,
        latent_low,
        queries,
        cos_rel,
        sin_rel,
        query_t,
        expand_w,
    )
    up_blocks = lax.all_gather(after(up_back, grad_q), "ctx", axis=0)
    summed = reduce_plane(leading(keep), leading(send), up_back, gate_shards)
    out_flows = [
        reduce_lead(after(flow, summed), "tp" if g % 2 else "ctx")
        for g, flow in enumerate(out_flows)
    ]
    out_home = jnp.concatenate(out_flows, axis=0)
    d_attn, d_w_expand = attend_weights(
        fs, grad_all, heads_out, after(grad_q, send), normed_all, grad_expanded, latent_low
    )
    summed = after(summed, d_attn)
    grad_latent_own = summed[:, width : width + LATENT + ROPE]
    up_shards = lay_out(up_blocks)
    latent_scale = lax.rsqrt(
        jnp.mean(latent_raw[:n, :LATENT] ** 2, axis=-1, keepdims=True) + EPSILON
    )
    grad_lat_raw, d_gain_latent = norm_back(
        latent_raw[:n, :LATENT], latent_scale, gain_lat, grad_latent_own[:, :LATENT]
    )
    grad_kv_raw = jnp.concatenate(
        [grad_lat_raw, rotate_back(grad_latent_own[:, LATENT:], cos_rel[:n], sin_rel[:n])], axis=1
    ).astype(bf16)
    grad_normed = summed[:, :width] + mm(grad_kv_raw, latent_t)
    kv_all = gather_plane(grad_kv_raw).reshape(length, -1)
    d_w_latent = mm_tn(
        lax.dynamic_slice_in_dim(kv_all, j * lat_cols, lat_cols, 1), normed_all
    ).astype(bf16)
    ex_part = d_w_expand.size // (fs * dpart)
    pack = jnp.concatenate(
        [d_attn, d_w_expand.reshape(fs, ex_part, dpart), split_cols(d_w_latent)], axis=1
    )
    bits = list(low_bits(fs))
    pack_sum = hops(pack, bits[:1])
    out_sum = hops(after(out_home, pack_sum), bits[:1])
    pack_sum = after(pack_sum, up_shards)
    out_total = hops(out_sum, bits[1:])[0]
    down_blocks = lax.all_gather(after(down_back, d_w_latent), "ctx", axis=0)
    grad_x_norm, d_gain_attn = norm_back(x_rel, attn_scale[:n], gain_norm, grad_normed)
    input_own = (grad_mid + grad_x_norm).astype(bf16)
    input_grad = rel_tp(spread_tp(input_own[None, None]).reshape(rows_dev, width)).astype(f32)

    out_own_rows = (middle + out_total).astype(bf16)
    layer_out = rel_tp(spread_tp(out_own_rows[None, None]).reshape(rows_dev, width))

    gate_cols = spread_tp(gate_cols[:, :EXPERTS][None, None]).reshape(rows_dev, EXPERTS)
    gate_cols = rel_tp(gate_cols)
    experts = jnp.arange(EXPERTS, dtype=jnp.int32)
    gates_grad = jnp.sum(
        jnp.where(routes[:, :, None] == experts, gate_cols[:, None, :], 0.0), axis=-1
    )

    blocks = over_ctx(hops(pack_sum, bits[1:])[0].astype(bf16))
    at_q, at_e = hd * VHEAD, hd * VHEAD + q_cols
    by_group = [(j ^ m) // share for m in members]
    w_out_grad = place(
        w_out.shape, f32, [v[:at_q] for v in blocks], [g * hd * VHEAD for g in by_group], 0
    )
    w_query_grad = place(
        w_query.shape[::-1], f32, [v[at_q:at_e] for v in blocks], [g * q_cols for g in by_group], 0
    ).T
    w_expand_grad = place(
        w_expand.shape,
        f32,
        [
            v[at_e : at_e + ex_part].reshape(w_expand.shape[0], hd * kv_width) for v in blocks
        ],
        [g * hd * kv_width for g in by_group],
        1,
    )
    w_latent_grad = place(
        w_latent.shape[::-1],
        f32,
        [v[at_e + ex_part :] for v in blocks],
        [(j ^ m) * lat_cols for m in members],
        0,
    ).T

    gain_parts = jnp.concatenate(
        [
            d_gain_attn.reshape(fs, -1),
            d_gain_moe.reshape(fs, -1),
            d_gain_latent.reshape(fs, -1),
        ],
        axis=1,
    )
    gain_sum = jnp.sum(turn(gain_parts[:, None, :]), axis=0)
    for bit in low_bits(tp):
        gain_sum = gain_sum + exchange(gain_sum, "tp", bit)
    for bit in low_bits(cx):
        gain_sum = gain_sum + exchange(gain_sum, "ctx", bit)
    gain_sum = gain_sum[0]
    cut_a, cut_b = gain_attn.shape[0], gain_attn.shape[0] + gain_moe.shape[0]

    expert_gate_grad = gate_shards.transpose(0, 2, 1)
    expert_up_grad = up_shards.transpose(0, 2, 1)
    expert_down_grad = lay_out(down_blocks)
    shared_grads = down_blocks[:, :, ffn:].reshape(cx, fs, 3, sh, dpart).transpose(2, 0, 1, 3, 4)
    shared_grads = shared_grads.reshape(3, cx * fs * sh, dpart).astype(f32)
    shared_gate_grad = shared_grads[0].T
    shared_up_grad = shared_grads[1].T
    shared_down_grad = shared_grads[2]

    return (
        layer_out,
        input_grad,
        gates_grad,
        gain_sum[:cut_a],
        gain_sum[cut_b:],
        w_query_grad,
        w_latent_grad,
        w_expand_grad,
        w_out_grad,
        gain_sum[cut_a:cut_b],
        expert_gate_grad,
        expert_up_grad,
        expert_down_grad,
        shared_gate_grad,
        shared_up_grad,
        shared_down_grad,
    )


def solution(mesh):
    placed = (
        P(("fsdp", "ctx"), None),
        P(("fsdp", "ctx"), None),
        P(("fsdp", "ctx"), None),
        P(("fsdp", "ctx"), None),
        P("fsdp"),
        P("fsdp"),
        P("fsdp", "tp"),
        P("fsdp", None),
        P("fsdp", "tp"),
        P("tp", "fsdp"),
        P("fsdp"),
        P(None, "fsdp", "tp"),
        P(None, "fsdp", "tp"),
        P(None, "tp", "fsdp"),
        P("fsdp", "tp"),
        P("fsdp", "tp"),
        P("tp", "fsdp"),
    )
    return jax.shard_map(
        local,
        mesh=mesh,
        in_specs=placed,
        out_specs=(
            P(("fsdp", "ctx"), None),
            P(("fsdp", "ctx"), None),
            P(("fsdp", "ctx"), None),
            P("fsdp"),
            P("fsdp"),
            P("fsdp", "tp"),
            P("fsdp", None),
            P("fsdp", "tp"),
            P("tp", "fsdp"),
            P("fsdp"),
            P(None, "fsdp", "tp"),
            P(None, "fsdp", "tp"),
            P(None, "tp", "fsdp"),
            P("fsdp", "tp"),
            P("fsdp", "tp"),
            P("tp", "fsdp"),
        ),
        check_vma=False,
    )
```

```python
import math

import jax
import jax.numpy as jnp
from jax import lax
from jax.experimental import pallas as pl
from jax.experimental.pallas import tpu as pltpu
from jax.sharding import PartitionSpec as P

NOPE = 128
ROPE = 64
LATENT = 512
VHEAD = 128
EXPERTS = 16
TOPK = 6
CAPACITY = 128
EPSILON = 1e-06

f32 = jnp.float32
bf16 = jnp.bfloat16


def norm_rows(values, gain_vec):
    scales = lax.rsqrt(jnp.mean(values * values, axis=-1, keepdims=True) + EPSILON)
    return (values * scales * gain_vec, scales)


def norm_back(values, scales, gain_vec, gradient):
    weighted = gradient * gain_vec
    inner = jnp.mean(weighted * values, axis=-1, keepdims=True)
    return (
        scales * weighted - values * scales**3 * inner,
        jnp.sum(gradient * values * scales, axis=0),
    )


def angle_tables(position, width):
    half_width = width // 2
    frequency = jnp.exp(
        jnp.arange(half_width, dtype=f32) * (-2.0 * math.log(10000.0) / width)
    )
    angles = position.astype(f32)[:, None] * frequency[None, :]
    return (jnp.cos(angles), jnp.sin(angles))


def rotate(values, cosine, sine_tab):
    half_width = values.shape[-1] // 2
    front_half = values[..., :half_width]
    back_half = values[..., half_width:]
    return jnp.concatenate(
        [front_half * cosine - back_half * sine_tab, back_half * cosine + front_half * sine_tab],
        axis=-1,
    )


def rotate_back(gradient, cosine, sine_tab):
    return rotate(gradient, cosine, -sine_tab)


def swiglu_back(gate_act, up_act, grad_hidden):
    sigmoid_g = jax.nn.sigmoid(gate_act)
    grad_up = (grad_hidden * gate_act * sigmoid_g).astype(bf16)
    grad_gate = (grad_hidden * up_act * sigmoid_g * (1.0 + gate_act * (1.0 - sigmoid_g))).astype(
        bf16
    )
    return (grad_gate, grad_up)


def mm(left, right):
    return jnp.dot(left, right, preferred_element_type=f32)


def mm_nt(left, right):
    return lax.dot_general(left, right, (((1,), (1,)), ((), ())), preferred_element_type=f32)


def mm_tn(left, right):
    return lax.dot_general(left, right, (((0,), (0,)), ((), ())), preferred_element_type=f32)


def after(value, *earlier):
    return lax.optimization_barrier((value,) + earlier)[0]


def exchange(value, axis, bit):
    size = lax.axis_size(axis)
    return lax.ppermute(value, axis, [(a, a ^ bit) for a in range(size)])


def high_bits(size):
    bit = size // 2
    while bit >= 2:
        yield bit
        bit //= 2


def low_bits(size):
    bit = 1
    while bit < size:
        yield bit
        bit *= 2


def place(shape, dtype, parts, starts, axis):
    buffer = jnp.zeros(shape, dtype)
    for part, start in zip(parts, starts):
        buffer = lax.dynamic_update_slice_in_dim(buffer, part.astype(dtype), start, axis)
    return buffer


def slot_masks(row_ref, pieces, tokens):
    iota = lax.broadcasted_iota(jnp.int32, (CAPACITY, tokens), 0)
    return [iota == row_ref[a] for a in range(pieces)]


def one_hot(mask):
    return jnp.where(mask, 1.0, 0.0).astype(bf16)


def rows_kernel(pieces, fs, steps, groups, *refs):
    row_ref, ws_ref = refs[:2]
    xs, dys = refs[2 : 2 + 2 * groups], refs[2 + 2 * groups : 2 + 4 * groups]
    wg, wu = refs[2 + 4 * groups : 4 + 4 * groups]
    slots_ref, sdy_ref, gate_ref, up_ref, ds_ref, dsh_ref, xbuf, dybuf, sems = refs[
        4 + 4 * groups :
    ]
    ffn = gate_ref.shape[1]
    step = pl.program_id(0)
    slot = lax.rem(step, 2)
    width = xbuf.shape[4]
    tokens = xbuf.shape[2] * xbuf.shape[3]
    dpart = wg.shape[2]
    shp = ws_ref.shape[0] // 3
    per = steps // (2 * groups)

    def begin(at, into):
        for q in range(steps):

            @pl.when(at == q)
            def _(q=q):
                chunk, other = q // 2, q % 2
                which, c = 2 * (chunk // per) + other, chunk % per
                pltpu.make_async_copy(xs[which].at[:, :, c], xbuf.at[into], sems.at[into, 0]).start()
                pltpu.make_async_copy(
                    dys[which].at[:, :, c], dybuf.at[into], sems.at[into, 1]
                ).start()

    @pl.when(step == 0)
    def _():
        begin(step, 0)

    @pl.when(step + 1 < steps)
    def _():
        begin(step + 1, 1 - slot)

    pltpu.make_async_copy(xs[0].at[:, :, 0], xbuf.at[slot], sems.at[slot, 0]).wait()
    pltpu.make_async_copy(dys[0].at[:, :, 0], dybuf.at[slot], sems.at[slot, 1]).wait()
    masks = slot_masks(row_ref, pieces, tokens)
    for a in range(pieces):
        pick = one_hot(masks[a])
        of = slice(a * CAPACITY, (a + 1) * CAPACITY)
        slots_ref[of, :] = mm(pick, xbuf[slot, a].reshape(tokens, width)).astype(bf16)
        sdy_ref[of, :] = mm(pick, dybuf[slot, a].reshape(tokens, width)).astype(bf16)
    gate_act = up_act = None
    for s in range(fs):
        part = slots_ref[:, s * dpart : (s + 1) * dpart]
        g, u = mm_nt(part, wg[s]), mm_nt(part, wu[s])
        gate_act = g if s == 0 else gate_act + g
        up_act = u if s == 0 else up_act + u
    gate_ref[...] = gate_act
    up_ref[...] = up_act
    flat = xbuf[slot].reshape(pieces * tokens, width)
    dflat = dybuf[slot].reshape(pieces * tokens, width)
    both = mm_nt(flat, ws_ref[: 2 * shp])
    sg, su = both[:, :shp], both[:, shp:]
    sd = mm_nt(dflat, ws_ref[2 * shp :])
    sig = 1.0 / (1.0 + jnp.exp(-sg))
    silu = sg * sig
    s_hid = (silu * su).astype(bf16)
    ds_up = (sd * silu).astype(bf16)
    ds_gate = (sd * su * sig * (1.0 + sg * (1.0 - sig))).astype(bf16)
    ds_ref[:, :shp] = ds_gate
    ds_ref[:, shp : 2 * shp] = ds_up
    ds_ref[:, 2 * shp :] = s_hid
    first = mm_tn(ds_ref[:, : 2 * shp], flat)
    second = mm_tn(s_hid, dflat)

    @pl.when(step == 0)
    def _():
        dsh_ref[: 2 * shp] = first
        dsh_ref[2 * shp :] = second

    @pl.when(step > 0)
    def _():
        dsh_ref[: 2 * shp] += first
        dsh_ref[2 * shp :] += second


def moe_rows(fs, ffn, xs, dys, slot_row, shared, gate_w, up_w):
    pieces, tp, per, n, width = xs[0].shape
    groups = len(xs) // 2
    tokens = tp * n
    steps = 2 * groups * per
    shp = shared.shape[0] // 3
    slots = pieces * CAPACITY
    once = pl.Buffered(buffer_count=1)

    def by_step(shape):
        return pl.BlockSpec(shape, lambda q: (q,) + (0,) * (len(shape) - 1))

    def fixed(shape):
        return pl.BlockSpec(shape, lambda q: (0,) * len(shape), pipeline_mode=once)

    total = steps * slots
    return pl.pallas_call(
        lambda *refs: rows_kernel(pieces, fs, steps, groups, *refs),
        grid=(steps,),
        in_specs=[by_step((pieces, 1, tokens)), fixed((3 * shp, width))]
        + [pl.BlockSpec(memory_space=pl.ANY)] * (4 * groups)
        + [fixed(gate_w.shape), fixed(up_w.shape)],
        out_specs=[
            by_step((slots, width)),
            by_step((slots, width)),
            by_step((slots, ffn)),
            by_step((slots, ffn)),
            by_step((pieces * tokens, 3 * shp)),
            fixed((3 * shp, width)),
        ],
        scratch_shapes=[
            pltpu.VMEM((2, pieces, tp, n, width), bf16),
            pltpu.VMEM((2, pieces, tp, n, width), bf16),
            pltpu.SemaphoreType.DMA((2, 2)),
        ],
        out_shape=[
            jax.ShapeDtypeStruct((total, width), bf16),
            jax.ShapeDtypeStruct((total, width), bf16),
            jax.ShapeDtypeStruct((total, ffn), f32),
            jax.ShapeDtypeStruct((total, ffn), f32),
            jax.ShapeDtypeStruct((steps * pieces * tokens, 3 * shp), bf16),
            jax.ShapeDtypeStruct((3 * shp, width), f32),
        ],
        compiler_params=pltpu.CompilerParams(vmem_limit_bytes=60 * 1024 * 1024),
        cost_estimate=pl.CostEstimate(flops=0, bytes_accessed=1_000_000, transcendentals=0),
        name="moe_rows",
    )(slot_row, shared, *xs, *dys, gate_w, up_w)


def back_kernel(pieces, fs, extra, tp_first, me_ref, *refs):
    sdy_ref, gate_ref, up_ref, row_ref, col_ref, wt_ref, ds_ref, ws_ref, wg, wu, wd = refs[:11]
    name_ref = refs[11]
    dg_ref, du_ref, hw_ref, keep_ref, send_ref = refs[12 + extra :]
    ffn = gate_ref.shape[1]
    n, width = keep_ref.shape[3], ws_ref.shape[1]
    half = lax.rem(pl.program_id(0), 2)
    tokens = row_ref.shape[2]
    dpart = wg.shape[2]
    shp = ws_ref.shape[0] // 3
    masks = slot_masks(row_ref, pieces, tokens)
    weight = jnp.concatenate(
        [
            jnp.sum(jnp.where(masks[a], wt_ref[a], 0.0), axis=1, keepdims=True)
            for a in range(pieces)
        ],
        axis=0,
    )
    dy_down = None
    for s in range(fs):
        d = mm_nt(sdy_ref[:, s * dpart : (s + 1) * dpart], wd[s])
        dy_down = d if s == 0 else dy_down + d
    gate_act, up_act = gate_ref[...], up_ref[...]
    sig = 1.0 / (1.0 + jnp.exp(-gate_act))
    silu = gate_act * sig
    hidden = (silu * up_act).astype(bf16).astype(f32)
    slot_grad = jnp.sum(hidden * dy_down, axis=1, keepdims=True)
    hw_ref[...] = (weight * hidden).astype(bf16)
    d_hidden = weight * dy_down
    du_ref[...] = (d_hidden * silu).astype(bf16)
    dg_ref[...] = (d_hidden * up_act * sig * (1.0 + gate_act * (1.0 - sig))).astype(bf16)
    across = lax.broadcasted_iota(jnp.int32, (tokens, CAPACITY), 1)
    picks = [one_hot(across == col_ref[a]) for a in range(pieces)]

    def write(a, at, value):
        for t in range(tokens // n):
            rows = value[t * n : (t + 1) * n]
            at_t = me_ref[0] ^ t
            index = (at_t, a) if tp_first else (a, at_t)

            @pl.when(half == 0)
            def _():
                keep_ref[index[0], index[1], 0, :, at] = rows

            @pl.when(half == 1)
            def _():
                send_ref[index[0], index[1], 0, :, at] = rows

    for s in range(fs):
        at = slice(s * dpart, (s + 1) * dpart)
        back = (
            mm(dg_ref[...], wg[s]) + mm(du_ref[...], wu[s])
        ).astype(bf16)
        s_back = mm(ds_ref[:, : 2 * shp], ws_ref[: 2 * shp, at])
        for a in range(pieces):
            part = mm(picks[a], back[a * CAPACITY : (a + 1) * CAPACITY])
            write(a, at, (part + s_back[a * tokens : (a + 1) * tokens]).astype(bf16))
    spread = (slot_grad * name_ref[...]).astype(bf16)
    for a in range(pieces):
        part = mm(picks[a], spread[a * CAPACITY : (a + 1) * CAPACITY])
        write(a, slice(width, width + 128), part.astype(bf16))


def moe_back(
    first, chunks, tp, fs, tp_first, me, sdy, gate, up, slot_row, slot_col, weight, ds, shared, gate_w, up_w, down_w, name, big
):
    width = sdy.shape[1]
    all_pieces, _, tokens = slot_row.shape
    pieces = all_pieces // (2 * fs)
    ffn, dpart = down_w.shape[1:]
    shp = shared.shape[0] // 3
    slots = pieces * CAPACITY
    once = pl.Buffered(buffer_count=1)

    def by_step(shape):
        return pl.BlockSpec(shape, lambda q, me: (2 * first + q,) + (0,) * (len(shape) - 1))

    def fixed(shape):
        return pl.BlockSpec(shape, lambda q, me: (0,) * len(shape), pipeline_mode=once)

    n = tokens // tp
    outer = (tp, pieces) if tp_first else (pieces, tp)
    half_spec = pl.BlockSpec(outer + (1, n, width + 128), lambda q, me: (0, 0, q // 2, 0, 0))
    total = sdy.shape[0]
    half = jax.ShapeDtypeStruct(outer + (chunks, n, width + 128), bf16)
    return pl.pallas_call(
        lambda *refs: back_kernel(pieces, fs, len(big), tp_first, *refs),
        grid_spec=pltpu.PrefetchScalarGridSpec(
            num_scalar_prefetch=1,
            grid=(2 * chunks,),
            in_specs=[
                by_step((slots, width)),
                by_step((slots, ffn)),
                by_step((slots, ffn)),
                by_step((pieces, 1, tokens)),
                by_step((pieces, tokens, 1)),
                by_step((pieces, 1, tokens)),
                by_step((pieces * tokens, 3 * shp)),
                fixed((3 * shp, width)),
            ]
            + [fixed(gate_w.shape), fixed(up_w.shape), fixed((fs, ffn, dpart))]
            + [fixed((1, 128))]
            + [pl.BlockSpec(memory_space=pl.ANY)] * len(big),
            out_specs=[
                by_step((slots, ffn)),
                by_step((slots, ffn)),
                by_step((slots, ffn)),
                half_spec,
                half_spec,
            ],
        ),
        out_shape=[
            jax.ShapeDtypeStruct((total, ffn), bf16),
            jax.ShapeDtypeStruct((total, ffn), bf16),
            jax.ShapeDtypeStruct((total, ffn), bf16),
            half,
            half,
        ],
        input_output_aliases={13 + b: b for b in range(len(big))},
        compiler_params=pltpu.CompilerParams(vmem_limit_bytes=60 * 1024 * 1024),
        cost_estimate=pl.CostEstimate(flops=0, bytes_accessed=1_000_000, transcendentals=0),
        name="moe_back",
    )(me, sdy, gate, up, slot_row, slot_col, weight, ds, shared, gate_w, up_w, down_w, name, *big)


def out_kernel(pieces, fs, ctx_first, me_ref, hw_ref, col_ref, ds_ref, ws_ref, wd, keep_ref, send_ref):
    tokens = col_ref.shape[1]
    n = keep_ref.shape[3]
    half = lax.rem(pl.program_id(0), 2)
    dpart = wd.shape[2]
    across = lax.broadcasted_iota(jnp.int32, (tokens, CAPACITY), 1)
    picks = [one_hot(across == col_ref[a]) for a in range(pieces)]
    for s in range(fs):
        at = slice(s * dpart, (s + 1) * dpart)
        out = mm(hw_ref[...], wd[s]).astype(bf16)
        shared = mm(ds_ref[...], ws_ref[:, at])
        for a in range(pieces):
            part = mm(picks[a], out[a * CAPACITY : (a + 1) * CAPACITY])
            value = (part + shared[a * tokens : (a + 1) * tokens]).astype(bf16)
            for t in range(tokens // n):
                rows = value[t * n : (t + 1) * n]
                at_t = me_ref[0] ^ t
                index = (a, at_t) if ctx_first else (at_t, a)

                @pl.when(half == 0)
                def _():
                    keep_ref[index[0], index[1], 0, :, at] = rows

                @pl.when(half == 1)
                def _():
                    send_ref[index[0], index[1], 0, :, at] = rows


def moe_out(first, chunks, tp, fs, ctx_first, me, hw, slot_col, ds, shared, down_w):
    all_pieces, tokens, _ = slot_col.shape
    ffn, dpart = down_w.shape[1:]
    width = shared.shape[1]
    shp = shared.shape[0] // 3
    pieces = all_pieces // (2 * fs)
    n = tokens // tp
    once = pl.Buffered(buffer_count=1)
    slots = 2 * chunks * pieces * CAPACITY
    outer = (pieces, tp) if ctx_first else (tp, pieces)
    half_spec = pl.BlockSpec(outer + (1, n, width), lambda q, me: (0, 0, q // 2, 0, 0))
    return pl.pallas_call(
        lambda *refs: out_kernel(pieces, fs, ctx_first, *refs),
        grid_spec=pltpu.PrefetchScalarGridSpec(
            num_scalar_prefetch=1,
            grid=(2 * chunks,),
            in_specs=[
                pl.BlockSpec((pieces * CAPACITY, ffn), lambda q, me: (2 * first + q, 0)),
                pl.BlockSpec((pieces, tokens, 1), lambda q, me: (2 * first + q, 0, 0)),
                pl.BlockSpec((pieces * tokens, shp), lambda q, me: (2 * first + q, 2)),
                pl.BlockSpec((shp, width), lambda q, me: (2, 0), pipeline_mode=once),
                pl.BlockSpec((fs, ffn, dpart), lambda q, me: (0, 0, 0), pipeline_mode=once),
            ],
            out_specs=[half_spec, half_spec],
        ),
        out_shape=[jax.ShapeDtypeStruct(outer + (chunks, n, width), bf16)] * 2,
        compiler_params=pltpu.CompilerParams(vmem_limit_bytes=40 * 1024 * 1024),
        cost_estimate=pl.CostEstimate(flops=0, bytes_accessed=1_000_000, transcendentals=0),
        name="moe_out",
    )(me, hw, slot_col, ds, shared, down_w)


def turned(front, back, cosine, sine):
    return front * cosine - back * sine, back * cosine + front * sine


def attend_kernel(hd, normed, query, latent, expand, out_w, gain, cos, sin, posq, posk, *outs):
    keep_ref, send_ref, raw_ref, low_ref, q_ref, ex_ref, prob_ref, heads_ref = outs
    length = normed.shape[0]
    q_width, kv_width, turn = NOPE + ROPE, NOPE + VHEAD, ROPE // 2
    scaling = q_width ** (-0.5)
    q_raw = mm_nt(normed[...], query[...])
    for h in range(hd):
        at = h * q_width
        q_ref[:, at : at + NOPE] = q_raw[:, at : at + NOPE].astype(bf16)
        front, back = q_raw[:, at + NOPE : at + NOPE + turn], q_raw[:, at + NOPE + turn : at + q_width]
        front, back = turned(front, back, cos[...], sin[...])
        q_ref[:, at + NOPE : at + NOPE + turn] = front.astype(bf16)
        q_ref[:, at + NOPE + turn : at + q_width] = back.astype(bf16)
    raw = mm_nt(normed[...], latent[...])
    raw_ref[...] = raw
    body = raw[:, :LATENT]
    scales = lax.rsqrt(jnp.mean(body * body, axis=-1, keepdims=True) + EPSILON)
    low_ref[:, :LATENT] = (body * scales * gain[...]).astype(bf16)
    front, back = turned(raw[:, LATENT : LATENT + turn], raw[:, LATENT + turn :], cos[...], sin[...])
    low_ref[:, LATENT : LATENT + turn] = front.astype(bf16)
    low_ref[:, LATENT + turn :] = back.astype(bf16)
    ex_ref[...] = mm(low_ref[:, :LATENT], expand[...]).astype(bf16)
    rope = low_ref[:, LATENT:]
    block = min(256, length)
    for h in range(hd):
        at, kv = h * q_width, h * kv_width
        keys, vals = ex_ref[:, kv : kv + NOPE], ex_ref[:, kv + NOPE : kv + kv_width]
        for r in range(0, length, block):
            rows = slice(r, r + block)
            scores = mm_nt(q_ref[rows, at : at + NOPE], keys)
            scores = (scores + mm_nt(q_ref[rows, at + NOPE : at + q_width], rope)) * scaling
            scores = jnp.where(posk[...] <= posq[rows, :], scores, -1e30)
            exponent = jnp.exp(scores - jnp.max(scores, axis=-1, keepdims=True))
            total = jnp.sum(exponent, axis=-1, keepdims=True)
            prob = (exponent / total).astype(bf16)
            prob_ref[h, rows, :] = prob
            heads_ref[rows, h * VHEAD : (h + 1) * VHEAD] = mm(prob, vals).astype(bf16)
    tp, pairs, n, _ = keep_ref.shape
    for ref, start in ((send_ref, length // 2), (keep_ref, 0)):
        for p in range(pairs):
            for t in range(tp):
                at = start + (p * tp + t) * n
                ref[t, p] = mm(heads_ref[at : at + n], out_w[...]).astype(bf16)


def whole_call(body, operands, out_shape, name, declared=1_000_000):
    return pl.pallas_call(
        body,
        in_specs=[pl.BlockSpec(memory_space=pltpu.VMEM)] * len(operands),
        out_specs=[pl.BlockSpec(memory_space=pltpu.VMEM)] * len(out_shape),
        out_shape=[jax.ShapeDtypeStruct(shape, dtype) for shape, dtype in out_shape],
        compiler_params=pltpu.CompilerParams(vmem_limit_bytes=60 * 1024 * 1024),
        cost_estimate=pl.CostEstimate(flops=0, bytes_accessed=declared, transcendentals=0),
        name=name,
    )(*operands)


def attend(hd, lead, normed, query, latent, expand, out_w, gain, cos, sin, position):
    length, width = normed.shape
    operands = (
        normed,
        query,
        latent,
        expand,
        out_w,
        gain[None],
        cos,
        sin,
        position[:, None],
        position[None],
    )
    out_shape = [
        (lead + (width,), bf16),
        (lead + (width,), bf16),
        ((length, LATENT + ROPE), f32),
        ((length, LATENT + ROPE), bf16),
        ((length, hd * (NOPE + ROPE)), bf16),
        ((length, hd * (NOPE + VHEAD)), bf16),
        ((hd, length, length), bf16),
        ((length, hd * VHEAD), bf16),
    ]
    return whole_call(lambda *refs: attend_kernel(hd, *refs), operands, out_shape, "attend")


def attend_back_kernel(hd, grad, out_w, prob, heads, ex, low, q, cos, sin, query, expand, *outs):
    keep_ref, send_ref, dq_ref, dex_ref = outs
    length, width = grad.shape
    half = length // 2
    q_width, kv_width, turn = NOPE + ROPE, NOPE + VHEAD, ROPE // 2
    scaling = q_width ** (-0.5)
    d_heads = mm_nt(grad[...], out_w[...]).astype(bf16)
    rope = low[:, LATENT:]
    block = min(256, length)
    d_rope = None
    for h in range(hd):
        at, kv = h * q_width, h * kv_width
        of = slice(h * VHEAD, (h + 1) * VHEAD)
        keys, vals = ex[:, kv : kv + NOPE], ex[:, kv + NOPE : kv + kv_width]
        d_key = d_kr = d_val = None
        for r in range(0, length, block):
            rows = slice(r, r + block)
            d_out = d_heads[rows, of]
            inner = jnp.sum(
                d_out.astype(f32) * heads[rows, of].astype(f32), axis=-1, keepdims=True
            )
            p = prob[h, rows, :]
            d_scores = (p.astype(f32) * (mm_nt(d_out, vals) - inner)).astype(bf16)
            dq_ref[rows, at : at + NOPE] = (mm(d_scores, keys) * scaling).astype(bf16)
            d_turn = mm(d_scores, rope) * scaling
            front, back = turned(d_turn[:, :turn], d_turn[:, turn:], cos[rows, :], -sin[rows, :])
            dq_ref[rows, at + NOPE : at + NOPE + turn] = front.astype(bf16)
            dq_ref[rows, at + NOPE + turn : at + q_width] = back.astype(bf16)
            one = mm_tn(d_scores, q[rows, at : at + NOPE])
            two = mm_tn(d_scores, q[rows, at + NOPE : at + q_width])
            three = mm_tn(p, d_out)
            d_key = one if r == 0 else d_key + one
            d_kr = two if r == 0 else d_kr + two
            d_val = three if r == 0 else d_val + three
        dex_ref[:, kv : kv + NOPE] = (d_key * scaling).astype(bf16)
        dex_ref[:, kv + NOPE : kv + kv_width] = d_val.astype(bf16)
        d_rope = d_kr if h == 0 else d_rope + d_kr
    d_rope = (d_rope * scaling).astype(bf16)
    tp, pairs, n, _ = keep_ref.shape
    for ref, start in ((send_ref, half), (keep_ref, 0)):
        for p in range(pairs):
            for t in range(tp):
                at = start + (p * tp + t) * n
                rows = slice(at, at + n)
                ref[t, p, :, :width] = mm(dq_ref[rows, :], query[...]).astype(bf16)
                ref[t, p, :, width : width + LATENT] = mm_nt(dex_ref[rows, :], expand[...]).astype(
                    bf16
                )
                ref[t, p, :, width + LATENT : width + LATENT + ROPE] = d_rope[rows]
                if ref.shape[3] > width + LATENT + ROPE:
                    ref[t, p, :, width + LATENT + ROPE :] = jnp.zeros(
                        (n, ref.shape[3] - width - LATENT - ROPE), bf16
                    )


def attend_back(hd, lead, grad, out_w, prob, heads, ex, low, q, cos, sin, query, expand):
    cols = -(-(grad.shape[1] + LATENT + ROPE) // 128) * 128
    operands = (grad, out_w, prob, heads, ex, low, q, cos, sin, query, expand)
    out_shape = [
        (lead + (cols,), bf16),
        (lead + (cols,), bf16),
        (q.shape, bf16),
        (ex.shape, bf16),
    ]
    return whole_call(
        lambda *refs: attend_back_kernel(hd, *refs), operands, out_shape, "attend_back"
    )


def attend_weights_kernel(grad, heads, dq, normed, dex, low, dw_ref, de_ref):
    fs, _, dpart = dw_ref.shape
    first = heads.shape[1]
    for z in range(fs):
        at = slice(z * dpart, (z + 1) * dpart)
        dw_ref[z, :first] = mm_tn(heads[...], grad[:, at]).astype(bf16)
        dw_ref[z, first:] = mm_tn(dq[...], normed[:, at]).astype(bf16)
    de_ref[...] = mm_tn(low[:, :LATENT], dex[...]).astype(bf16)


def attend_weights(fs, grad, heads, dq, normed, dex, low):
    rows = heads.shape[1] + dq.shape[1]
    out_shape = [((fs, rows, grad.shape[1] // fs), bf16), ((LATENT, dex.shape[1]), bf16)]
    return whole_call(
        attend_weights_kernel,
        (grad, heads, dq, normed, dex, low),
        out_shape,
        "attend_weights",
        30_000_000,
    )


def weight_grads(left, right, fs, more=None, sh=0):
    slots, ffn = left.shape
    dpart = right.shape[1] // fs
    extra = 3 * sh if more is not None else 0
    once = pl.Buffered(buffer_count=1)

    def body(left_ref, right_ref, *refs):
        out_ref = refs[-1]
        out_ref[0, :ffn] = mm_tn(left_ref[...], right_ref[...]).astype(bf16)
        if more is not None:
            shp = more.shape[0] // 3
            for b in range(3):
                out_ref[0, ffn + b * sh : ffn + (b + 1) * sh] = refs[0][
                    b * shp : b * shp + sh
                ].astype(bf16)

    in_specs = [
        pl.BlockSpec((slots, ffn), lambda z: (0, 0), pipeline_mode=once),
        pl.BlockSpec((slots, dpart), lambda z: (0, z)),
    ]
    operands = [left, right]
    if more is not None:
        in_specs.append(pl.BlockSpec((more.shape[0], dpart), lambda z: (0, z)))
        operands.append(more)
    return pl.pallas_call(
        body,
        grid=(fs,),
        in_specs=in_specs,
        out_specs=pl.BlockSpec((1, ffn + extra, dpart), lambda z: (z, 0, 0)),
        out_shape=jax.ShapeDtypeStruct((fs, ffn + extra, dpart), bf16),
        compiler_params=pltpu.CompilerParams(vmem_limit_bytes=50 * 1024 * 1024),
        cost_estimate=pl.CostEstimate(flops=0, bytes_accessed=1_000_000, transcendentals=0),
        name="weight_grads",
    )(*operands)


def assemble(blocks, dest, count, rows):
    each, _, cols = blocks[0].shape
    parts = len(blocks)

    def body(dest_ref, *refs):
        step = pl.program_id(0)
        for q in range(parts):

            @pl.when(step // each == q)
            def _(q=q):
                refs[parts][...] = refs[q][...].astype(f32)

    def source(q):
        return pl.BlockSpec(
            (1, rows, cols), lambda g, dest: (jnp.clip(g - q * each, 0, each - 1), 0, 0)
        )

    return pl.pallas_call(
        body,
        grid_spec=pltpu.PrefetchScalarGridSpec(
            num_scalar_prefetch=1,
            grid=(parts * each,),
            in_specs=[source(q) for q in range(parts)],
            out_specs=pl.BlockSpec((1, rows, cols), lambda g, dest: (dest[g], 0, 0)),
        ),
        out_shape=jax.ShapeDtypeStruct((count, rows, cols), f32),
        compiler_params=pltpu.CompilerParams(vmem_limit_bytes=40 * 1024 * 1024),
        cost_estimate=pl.CostEstimate(flops=0, bytes_accessed=36_000_000, transcendentals=0),
        name="assemble",
    )(dest, *blocks)


def local(
    hidden_in,
    cotangent,
    routes,
    gate_weights,
    gain_attn,
    gain_latent,
    w_query,
    w_latent,
    w_expand,
    w_out,
    gain_moe,
    expert_gate,
    expert_up,
    expert_down,
    shared_gate,
    shared_up,
    shared_down,
):
    fs, cx, tp = lax.axis_size("fsdp"), lax.axis_size("ctx"), lax.axis_size("tp")
    i, j, k = lax.axis_index("fsdp"), lax.axis_index("ctx"), lax.axis_index("tp")
    rows_dev, width = hidden_in.shape
    n = rows_dev // tp
    length = rows_dev * cx
    dpart = width // fs
    q_width = NOPE + ROPE
    kv_width = NOPE + VHEAD
    heads_dev = w_out.shape[0] // VHEAD
    groups = min(cx, heads_dev)
    share = cx // groups
    hd = heads_dev // groups
    group = j // share
    lead = j % share == 0
    scaling = q_width ** (-0.5)
    assert EXPERTS == fs * cx

    members = [0]
    for bit in list(high_bits(cx)) + [1]:
        members = members + [m ^ bit for m in members]
    place_of = [members.index(m) for m in range(cx)]

    def spot(m):
        return jnp.asarray(place_of, jnp.int32)[m]

    def spread_ctx(cur):
        for bit in high_bits(cx):
            cur = jnp.concatenate([cur, exchange(cur, "ctx", bit)], axis=0)
        return cur

    def spread_core(cur):
        return jnp.concatenate([cur, exchange(cur, "ctx", 1)], axis=0)

    def spread_tp(cur):
        for bit in low_bits(tp):
            cur = jnp.concatenate([cur, exchange(cur, "tp", bit)], axis=1)
        return cur

    def gather_halves(own, ctx_first):
        cur = own[None, None]
        cur = spread_tp(spread_ctx(cur)) if ctx_first else spread_ctx(spread_tp(cur))
        return cur, exchange(cur, "ctx", 1)

    def gather_plane(own, ctx_first=True):
        return jnp.concatenate(gather_halves(own, ctx_first), axis=0)

    def gather_ctx(own):
        return spread_core(spread_ctx(own[None]))

    def over_ctx(stack, *pins):
        blocks = [stack]
        for bit in list(high_bits(cx)) + [1]:
            if bit == 1 and pins:
                blocks = [after(block, *pins) for block in blocks]
            blocks = blocks + [exchange(block, "ctx", bit) for block in blocks]
        return blocks

    def reduce_core(keep, send):
        return (keep.astype(f32) + exchange(send, "ctx", 1).astype(f32)).astype(bf16)

    def reduce_lead(cur, axis):
        bits = low_bits(tp) if axis == "tp" else high_bits(cx)
        for bit in sorted(bits, reverse=True):
            at = cur.shape[0] // 2
            other = exchange(cur[at:], axis, bit)
            cur = (cur[:at].astype(f32) + other.astype(f32)).astype(bf16)
        return cur[0]

    def reduce_plane(keep, send, *pins):
        cur = after(reduce_core(keep, send), *pins[:1])
        cur = after(reduce_lead(cur, "tp"), *pins[1:])
        return reduce_lead(cur, "ctx").astype(f32)

    def rel_tp(value):
        blocks = value.reshape((tp, n) + value.shape[1:])
        return jnp.concatenate(
            [lax.dynamic_index_in_dim(blocks, k ^ t, 0, keepdims=False) for t in range(tp)], axis=0
        )

    def own_rows(value):
        return lax.dynamic_slice_in_dim(value, k * n, n, 0)

    def hop(cur, bit):
        cur = cur.reshape((cur.shape[0] // 2, 2) + cur.shape[1:])
        mine = (i // bit) % 2
        send = lax.dynamic_index_in_dim(cur, 1 - mine, 1, keepdims=False).astype(bf16)
        keep = lax.dynamic_index_in_dim(cur, mine, 1, keepdims=False)
        return keep.astype(f32) + exchange(send, "fsdp", bit).astype(f32)

    def hops(cur, bits):
        for bit in bits:
            cur = hop(cur, bit)
        return cur

    def turn(value):
        return lax.all_to_all(value, "fsdp", 0, 0)

    hid_rel = rel_tp(hidden_in)
    x_rel = hid_rel[:n].astype(f32)
    hid_all = gather_ctx(hid_rel).reshape(length, width)
    row = jnp.arange(n, dtype=jnp.int32)
    pos_rel = jnp.concatenate(
        [(j ^ m) * rows_dev + (k ^ t) * n + row for m in members for t in range(tp)]
    )
    cos_rel, sin_rel = angle_tables(pos_rel, ROPE)
    hid_all = after(hid_all, cos_rel, sin_rel)

    lat_cols = w_latent.shape[1] // cx
    query_own = lax.dynamic_slice_in_dim(w_query, group * hd * q_width, hd * q_width, 1)
    latent_own = lax.dynamic_slice_in_dim(w_latent.T, j * lat_cols, lat_cols, 0)
    expand_own = lax.dynamic_slice_in_dim(w_expand, group * hd * kv_width, hd * kv_width, 1)
    out_own = lax.dynamic_slice_in_dim(w_out, group * hd * VHEAD, hd * VHEAD, 0)
    lat_part = gain_latent.shape[0]
    gate_high = lax.reduce_precision(gate_weights, 8, 7)
    gate_low = (gate_weights - gate_high).astype(bf16)
    small = jnp.concatenate(
        [routes.T.astype(bf16), gate_high.T.astype(bf16), gate_low.T], axis=0
    )
    small_rows = -(-small.size // dpart)
    small = rel_tp(small.T).T.reshape(-1)
    small = jnp.pad(small, (0, small_rows * dpart - small.shape[0])).reshape(small_rows, dpart)
    extra = jnp.concatenate(
        [
            gain_attn[None],
            gain_moe[None],
            jnp.pad(gain_latent, (0, dpart - lat_part))[None],
            small,
        ],
        axis=0,
    )
    extra = jnp.pad(extra, ((0, -extra.shape[0] % 16), (0, 0)))
    first_pack = jnp.concatenate([query_own.T, latent_own, extra], axis=0)
    first_pack = after(lax.all_gather(first_pack, "fsdp", axis=0), hid_all)
    q_cols = hd * q_width
    query_t = first_pack[:, :q_cols].transpose(1, 0, 2).reshape(q_cols, width)
    latent_t = first_pack[:, q_cols : q_cols + lat_cols].transpose(1, 0, 2)
    latent_t = gather_ctx(latent_t.reshape(lat_cols, width))
    latent_t = place(
        (cx * lat_cols, width), bf16, list(latent_t), [(j ^ m) * lat_cols for m in members], 0
    )
    extra = first_pack[:, q_cols + lat_cols :]
    gain_norm = extra[:, 0].reshape(-1).astype(f32)
    gain_mix = extra[:, 1].reshape(-1).astype(f32)
    gain_lat = extra[:, 2, :lat_part].reshape(-1).astype(f32)
    small = extra[:, 3 : 3 + small_rows].reshape(fs, -1)[:, : 3 * TOPK * rows_dev]
    small = gather_ctx(small.reshape(fs, 3 * TOPK, rows_dev))
    small = small.transpose(1, 0, 2, 3).reshape(fs * cx, 3 * TOPK, rows_dev).astype(f32)
    ex_rows = expand_own.size // dpart
    second_pack = lax.all_gather(
        after(
            jnp.concatenate([expand_own.reshape(ex_rows, dpart), out_own], axis=0), first_pack
        ),
        "fsdp",
        axis=0,
    )
    second_pack = after(second_pack, latent_t)
    expand_w = second_pack[:, :ex_rows].reshape(-1, hd * kv_width)
    output_w = second_pack[:, ex_rows:].transpose(1, 0, 2).reshape(hd * VHEAD, width)

    dy_own = own_rows(cotangent)
    dy_seqs = lax.all_gather(after(dy_own, second_pack), "fsdp", axis=0)

    sh = shared_gate.shape[1] // (cx * fs)
    shp = -(-sh // 128) * 128
    ffn = expert_down.shape[1]
    cut = j * fs * sh
    gate_w = turn(
        after(
            lax.dynamic_slice_in_dim(expert_gate.transpose(0, 2, 1), j * fs, fs, 0), second_pack
        )
    )
    shared_own = jnp.stack(
        [
            lax.dynamic_slice_in_dim(shared_gate, cut, fs * sh, 1).T.reshape(fs, sh, dpart),
            lax.dynamic_slice_in_dim(shared_up, cut, fs * sh, 1).T.reshape(fs, sh, dpart),
            lax.dynamic_slice_in_dim(shared_down, cut, fs * sh, 0).reshape(fs, sh, dpart),
        ],
        axis=1,
    )

    normed, attn_scale = norm_rows(hid_all.astype(f32), gain_norm)
    normed_all = normed.astype(bf16)
    expert = (j * fs + i).astype(f32)
    named = small[:, :TOPK] == expert
    chosen = jnp.any(named, axis=1).astype(f32)
    gates_all = small[:, TOPK : 2 * TOPK] + small[:, 2 * TOPK :]
    weight = jnp.sum(jnp.where(named, gates_all, 0.0), axis=1)
    ahead = (
        jnp.arange(rows_dev, dtype=jnp.int32)[:, None]
        < jnp.arange(rows_dev, dtype=jnp.int32)[None, :]
    ).astype(bf16)
    earlier = mm(chosen.astype(bf16), ahead).astype(jnp.int32)
    slot_of = jnp.where(chosen > 0.5, earlier, -1).reshape(fs * cx, 1, rows_dev)
    weight = weight.reshape(fs * cx, 1, rows_dev)
    slot_col = slot_of.reshape(fs * cx, rows_dev, 1)
    expand_w = after(expand_w, slot_of, slot_col, weight)

    keep, send, latent_raw, latent_low, queries, expanded, attn_prob, heads_out = attend(
        hd, (tp, cx // 2, n), normed_all, query_t, latent_t, expand_w, output_w, gain_lat, cos_rel, sin_rel, pos_rel
    )
    half = length // 2

    def leading(value):
        return value if share == 1 else jnp.where(lead, value, jnp.zeros((), value.dtype))

    attn_sum = after(reduce_plane(leading(keep), leading(send), dy_seqs), gate_w)
    middle = x_rel + attn_sum
    normed_moe, moe_scale = norm_rows(middle, gain_mix)
    moe_low = normed_moe.astype(bf16)

    per = fs // 2 if fs > 1 else 1
    row_seqs = lax.all_gather(moe_low, "fsdp", axis=0)

    def to_all(seqs, *pins):
        halves = []
        for g in range(fs // per):
            cur = seqs[g * per : (g + 1) * per][None, None]
            if g % 2 == 0:
                cur = spread_ctx(cur)
                cur = spread_tp(after(cur, *pins) if pins else cur)
            else:
                cur = spread_tp(cur)
                cur = spread_ctx(after(cur, *pins) if pins else cur)
            halves += [cur, exchange(cur, "ctx", 1)]
        return halves

    dy_halves = to_all(after(dy_seqs, middle), moe_low)
    up_w = turn(
        after(lax.dynamic_slice_in_dim(expert_up.transpose(0, 2, 1), j * fs, fs, 0), row_seqs)
    )
    row_halves = to_all(after(row_seqs, *dy_halves[::2]))
    shared_w = turn(after(shared_own, up_w))
    down_w = turn(after(lax.dynamic_slice_in_dim(expert_down, j * fs, fs, 0), shared_w))
    shared_w = shared_w.transpose(1, 2, 0, 3).reshape(3, sh, width)
    shared_w = jnp.pad(shared_w, ((0, 0), (0, shp - sh), (0, 0))).reshape(3 * shp, width)


    all_slots, all_dy, gate_act, up_act, shared_ds, d_shared = moe_rows(
        fs, ffn, row_halves, dy_halves, slot_of, shared_w, gate_w, up_w
    )
    me = jnp.zeros((1,), jnp.int32)

    name = (jnp.arange(128, dtype=jnp.int32) == j * fs + i).astype(f32)[None]
    big, flows = [], []
    dy_in = all_dy
    for g in range(fs // per):
        results = moe_back(
            g * per,
            per,
            tp,
            fs,
            g % 2 == 0,
            me,
            dy_in,
            gate_act,
            up_act,
            slot_of,
            slot_col,
            weight,
            shared_ds,
            shared_w,
            gate_w,
            up_w,
            down_w,
            name,
            big,
        )
        big = list(results[:3])
        dy_in = after(all_dy, results[4])
        flows.append(reduce_core(results[3], results[4]))
    all_dg, all_du, all_hw = big

    def split_cols(value):
        return value.reshape(value.shape[0], fs, dpart).transpose(1, 0, 2)

    d_gate_w = weight_grads(after(all_dg, *flows), all_slots, fs)
    gate_back = turn(d_gate_w)
    firsts = [reduce_lead(flow, "ctx" if g % 2 else "tp") for g, flow in enumerate(flows)]
    out_args = (slot_col, shared_ds, shared_w, down_w)
    outs = [
        moe_out(g * per, per, tp, fs, g % 2 == 1, me, after(all_hw, d_gate_w), *out_args)
        for g in range(fs // per)
    ]
    firsts = [after(flow, *outs[0], *outs[-1]) for flow in firsts]
    seconds = [reduce_lead(flow, "tp" if g % 2 else "ctx") for g, flow in enumerate(firsts)]
    home = after(jnp.concatenate(seconds, axis=0), gate_back)
    d_up_w = weight_grads(after(all_du, home), all_slots, fs)
    d_down_w = weight_grads(after(all_hw, home), all_dy, fs, d_shared, sh)
    out_flows = [
        reduce_lead(after(reduce_core(keep, send), home), "ctx" if g % 2 else "tp")
        for g, (keep, send) in enumerate(outs)
    ]
    home_own = jnp.sum(turn(home).astype(f32), axis=0)
    home_own = after(home_own, d_up_w, d_down_w, *out_flows)
    up_back = turn(after(d_up_w, home_own))
    grad_total, gate_cols = home_own[:, :width], home_own[:, width:]
    in_order = jnp.arange(EXPERTS, dtype=jnp.int32)

    def lay_out(blocks):
        return assemble([blocks.reshape(EXPERTS, -1, dpart)], in_order, EXPERTS, ffn)

    grad_mid_norm, d_gain_moe = norm_back(middle, moe_scale, gain_mix, grad_total)
    grad_mid = dy_own.astype(f32) + grad_mid_norm
    grad_low = grad_mid.astype(bf16)
    grad_cur = spread_ctx(grad_low[None, None])
    gate_blocks = lax.all_gather(after(gate_back, grad_cur), "ctx", axis=0)
    grad_all = spread_core(spread_tp(grad_cur)).reshape(length, width)

    down_back = turn(after(d_down_w, up_back))
    gate_shards = lay_out(gate_blocks)
    keep, send, grad_q, grad_expanded = attend_back(
        hd,
        (tp, cx // 2, n),
        grad_all,
        output_w,
        attn_prob,
        heads_out,
        expanded,
        latent_low,
        queries,
        cos_rel,
        sin_rel,
        query_t,
        expand_w,
    )
    up_blocks = lax.all_gather(after(up_back, grad_q), "ctx", axis=0)
    summed = reduce_plane(leading(keep), leading(send), up_back, gate_shards)
    out_flows = [
        reduce_lead(after(flow, summed), "tp" if g % 2 else "ctx")
        for g, flow in enumerate(out_flows)
    ]
    out_home = jnp.concatenate(out_flows, axis=0)
    d_attn, d_w_expand = attend_weights(
        fs, grad_all, heads_out, after(grad_q, send), normed_all, grad_expanded, latent_low
    )
    summed = after(summed, d_attn)
    grad_latent_own = summed[:, width : width + LATENT + ROPE]
    up_shards = lay_out(up_blocks)
    latent_scale = lax.rsqrt(
        jnp.mean(latent_raw[:n, :LATENT] ** 2, axis=-1, keepdims=True) + EPSILON
    )
    grad_lat_raw, d_gain_latent = norm_back(
        latent_raw[:n, :LATENT], latent_scale, gain_lat, grad_latent_own[:, :LATENT]
    )
    grad_kv_raw = jnp.concatenate(
        [grad_lat_raw, rotate_back(grad_latent_own[:, LATENT:], cos_rel[:n], sin_rel[:n])], axis=1
    ).astype(bf16)
    grad_normed = summed[:, :width] + mm(grad_kv_raw, latent_t)
    kv_all = gather_plane(grad_kv_raw).reshape(length, -1)
    d_w_latent = mm_tn(
        lax.dynamic_slice_in_dim(kv_all, j * lat_cols, lat_cols, 1), normed_all
    ).astype(bf16)
    ex_part = d_w_expand.size // (fs * dpart)
    pack = jnp.concatenate(
        [d_attn, d_w_expand.reshape(fs, ex_part, dpart), split_cols(d_w_latent)], axis=1
    )
    bits = list(low_bits(fs))
    pack_sum = hops(pack, bits[:1])
    out_sum = hops(after(out_home, pack_sum), bits[:1])
    pack_sum = after(pack_sum, up_shards)
    pack_total = hops(pack_sum, bits[1:])[0]
    out_total = hops(out_sum, bits[1:])[0]
    down_blocks = lax.all_gather(after(down_back, d_w_latent), "ctx", axis=0)
    grad_x_norm, d_gain_attn = norm_back(x_rel, attn_scale[:n], gain_norm, grad_normed)
    input_own = (grad_mid + grad_x_norm).astype(bf16)
    input_grad = rel_tp(spread_tp(input_own[None, None]).reshape(rows_dev, width)).astype(f32)

    out_own_rows = (middle + out_total).astype(bf16)
    layer_out = rel_tp(spread_tp(out_own_rows[None, None]).reshape(rows_dev, width))

    gate_cols = spread_tp(gate_cols[:, :EXPERTS][None, None]).reshape(rows_dev, EXPERTS)
    gate_cols = rel_tp(gate_cols)
    experts = jnp.arange(EXPERTS, dtype=jnp.int32)
    gates_grad = jnp.sum(
        jnp.where(routes[:, :, None] == experts, gate_cols[:, None, :], 0.0), axis=-1
    )

    blocks = over_ctx(pack_total.astype(bf16))
    at_q, at_e = hd * VHEAD, hd * VHEAD + q_cols
    by_group = [(j ^ m) // share for m in members]
    w_out_grad = place(
        w_out.shape, f32, [v[:at_q] for v in blocks], [g * hd * VHEAD for g in by_group], 0
    )
    w_query_grad = place(
        w_query.shape[::-1], f32, [v[at_q:at_e] for v in blocks], [g * q_cols for g in by_group], 0
    ).T
    w_expand_grad = place(
        w_expand.shape,
        f32,
        [
            v[at_e : at_e + ex_part].reshape(w_expand.shape[0], hd * kv_width) for v in blocks
        ],
        [g * hd * kv_width for g in by_group],
        1,
    )
    w_latent_grad = place(
        w_latent.shape[::-1],
        f32,
        [v[at_e + ex_part :] for v in blocks],
        [(j ^ m) * lat_cols for m in members],
        0,
    ).T

    gain_parts = jnp.concatenate(
        [
            d_gain_attn.reshape(fs, -1),
            d_gain_moe.reshape(fs, -1),
            d_gain_latent.reshape(fs, -1),
        ],
        axis=1,
    )
    gain_sum = jnp.sum(turn(after(gain_parts[:, None, :], pack_total)), axis=0)
    for bit in low_bits(tp):
        gain_sum = gain_sum + exchange(gain_sum, "tp", bit)
    for bit in low_bits(cx):
        gain_sum = gain_sum + exchange(gain_sum, "ctx", bit)
    gain_sum = gain_sum[0]
    cut_a, cut_b = gain_attn.shape[0], gain_attn.shape[0] + gain_moe.shape[0]

    expert_gate_grad = gate_shards.transpose(0, 2, 1)
    expert_up_grad = up_shards.transpose(0, 2, 1)
    expert_down_grad = lay_out(down_blocks)
    shared_grads = down_blocks[:, :, ffn:].reshape(cx, fs, 3, sh, dpart).transpose(2, 0, 1, 3, 4)
    shared_grads = shared_grads.reshape(3, cx * fs * sh, dpart).astype(f32)
    shared_gate_grad = shared_grads[0].T
    shared_up_grad = shared_grads[1].T
    shared_down_grad = shared_grads[2]

    return (
        layer_out,
        input_grad,
        gates_grad,
        gain_sum[:cut_a],
        gain_sum[cut_b:],
        w_query_grad,
        w_latent_grad,
        w_expand_grad,
        w_out_grad,
        gain_sum[cut_a:cut_b],
        expert_gate_grad,
        expert_up_grad,
        expert_down_grad,
        shared_gate_grad,
        shared_up_grad,
        shared_down_grad,
    )


def solution(mesh):
    placed = (
        P(("fsdp", "ctx"), None),
        P(("fsdp", "ctx"), None),
        P(("fsdp", "ctx"), None),
        P(("fsdp", "ctx"), None),
        P("fsdp"),
        P("fsdp"),
        P("fsdp", "tp"),
        P("fsdp", None),
        P("fsdp", "tp"),
        P("tp", "fsdp"),
        P("fsdp"),
        P(None, "fsdp", "tp"),
        P(None, "fsdp", "tp"),
        P(None, "tp", "fsdp"),
        P("fsdp", "tp"),
        P("fsdp", "tp"),
        P("tp", "fsdp"),
    )
    return jax.shard_map(
        local,
        mesh=mesh,
        in_specs=placed,
        out_specs=(
            P(("fsdp", "ctx"), None),
            P(("fsdp", "ctx"), None),
            P(("fsdp", "ctx"), None),
            P("fsdp"),
            P("fsdp"),
            P("fsdp", "tp"),
            P("fsdp", None),
            P("fsdp", "tp"),
            P("tp", "fsdp"),
            P("fsdp"),
            P(None, "fsdp", "tp"),
            P(None, "fsdp", "tp"),
            P(None, "tp", "fsdp"),
            P("fsdp", "tp"),
            P("fsdp", "tp"),
            P("tp", "fsdp"),
        ),
        check_vma=False,
    )
```

```python
import math

import jax
import jax.numpy as jnp
from jax import lax
from jax.experimental import pallas as pl
from jax.experimental.pallas import tpu as pltpu
from jax.sharding import PartitionSpec as P

NOPE = 128
ROPE = 64
LATENT = 512
VHEAD = 128
EXPERTS = 16
TOPK = 6
CAPACITY = 128
EPSILON = 1e-06

f32 = jnp.float32
bf16 = jnp.bfloat16


def norm_rows(values, gain_vec):
    scales = lax.rsqrt(jnp.mean(values * values, axis=-1, keepdims=True) + EPSILON)
    return (values * scales * gain_vec, scales)


def norm_back(values, scales, gain_vec, gradient):
    weighted = gradient * gain_vec
    inner = jnp.mean(weighted * values, axis=-1, keepdims=True)
    return (
        scales * weighted - values * scales**3 * inner,
        jnp.sum(gradient * values * scales, axis=0),
    )


def angle_tables(position, width):
    half_width = width // 2
    frequency = jnp.exp(
        jnp.arange(half_width, dtype=f32) * (-2.0 * math.log(10000.0) / width)
    )
    angles = position.astype(f32)[:, None] * frequency[None, :]
    return (jnp.cos(angles), jnp.sin(angles))


def rotate(values, cosine, sine_tab):
    half_width = values.shape[-1] // 2
    front_half = values[..., :half_width]
    back_half = values[..., half_width:]
    return jnp.concatenate(
        [front_half * cosine - back_half * sine_tab, back_half * cosine + front_half * sine_tab],
        axis=-1,
    )


def rotate_back(gradient, cosine, sine_tab):
    return rotate(gradient, cosine, -sine_tab)


def swiglu_back(gate_act, up_act, grad_hidden):
    sigmoid_g = jax.nn.sigmoid(gate_act)
    grad_up = (grad_hidden * gate_act * sigmoid_g).astype(bf16)
    grad_gate = (grad_hidden * up_act * sigmoid_g * (1.0 + gate_act * (1.0 - sigmoid_g))).astype(
        bf16
    )
    return (grad_gate, grad_up)


def mm(left, right):
    return jnp.dot(left, right, preferred_element_type=f32)


def mm_nt(left, right):
    return lax.dot_general(left, right, (((1,), (1,)), ((), ())), preferred_element_type=f32)


def mm_tn(left, right):
    return lax.dot_general(left, right, (((0,), (0,)), ((), ())), preferred_element_type=f32)


def after(value, *earlier):
    return lax.optimization_barrier((value,) + earlier)[0]


def exchange(value, axis, bit):
    size = lax.axis_size(axis)
    return lax.ppermute(value, axis, [(a, a ^ bit) for a in range(size)])


def high_bits(size):
    bit = size // 2
    while bit >= 2:
        yield bit
        bit //= 2


def low_bits(size):
    bit = 1
    while bit < size:
        yield bit
        bit *= 2


def place(shape, dtype, parts, starts, axis):
    buffer = jnp.zeros(shape, dtype)
    for part, start in zip(parts, starts):
        buffer = lax.dynamic_update_slice_in_dim(buffer, part.astype(dtype), start, axis)
    return buffer


def slot_masks(row_ref, pieces, tokens):
    iota = lax.broadcasted_iota(jnp.int32, (CAPACITY, tokens), 0)
    return [iota == row_ref[a] for a in range(pieces)]


def one_hot(mask):
    return jnp.where(mask, 1.0, 0.0).astype(bf16)


def rows_kernel(pieces, fs, steps, groups, *refs):
    row_ref, ws_ref = refs[:2]
    xs, dys = refs[2 : 2 + 2 * groups], refs[2 + 2 * groups : 2 + 4 * groups]
    wg, wu = refs[2 + 4 * groups : 4 + 4 * groups]
    slots_ref, sdy_ref, gate_ref, up_ref, ds_ref, dsh_ref, xbuf, dybuf, sems = refs[
        4 + 4 * groups :
    ]
    ffn = gate_ref.shape[1]
    step = pl.program_id(0)
    slot = lax.rem(step, 2)
    width = xbuf.shape[4]
    tokens = xbuf.shape[2] * xbuf.shape[3]
    dpart = wg.shape[2]
    shp = ws_ref.shape[0] // 3
    per = steps // (2 * groups)

    def begin(at, into):
        for q in range(steps):

            @pl.when(at == q)
            def _(q=q):
                chunk, other = q // 2, q % 2
                which, c = 2 * (chunk // per) + other, chunk % per
                pltpu.make_async_copy(xs[which].at[:, :, c], xbuf.at[into], sems.at[into, 0]).start()
                pltpu.make_async_copy(
                    dys[which].at[:, :, c], dybuf.at[into], sems.at[into, 1]
                ).start()

    @pl.when(step == 0)
    def _():
        begin(step, 0)

    @pl.when(step + 1 < steps)
    def _():
        begin(step + 1, 1 - slot)

    pltpu.make_async_copy(xs[0].at[:, :, 0], xbuf.at[slot], sems.at[slot, 0]).wait()
    pltpu.make_async_copy(dys[0].at[:, :, 0], dybuf.at[slot], sems.at[slot, 1]).wait()
    masks = slot_masks(row_ref, pieces, tokens)
    for a in range(pieces):
        pick = one_hot(masks[a])
        of = slice(a * CAPACITY, (a + 1) * CAPACITY)
        slots_ref[of, :] = mm(pick, xbuf[slot, a].reshape(tokens, width)).astype(bf16)
        sdy_ref[of, :] = mm(pick, dybuf[slot, a].reshape(tokens, width)).astype(bf16)
    gate_act = up_act = None
    for s in range(fs):
        part = slots_ref[:, s * dpart : (s + 1) * dpart]
        g, u = mm_nt(part, wg[s]), mm_nt(part, wu[s])
        gate_act = g if s == 0 else gate_act + g
        up_act = u if s == 0 else up_act + u
    gate_ref[...] = gate_act
    up_ref[...] = up_act
    flat = xbuf[slot].reshape(pieces * tokens, width)
    dflat = dybuf[slot].reshape(pieces * tokens, width)
    both = mm_nt(flat, ws_ref[: 2 * shp])
    sg, su = both[:, :shp], both[:, shp:]
    sd = mm_nt(dflat, ws_ref[2 * shp :])
    sig = 1.0 / (1.0 + jnp.exp(-sg))
    silu = sg * sig
    s_hid = (silu * su).astype(bf16)
    ds_up = (sd * silu).astype(bf16)
    ds_gate = (sd * su * sig * (1.0 + sg * (1.0 - sig))).astype(bf16)
    ds_ref[:, :shp] = ds_gate
    ds_ref[:, shp : 2 * shp] = ds_up
    ds_ref[:, 2 * shp :] = s_hid
    first = mm_tn(ds_ref[:, : 2 * shp], flat)
    second = mm_tn(s_hid, dflat)

    @pl.when(step == 0)
    def _():
        dsh_ref[: 2 * shp] = first
        dsh_ref[2 * shp :] = second

    @pl.when(step > 0)
    def _():
        dsh_ref[: 2 * shp] += first
        dsh_ref[2 * shp :] += second


def moe_rows(fs, ffn, xs, dys, slot_row, shared, gate_w, up_w):
    pieces, tp, per, n, width = xs[0].shape
    groups = len(xs) // 2
    tokens = tp * n
    steps = 2 * groups * per
    shp = shared.shape[0] // 3
    slots = pieces * CAPACITY
    once = pl.Buffered(buffer_count=1)

    def by_step(shape):
        return pl.BlockSpec(shape, lambda q: (q,) + (0,) * (len(shape) - 1))

    def fixed(shape):
        return pl.BlockSpec(shape, lambda q: (0,) * len(shape), pipeline_mode=once)

    total = steps * slots
    return pl.pallas_call(
        lambda *refs: rows_kernel(pieces, fs, steps, groups, *refs),
        grid=(steps,),
        in_specs=[by_step((pieces, 1, tokens)), fixed((3 * shp, width))]
        + [pl.BlockSpec(memory_space=pl.ANY)] * (4 * groups)
        + [fixed(gate_w.shape), fixed(up_w.shape)],
        out_specs=[
            by_step((slots, width)),
            by_step((slots, width)),
            by_step((slots, ffn)),
            by_step((slots, ffn)),
            by_step((pieces * tokens, 3 * shp)),
            fixed((3 * shp, width)),
        ],
        scratch_shapes=[
            pltpu.VMEM((2, pieces, tp, n, width), bf16),
            pltpu.VMEM((2, pieces, tp, n, width), bf16),
            pltpu.SemaphoreType.DMA((2, 2)),
        ],
        out_shape=[
            jax.ShapeDtypeStruct((total, width), bf16),
            jax.ShapeDtypeStruct((total, width), bf16),
            jax.ShapeDtypeStruct((total, ffn), f32),
            jax.ShapeDtypeStruct((total, ffn), f32),
            jax.ShapeDtypeStruct((steps * pieces * tokens, 3 * shp), bf16),
            jax.ShapeDtypeStruct((3 * shp, width), f32),
        ],
        compiler_params=pltpu.CompilerParams(vmem_limit_bytes=60 * 1024 * 1024),
        cost_estimate=pl.CostEstimate(flops=0, bytes_accessed=1_000_000, transcendentals=0),
        name="moe_rows",
    )(slot_row, shared, *xs, *dys, gate_w, up_w)


def back_kernel(pieces, fs, extra, tp_first, me_ref, *refs):
    sdy_ref, gate_ref, up_ref, row_ref, col_ref, wt_ref, ds_ref, ws_ref, wg, wu, wd = refs[:11]
    name_ref = refs[11]
    dg_ref, du_ref, hw_ref, keep_ref, send_ref = refs[12 + extra :]
    ffn = gate_ref.shape[1]
    n, width = keep_ref.shape[3], ws_ref.shape[1]
    half = lax.rem(pl.program_id(0), 2)
    tokens = row_ref.shape[2]
    dpart = wg.shape[2]
    shp = ws_ref.shape[0] // 3
    masks = slot_masks(row_ref, pieces, tokens)
    weight = jnp.concatenate(
        [
            jnp.sum(jnp.where(masks[a], wt_ref[a], 0.0), axis=1, keepdims=True)
            for a in range(pieces)
        ],
        axis=0,
    )
    dy_down = None
    for s in range(fs):
        d = mm_nt(sdy_ref[:, s * dpart : (s + 1) * dpart], wd[s])
        dy_down = d if s == 0 else dy_down + d
    gate_act, up_act = gate_ref[...], up_ref[...]
    sig = 1.0 / (1.0 + jnp.exp(-gate_act))
    silu = gate_act * sig
    hidden = (silu * up_act).astype(bf16).astype(f32)
    slot_grad = jnp.sum(hidden * dy_down, axis=1, keepdims=True)
    hw_ref[...] = (weight * hidden).astype(bf16)
    d_hidden = weight * dy_down
    du_ref[...] = (d_hidden * silu).astype(bf16)
    dg_ref[...] = (d_hidden * up_act * sig * (1.0 + gate_act * (1.0 - sig))).astype(bf16)
    across = lax.broadcasted_iota(jnp.int32, (tokens, CAPACITY), 1)
    picks = [one_hot(across == col_ref[a]) for a in range(pieces)]

    def write(a, at, value):
        for t in range(tokens // n):
            rows = value[t * n : (t + 1) * n]
            at_t = me_ref[0] ^ t
            index = (at_t, a) if tp_first else (a, at_t)

            @pl.when(half == 0)
            def _():
                keep_ref[index[0], index[1], 0, :, at] = rows

            @pl.when(half == 1)
            def _():
                send_ref[index[0], index[1], 0, :, at] = rows

    for s in range(fs):
        at = slice(s * dpart, (s + 1) * dpart)
        back = (
            mm(dg_ref[...], wg[s]) + mm(du_ref[...], wu[s])
        ).astype(bf16)
        s_back = mm(ds_ref[:, : 2 * shp], ws_ref[: 2 * shp, at])
        for a in range(pieces):
            part = mm(picks[a], back[a * CAPACITY : (a + 1) * CAPACITY])
            write(a, at, (part + s_back[a * tokens : (a + 1) * tokens]).astype(bf16))
    spread = (slot_grad * name_ref[...]).astype(bf16)
    for a in range(pieces):
        part = mm(picks[a], spread[a * CAPACITY : (a + 1) * CAPACITY])
        write(a, slice(width, width + 128), part.astype(bf16))


def moe_back(
    first, chunks, tp, fs, tp_first, me, sdy, gate, up, slot_row, slot_col, weight, ds, shared, gate_w, up_w, down_w, name, big
):
    width = sdy.shape[1]
    all_pieces, _, tokens = slot_row.shape
    pieces = all_pieces // (2 * fs)
    ffn, dpart = down_w.shape[1:]
    shp = shared.shape[0] // 3
    slots = pieces * CAPACITY
    once = pl.Buffered(buffer_count=1)

    def by_step(shape):
        return pl.BlockSpec(shape, lambda q, me: (2 * first + q,) + (0,) * (len(shape) - 1))

    def fixed(shape):
        return pl.BlockSpec(shape, lambda q, me: (0,) * len(shape), pipeline_mode=once)

    n = tokens // tp
    outer = (tp, pieces) if tp_first else (pieces, tp)
    half_spec = pl.BlockSpec(outer + (1, n, width + 128), lambda q, me: (0, 0, q // 2, 0, 0))
    total = sdy.shape[0]
    half = jax.ShapeDtypeStruct(outer + (chunks, n, width + 128), bf16)
    return pl.pallas_call(
        lambda *refs: back_kernel(pieces, fs, len(big), tp_first, *refs),
        grid_spec=pltpu.PrefetchScalarGridSpec(
            num_scalar_prefetch=1,
            grid=(2 * chunks,),
            in_specs=[
                by_step((slots, width)),
                by_step((slots, ffn)),
                by_step((slots, ffn)),
                by_step((pieces, 1, tokens)),
                by_step((pieces, tokens, 1)),
                by_step((pieces, 1, tokens)),
                by_step((pieces * tokens, 3 * shp)),
                fixed((3 * shp, width)),
            ]
            + [fixed(gate_w.shape), fixed(up_w.shape), fixed((fs, ffn, dpart))]
            + [fixed((1, 128))]
            + [pl.BlockSpec(memory_space=pl.ANY)] * len(big),
            out_specs=[
                by_step((slots, ffn)),
                by_step((slots, ffn)),
                by_step((slots, ffn)),
                half_spec,
                half_spec,
            ],
        ),
        out_shape=[
            jax.ShapeDtypeStruct((total, ffn), bf16),
            jax.ShapeDtypeStruct((total, ffn), bf16),
            jax.ShapeDtypeStruct((total, ffn), bf16),
            half,
            half,
        ],
        input_output_aliases={13 + b: b for b in range(len(big))},
        compiler_params=pltpu.CompilerParams(vmem_limit_bytes=60 * 1024 * 1024),
        cost_estimate=pl.CostEstimate(flops=0, bytes_accessed=1_000_000, transcendentals=0),
        name="moe_back",
    )(me, sdy, gate, up, slot_row, slot_col, weight, ds, shared, gate_w, up_w, down_w, name, *big)


def out_kernel(pieces, fs, ctx_first, me_ref, hw_ref, col_ref, ds_ref, ws_ref, wd, keep_ref, send_ref):
    tokens = col_ref.shape[1]
    n = keep_ref.shape[3]
    half = lax.rem(pl.program_id(0), 2)
    dpart = wd.shape[2]
    across = lax.broadcasted_iota(jnp.int32, (tokens, CAPACITY), 1)
    picks = [one_hot(across == col_ref[a]) for a in range(pieces)]
    for s in range(fs):
        at = slice(s * dpart, (s + 1) * dpart)
        out = mm(hw_ref[...], wd[s]).astype(bf16)
        shared = mm(ds_ref[...], ws_ref[:, at])
        for a in range(pieces):
            part = mm(picks[a], out[a * CAPACITY : (a + 1) * CAPACITY])
            value = (part + shared[a * tokens : (a + 1) * tokens]).astype(bf16)
            for t in range(tokens // n):
                rows = value[t * n : (t + 1) * n]
                at_t = me_ref[0] ^ t
                index = (a, at_t) if ctx_first else (at_t, a)

                @pl.when(half == 0)
                def _():
                    keep_ref[index[0], index[1], 0, :, at] = rows

                @pl.when(half == 1)
                def _():
                    send_ref[index[0], index[1], 0, :, at] = rows


def moe_out(first, chunks, tp, fs, ctx_first, me, hw, slot_col, ds, shared, down_w):
    all_pieces, tokens, _ = slot_col.shape
    ffn, dpart = down_w.shape[1:]
    width = shared.shape[1]
    shp = shared.shape[0] // 3
    pieces = all_pieces // (2 * fs)
    n = tokens // tp
    once = pl.Buffered(buffer_count=1)
    slots = 2 * chunks * pieces * CAPACITY
    outer = (pieces, tp) if ctx_first else (tp, pieces)
    half_spec = pl.BlockSpec(outer + (1, n, width), lambda q, me: (0, 0, q // 2, 0, 0))
    return pl.pallas_call(
        lambda *refs: out_kernel(pieces, fs, ctx_first, *refs),
        grid_spec=pltpu.PrefetchScalarGridSpec(
            num_scalar_prefetch=1,
            grid=(2 * chunks,),
            in_specs=[
                pl.BlockSpec((pieces * CAPACITY, ffn), lambda q, me: (2 * first + q, 0)),
                pl.BlockSpec((pieces, tokens, 1), lambda q, me: (2 * first + q, 0, 0)),
                pl.BlockSpec((pieces * tokens, shp), lambda q, me: (2 * first + q, 2)),
                pl.BlockSpec((shp, width), lambda q, me: (2, 0), pipeline_mode=once),
                pl.BlockSpec((fs, ffn, dpart), lambda q, me: (0, 0, 0), pipeline_mode=once),
            ],
            out_specs=[half_spec, half_spec],
        ),
        out_shape=[jax.ShapeDtypeStruct(outer + (chunks, n, width), bf16)] * 2,
        compiler_params=pltpu.CompilerParams(vmem_limit_bytes=40 * 1024 * 1024),
        cost_estimate=pl.CostEstimate(flops=0, bytes_accessed=1_000_000, transcendentals=0),
        name="moe_out",
    )(me, hw, slot_col, ds, shared, down_w)


def turned(front, back, cosine, sine):
    return front * cosine - back * sine, back * cosine + front * sine


def attend_kernel(hd, normed, query, latent, expand, out_w, gain, cos, sin, posq, posk, *outs):
    keep_ref, send_ref, raw_ref, low_ref, q_ref, ex_ref, prob_ref, heads_ref = outs
    length = normed.shape[0]
    q_width, kv_width, turn = NOPE + ROPE, NOPE + VHEAD, ROPE // 2
    scaling = q_width ** (-0.5)
    q_raw = mm_nt(normed[...], query[...])
    for h in range(hd):
        at = h * q_width
        q_ref[:, at : at + NOPE] = q_raw[:, at : at + NOPE].astype(bf16)
        front, back = q_raw[:, at + NOPE : at + NOPE + turn], q_raw[:, at + NOPE + turn : at + q_width]
        front, back = turned(front, back, cos[...], sin[...])
        q_ref[:, at + NOPE : at + NOPE + turn] = front.astype(bf16)
        q_ref[:, at + NOPE + turn : at + q_width] = back.astype(bf16)
    raw = mm_nt(normed[...], latent[...])
    raw_ref[...] = raw
    body = raw[:, :LATENT]
    scales = lax.rsqrt(jnp.mean(body * body, axis=-1, keepdims=True) + EPSILON)
    low_ref[:, :LATENT] = (body * scales * gain[...]).astype(bf16)
    front, back = turned(raw[:, LATENT : LATENT + turn], raw[:, LATENT + turn :], cos[...], sin[...])
    low_ref[:, LATENT : LATENT + turn] = front.astype(bf16)
    low_ref[:, LATENT + turn :] = back.astype(bf16)
    ex_ref[...] = mm(low_ref[:, :LATENT], expand[...]).astype(bf16)
    rope = low_ref[:, LATENT:]
    block = min(256, length)
    for h in range(hd):
        at, kv = h * q_width, h * kv_width
        keys, vals = ex_ref[:, kv : kv + NOPE], ex_ref[:, kv + NOPE : kv + kv_width]
        for r in range(0, length, block):
            rows = slice(r, r + block)
            scores = mm_nt(q_ref[rows, at : at + NOPE], keys)
            scores = (scores + mm_nt(q_ref[rows, at + NOPE : at + q_width], rope)) * scaling
            scores = jnp.where(posk[...] <= posq[rows, :], scores, -1e30)
            exponent = jnp.exp(scores - jnp.max(scores, axis=-1, keepdims=True))
            total = jnp.sum(exponent, axis=-1, keepdims=True)
            prob = (exponent / total).astype(bf16)
            prob_ref[h, rows, :] = prob
            heads_ref[rows, h * VHEAD : (h + 1) * VHEAD] = mm(prob, vals).astype(bf16)
    tp, pairs, n, _ = keep_ref.shape
    for ref, start in ((send_ref, length // 2), (keep_ref, 0)):
        for p in range(pairs):
            for t in range(tp):
                at = start + (p * tp + t) * n
                ref[t, p] = mm(heads_ref[at : at + n], out_w[...]).astype(bf16)


def whole_call(body, operands, out_shape, name, declared=1_000_000):
    return pl.pallas_call(
        body,
        in_specs=[pl.BlockSpec(memory_space=pltpu.VMEM)] * len(operands),
        out_specs=[pl.BlockSpec(memory_space=pltpu.VMEM)] * len(out_shape),
        out_shape=[jax.ShapeDtypeStruct(shape, dtype) for shape, dtype in out_shape],
        compiler_params=pltpu.CompilerParams(vmem_limit_bytes=60 * 1024 * 1024),
        cost_estimate=pl.CostEstimate(flops=0, bytes_accessed=declared, transcendentals=0),
        name=name,
    )(*operands)


def attend(hd, lead, normed, query, latent, expand, out_w, gain, cos, sin, position):
    length, width = normed.shape
    operands = (
        normed,
        query,
        latent,
        expand,
        out_w,
        gain[None],
        cos,
        sin,
        position[:, None],
        position[None],
    )
    out_shape = [
        (lead + (width,), bf16),
        (lead + (width,), bf16),
        ((length, LATENT + ROPE), f32),
        ((length, LATENT + ROPE), bf16),
        ((length, hd * (NOPE + ROPE)), bf16),
        ((length, hd * (NOPE + VHEAD)), bf16),
        ((hd, length, length), bf16),
        ((length, hd * VHEAD), bf16),
    ]
    return whole_call(lambda *refs: attend_kernel(hd, *refs), operands, out_shape, "attend")


def attend_back_kernel(hd, grad, out_w, prob, heads, ex, low, q, cos, sin, query, expand, *outs):
    keep_ref, send_ref, dq_ref, dex_ref = outs
    length, width = grad.shape
    half = length // 2
    q_width, kv_width, turn = NOPE + ROPE, NOPE + VHEAD, ROPE // 2
    scaling = q_width ** (-0.5)
    d_heads = mm_nt(grad[...], out_w[...]).astype(bf16)
    rope = low[:, LATENT:]
    block = min(256, length)
    d_rope = None
    for h in range(hd):
        at, kv = h * q_width, h * kv_width
        of = slice(h * VHEAD, (h + 1) * VHEAD)
        keys, vals = ex[:, kv : kv + NOPE], ex[:, kv + NOPE : kv + kv_width]
        d_key = d_kr = d_val = None
        for r in range(0, length, block):
            rows = slice(r, r + block)
            d_out = d_heads[rows, of]
            inner = jnp.sum(
                d_out.astype(f32) * heads[rows, of].astype(f32), axis=-1, keepdims=True
            )
            p = prob[h, rows, :]
            d_scores = (p.astype(f32) * (mm_nt(d_out, vals) - inner)).astype(bf16)
            dq_ref[rows, at : at + NOPE] = (mm(d_scores, keys) * scaling).astype(bf16)
            d_turn = mm(d_scores, rope) * scaling
            front, back = turned(d_turn[:, :turn], d_turn[:, turn:], cos[rows, :], -sin[rows, :])
            dq_ref[rows, at + NOPE : at + NOPE + turn] = front.astype(bf16)
            dq_ref[rows, at + NOPE + turn : at + q_width] = back.astype(bf16)
            one = mm_tn(d_scores, q[rows, at : at + NOPE])
            two = mm_tn(d_scores, q[rows, at + NOPE : at + q_width])
            three = mm_tn(p, d_out)
            d_key = one if r == 0 else d_key + one
            d_kr = two if r == 0 else d_kr + two
            d_val = three if r == 0 else d_val + three
        dex_ref[:, kv : kv + NOPE] = (d_key * scaling).astype(bf16)
        dex_ref[:, kv + NOPE : kv + kv_width] = d_val.astype(bf16)
        d_rope = d_kr if h == 0 else d_rope + d_kr
    d_rope = (d_rope * scaling).astype(bf16)
    tp, pairs, n, _ = keep_ref.shape
    for ref, start in ((send_ref, half), (keep_ref, 0)):
        for p in range(pairs):
            for t in range(tp):
                at = start + (p * tp + t) * n
                rows = slice(at, at + n)
                ref[t, p, :, :width] = mm(dq_ref[rows, :], query[...]).astype(bf16)
                ref[t, p, :, width : width + LATENT] = mm_nt(dex_ref[rows, :], expand[...]).astype(
                    bf16
                )
                ref[t, p, :, width + LATENT : width + LATENT + ROPE] = d_rope[rows]
                if ref.shape[3] > width + LATENT + ROPE:
                    ref[t, p, :, width + LATENT + ROPE :] = jnp.zeros(
                        (n, ref.shape[3] - width - LATENT - ROPE), bf16
                    )


def attend_back(hd, lead, grad, out_w, prob, heads, ex, low, q, cos, sin, query, expand):
    cols = -(-(grad.shape[1] + LATENT + ROPE) // 128) * 128
    operands = (grad, out_w, prob, heads, ex, low, q, cos, sin, query, expand)
    out_shape = [
        (lead + (cols,), bf16),
        (lead + (cols,), bf16),
        (q.shape, bf16),
        (ex.shape, bf16),
    ]
    return whole_call(
        lambda *refs: attend_back_kernel(hd, *refs), operands, out_shape, "attend_back"
    )


def attend_weights_kernel(grad, heads, dq, normed, dex, low, dw_ref, de_ref):
    fs, _, dpart = dw_ref.shape
    first = heads.shape[1]
    for z in range(fs):
        at = slice(z * dpart, (z + 1) * dpart)
        dw_ref[z, :first] = mm_tn(heads[...], grad[:, at]).astype(bf16)
        dw_ref[z, first:] = mm_tn(dq[...], normed[:, at]).astype(bf16)
    de_ref[...] = mm_tn(low[:, :LATENT], dex[...]).astype(bf16)


def attend_weights(fs, grad, heads, dq, normed, dex, low):
    rows = heads.shape[1] + dq.shape[1]
    out_shape = [((fs, rows, grad.shape[1] // fs), bf16), ((LATENT, dex.shape[1]), bf16)]
    return whole_call(
        attend_weights_kernel,
        (grad, heads, dq, normed, dex, low),
        out_shape,
        "attend_weights",
        30_000_000,
    )


def weight_grads(left, right, fs, more=None, sh=0):
    slots, ffn = left.shape
    dpart = right.shape[1] // fs
    extra = 3 * sh if more is not None else 0
    once = pl.Buffered(buffer_count=1)

    def body(left_ref, right_ref, *refs):
        out_ref = refs[-1]
        out_ref[0, :ffn] = mm_tn(left_ref[...], right_ref[...]).astype(bf16)
        if more is not None:
            shp = more.shape[0] // 3
            for b in range(3):
                out_ref[0, ffn + b * sh : ffn + (b + 1) * sh] = refs[0][
                    b * shp : b * shp + sh
                ].astype(bf16)

    in_specs = [
        pl.BlockSpec((slots, ffn), lambda z: (0, 0), pipeline_mode=once),
        pl.BlockSpec((slots, dpart), lambda z: (0, z)),
    ]
    operands = [left, right]
    if more is not None:
        in_specs.append(pl.BlockSpec((more.shape[0], dpart), lambda z: (0, z)))
        operands.append(more)
    return pl.pallas_call(
        body,
        grid=(fs,),
        in_specs=in_specs,
        out_specs=pl.BlockSpec((1, ffn + extra, dpart), lambda z: (z, 0, 0)),
        out_shape=jax.ShapeDtypeStruct((fs, ffn + extra, dpart), bf16),
        compiler_params=pltpu.CompilerParams(vmem_limit_bytes=50 * 1024 * 1024),
        cost_estimate=pl.CostEstimate(flops=0, bytes_accessed=1_000_000, transcendentals=0),
        name="weight_grads",
    )(*operands)


def assemble(blocks, dest, count, rows):
    each, _, cols = blocks[0].shape
    parts = len(blocks)

    def body(dest_ref, *refs):
        step = pl.program_id(0)
        for q in range(parts):

            @pl.when(step // each == q)
            def _(q=q):
                refs[parts][...] = refs[q][...].astype(f32)

    def source(q):
        return pl.BlockSpec(
            (1, rows, cols), lambda g, dest: (jnp.clip(g - q * each, 0, each - 1), 0, 0)
        )

    return pl.pallas_call(
        body,
        grid_spec=pltpu.PrefetchScalarGridSpec(
            num_scalar_prefetch=1,
            grid=(parts * each,),
            in_specs=[source(q) for q in range(parts)],
            out_specs=pl.BlockSpec((1, rows, cols), lambda g, dest: (dest[g], 0, 0)),
        ),
        out_shape=jax.ShapeDtypeStruct((count, rows, cols), f32),
        compiler_params=pltpu.CompilerParams(vmem_limit_bytes=40 * 1024 * 1024),
        cost_estimate=pl.CostEstimate(flops=0, bytes_accessed=36_000_000, transcendentals=0),
        name="assemble",
    )(dest, *blocks)


def local(
    hidden_in,
    cotangent,
    routes,
    gate_weights,
    gain_attn,
    gain_latent,
    w_query,
    w_latent,
    w_expand,
    w_out,
    gain_moe,
    expert_gate,
    expert_up,
    expert_down,
    shared_gate,
    shared_up,
    shared_down,
):
    fs, cx, tp = lax.axis_size("fsdp"), lax.axis_size("ctx"), lax.axis_size("tp")
    i, j, k = lax.axis_index("fsdp"), lax.axis_index("ctx"), lax.axis_index("tp")
    rows_dev, width = hidden_in.shape
    n = rows_dev // tp
    length = rows_dev * cx
    dpart = width // fs
    q_width = NOPE + ROPE
    kv_width = NOPE + VHEAD
    heads_dev = w_out.shape[0] // VHEAD
    groups = min(cx, heads_dev)
    share = cx // groups
    hd = heads_dev // groups
    group = j // share
    lead = j % share == 0
    scaling = q_width ** (-0.5)
    assert EXPERTS == fs * cx

    members = [0]
    for bit in list(high_bits(cx)) + [1]:
        members = members + [m ^ bit for m in members]
    place_of = [members.index(m) for m in range(cx)]

    def spot(m):
        return jnp.asarray(place_of, jnp.int32)[m]

    def spread_ctx(cur):
        for bit in high_bits(cx):
            cur = jnp.concatenate([cur, exchange(cur, "ctx", bit)], axis=0)
        return cur

    def spread_core(cur):
        return jnp.concatenate([cur, exchange(cur, "ctx", 1)], axis=0)

    def spread_tp(cur):
        for bit in low_bits(tp):
            cur = jnp.concatenate([cur, exchange(cur, "tp", bit)], axis=1)
        return cur

    def gather_halves(own, ctx_first):
        cur = own[None, None]
        cur = spread_tp(spread_ctx(cur)) if ctx_first else spread_ctx(spread_tp(cur))
        return cur, exchange(cur, "ctx", 1)

    def gather_plane(own, ctx_first=True):
        return jnp.concatenate(gather_halves(own, ctx_first), axis=0)

    def gather_ctx(own):
        return spread_core(spread_ctx(own[None]))

    def over_ctx(stack, *pins):
        blocks = [stack]
        for bit in list(high_bits(cx)) + [1]:
            if bit == 1 and pins:
                blocks = [after(block, *pins) for block in blocks]
            blocks = blocks + [exchange(block, "ctx", bit) for block in blocks]
        return blocks

    def reduce_core(keep, send):
        return (keep.astype(f32) + exchange(send, "ctx", 1).astype(f32)).astype(bf16)

    def reduce_lead(cur, axis):
        bits = low_bits(tp) if axis == "tp" else high_bits(cx)
        for bit in sorted(bits, reverse=True):
            at = cur.shape[0] // 2
            other = exchange(cur[at:], axis, bit)
            cur = (cur[:at].astype(f32) + other.astype(f32)).astype(bf16)
        return cur[0]

    def reduce_plane(keep, send, *pins):
        cur = after(reduce_core(keep, send), *pins[:1])
        cur = after(reduce_lead(cur, "tp"), *pins[1:])
        return reduce_lead(cur, "ctx").astype(f32)

    def rel_tp(value):
        blocks = value.reshape((tp, n) + value.shape[1:])
        return jnp.concatenate(
            [lax.dynamic_index_in_dim(blocks, k ^ t, 0, keepdims=False) for t in range(tp)], axis=0
        )

    def own_rows(value):
        return lax.dynamic_slice_in_dim(value, k * n, n, 0)

    def hop(cur, bit):
        cur = cur.reshape((cur.shape[0] // 2, 2) + cur.shape[1:])
        mine = (i // bit) % 2
        send = lax.dynamic_index_in_dim(cur, 1 - mine, 1, keepdims=False).astype(bf16)
        keep = lax.dynamic_index_in_dim(cur, mine, 1, keepdims=False)
        return keep.astype(f32) + exchange(send, "fsdp", bit).astype(f32)

    def hops(cur, bits):
        for bit in bits:
            cur = hop(cur, bit)
        return cur

    def turn(value):
        return lax.all_to_all(value, "fsdp", 0, 0)

    hid_rel = rel_tp(hidden_in)
    x_rel = hid_rel[:n].astype(f32)
    hid_all = gather_ctx(hid_rel).reshape(length, width)
    row = jnp.arange(n, dtype=jnp.int32)
    pos_rel = jnp.concatenate(
        [(j ^ m) * rows_dev + (k ^ t) * n + row for m in members for t in range(tp)]
    )
    cos_rel, sin_rel = angle_tables(pos_rel, ROPE)
    hid_all = after(hid_all, cos_rel, sin_rel)

    lat_cols = w_latent.shape[1] // cx
    query_own = lax.dynamic_slice_in_dim(w_query, group * hd * q_width, hd * q_width, 1)
    latent_own = lax.dynamic_slice_in_dim(w_latent.T, j * lat_cols, lat_cols, 0)
    expand_own = lax.dynamic_slice_in_dim(w_expand, group * hd * kv_width, hd * kv_width, 1)
    out_own = lax.dynamic_slice_in_dim(w_out, group * hd * VHEAD, hd * VHEAD, 0)
    lat_part = gain_latent.shape[0]
    gate_high = lax.reduce_precision(gate_weights, 8, 7)
    gate_low = (gate_weights - gate_high).astype(bf16)
    small = jnp.concatenate(
        [routes.T.astype(bf16), gate_high.T.astype(bf16), gate_low.T], axis=0
    )
    small_rows = -(-small.size // dpart)
    small = rel_tp(small.T).T.reshape(-1)
    small = jnp.pad(small, (0, small_rows * dpart - small.shape[0])).reshape(small_rows, dpart)
    extra = jnp.concatenate(
        [
            gain_attn[None],
            gain_moe[None],
            jnp.pad(gain_latent, (0, dpart - lat_part))[None],
            small,
        ],
        axis=0,
    )
    extra = jnp.pad(extra, ((0, -extra.shape[0] % 16), (0, 0)))
    first_pack = jnp.concatenate([query_own.T, latent_own, extra], axis=0)
    first_pack = after(lax.all_gather(first_pack, "fsdp", axis=0), hid_all)
    q_cols = hd * q_width
    query_t = first_pack[:, :q_cols].transpose(1, 0, 2).reshape(q_cols, width)
    latent_t = first_pack[:, q_cols : q_cols + lat_cols].transpose(1, 0, 2)
    latent_t = gather_ctx(latent_t.reshape(lat_cols, width))
    latent_t = place(
        (cx * lat_cols, width), bf16, list(latent_t), [(j ^ m) * lat_cols for m in members], 0
    )
    extra = first_pack[:, q_cols + lat_cols :]
    gain_norm = extra[:, 0].reshape(-1).astype(f32)
    gain_mix = extra[:, 1].reshape(-1).astype(f32)
    gain_lat = extra[:, 2, :lat_part].reshape(-1).astype(f32)
    small = extra[:, 3 : 3 + small_rows].reshape(fs, -1)[:, : 3 * TOPK * rows_dev]
    small = gather_ctx(small.reshape(fs, 3 * TOPK, rows_dev))
    small = small.transpose(1, 0, 2, 3).reshape(fs * cx, 3 * TOPK, rows_dev).astype(f32)
    ex_rows = expand_own.size // dpart
    second_pack = lax.all_gather(
        after(
            jnp.concatenate([expand_own.reshape(ex_rows, dpart), out_own], axis=0), first_pack
        ),
        "fsdp",
        axis=0,
    )
    second_pack = after(second_pack, latent_t)
    expand_w = second_pack[:, :ex_rows].reshape(-1, hd * kv_width)
    output_w = second_pack[:, ex_rows:].transpose(1, 0, 2).reshape(hd * VHEAD, width)

    dy_own = own_rows(cotangent)
    dy_seqs = lax.all_gather(after(dy_own, second_pack), "fsdp", axis=0)

    sh = shared_gate.shape[1] // (cx * fs)
    shp = -(-sh // 128) * 128
    ffn = expert_down.shape[1]
    cut = j * fs * sh
    gate_w = turn(
        after(
            lax.dynamic_slice_in_dim(expert_gate.transpose(0, 2, 1), j * fs, fs, 0), second_pack
        )
    )
    shared_own = jnp.stack(
        [
            lax.dynamic_slice_in_dim(shared_gate, cut, fs * sh, 1).T.reshape(fs, sh, dpart),
            lax.dynamic_slice_in_dim(shared_up, cut, fs * sh, 1).T.reshape(fs, sh, dpart),
            lax.dynamic_slice_in_dim(shared_down, cut, fs * sh, 0).reshape(fs, sh, dpart),
        ],
        axis=1,
    )

    normed, attn_scale = norm_rows(hid_all.astype(f32), gain_norm)
    normed_all = normed.astype(bf16)
    expert = (j * fs + i).astype(f32)
    named = small[:, :TOPK] == expert
    chosen = jnp.any(named, axis=1).astype(f32)
    gates_all = small[:, TOPK : 2 * TOPK] + small[:, 2 * TOPK :]
    weight = jnp.sum(jnp.where(named, gates_all, 0.0), axis=1)
    ahead = (
        jnp.arange(rows_dev, dtype=jnp.int32)[:, None]
        < jnp.arange(rows_dev, dtype=jnp.int32)[None, :]
    ).astype(bf16)
    earlier = mm(chosen.astype(bf16), ahead).astype(jnp.int32)
    slot_of = jnp.where(chosen > 0.5, earlier, -1).reshape(fs * cx, 1, rows_dev)
    weight = weight.reshape(fs * cx, 1, rows_dev)
    slot_col = slot_of.reshape(fs * cx, rows_dev, 1)
    expand_w = after(expand_w, slot_of, slot_col, weight)

    keep, send, latent_raw, latent_low, queries, expanded, attn_prob, heads_out = attend(
        hd, (tp, cx // 2, n), normed_all, query_t, latent_t, expand_w, output_w, gain_lat, cos_rel, sin_rel, pos_rel
    )
    half = length // 2

    def leading(value):
        return value if share == 1 else jnp.where(lead, value, jnp.zeros((), value.dtype))

    attn_sum = after(reduce_plane(leading(keep), leading(send), dy_seqs), gate_w)
    middle = x_rel + attn_sum
    normed_moe, moe_scale = norm_rows(middle, gain_mix)
    moe_low = normed_moe.astype(bf16)

    per = fs // 2 if fs > 1 else 1
    row_seqs = lax.all_gather(moe_low, "fsdp", axis=0)

    def to_all(seqs, *pins):
        halves = []
        for g in range(fs // per):
            cur = seqs[g * per : (g + 1) * per][None, None]
            if g % 2 == 0:
                cur = spread_ctx(cur)
                cur = spread_tp(after(cur, *pins) if pins else cur)
            else:
                cur = spread_tp(cur)
                cur = spread_ctx(after(cur, *pins) if pins else cur)
            halves += [cur, exchange(cur, "ctx", 1)]
        return halves

    dy_halves = to_all(after(dy_seqs, middle), moe_low)
    up_w = turn(
        after(lax.dynamic_slice_in_dim(expert_up.transpose(0, 2, 1), j * fs, fs, 0), row_seqs)
    )
    row_halves = to_all(after(row_seqs, *dy_halves[::2]))
    shared_w = turn(after(shared_own, up_w))
    down_w = turn(after(lax.dynamic_slice_in_dim(expert_down, j * fs, fs, 0), shared_w))
    shared_w = shared_w.transpose(1, 2, 0, 3).reshape(3, sh, width)
    shared_w = jnp.pad(shared_w, ((0, 0), (0, shp - sh), (0, 0))).reshape(3 * shp, width)


    all_slots, all_dy, gate_act, up_act, shared_ds, d_shared = moe_rows(
        fs, ffn, row_halves, dy_halves, slot_of, shared_w, gate_w, up_w
    )
    me = jnp.zeros((1,), jnp.int32)

    name = (jnp.arange(128, dtype=jnp.int32) == j * fs + i).astype(f32)[None]
    big, flows = [], []
    dy_in = all_dy
    for g in range(fs // per):
        results = moe_back(
            g * per,
            per,
            tp,
            fs,
            g % 2 == 0,
            me,
            dy_in,
            gate_act,
            up_act,
            slot_of,
            slot_col,
            weight,
            shared_ds,
            shared_w,
            gate_w,
            up_w,
            down_w,
            name,
            big,
        )
        big = list(results[:3])
        dy_in = after(all_dy, results[4])
        flows.append(reduce_core(results[3], results[4]))
    all_dg, all_du, all_hw = big

    def split_cols(value):
        return value.reshape(value.shape[0], fs, dpart).transpose(1, 0, 2)

    d_gate_w = weight_grads(after(all_dg, *flows), all_slots, fs)
    gate_back = turn(d_gate_w)
    firsts = [reduce_lead(flow, "ctx" if g % 2 else "tp") for g, flow in enumerate(flows)]
    out_args = (slot_col, shared_ds, shared_w, down_w)
    outs = [
        moe_out(g * per, per, tp, fs, g % 2 == 1, me, after(all_hw, d_gate_w), *out_args)
        for g in range(fs // per)
    ]
    firsts = [after(flow, *outs[0], *outs[-1]) for flow in firsts]
    seconds = [reduce_lead(flow, "tp" if g % 2 else "ctx") for g, flow in enumerate(firsts)]
    home = after(jnp.concatenate(seconds, axis=0), gate_back)
    d_up_w = weight_grads(after(all_du, home), all_slots, fs)
    d_down_w = weight_grads(after(all_hw, home), all_dy, fs, d_shared, sh)
    out_flows = [
        reduce_lead(after(reduce_core(keep, send), home), "ctx" if g % 2 else "tp")
        for g, (keep, send) in enumerate(outs)
    ]
    home_own = jnp.sum(turn(home).astype(f32), axis=0)
    home_own = after(home_own, d_up_w, d_down_w, *out_flows)
    up_back = turn(after(d_up_w, home_own))
    grad_total, gate_cols = home_own[:, :width], home_own[:, width:]
    in_order = jnp.arange(EXPERTS, dtype=jnp.int32)

    def lay_out(blocks):
        return assemble([blocks.reshape(EXPERTS, -1, dpart)], in_order, EXPERTS, ffn)

    grad_mid_norm, d_gain_moe = norm_back(middle, moe_scale, gain_mix, grad_total)
    grad_mid = dy_own.astype(f32) + grad_mid_norm
    grad_low = grad_mid.astype(bf16)
    grad_cur = spread_ctx(grad_low[None, None])
    gate_blocks = lax.all_gather(after(gate_back, grad_cur), "ctx", axis=0)
    grad_all = spread_core(spread_tp(grad_cur)).reshape(length, width)

    down_back = turn(after(d_down_w, up_back))
    gate_shards = lay_out(gate_blocks)
    keep, send, grad_q, grad_expanded = attend_back(
        hd,
        (tp, cx // 2, n),
        grad_all,
        output_w,
        attn_prob,
        heads_out,
        expanded,
        latent_low,
        queries,
        cos_rel,
        sin_rel,
        query_t,
        expand_w,
    )
    up_blocks = lax.all_gather(after(up_back, grad_q), "ctx", axis=0)
    summed = reduce_plane(leading(keep), leading(send), up_back, gate_shards)
    out_flows = [
        reduce_lead(after(flow, summed), "tp" if g % 2 else "ctx")
        for g, flow in enumerate(out_flows)
    ]
    out_home = jnp.concatenate(out_flows, axis=0)
    d_attn, d_w_expand = attend_weights(
        fs, grad_all, heads_out, after(grad_q, send), normed_all, grad_expanded, latent_low
    )
    summed = after(summed, d_attn)
    grad_latent_own = summed[:, width : width + LATENT + ROPE]
    up_shards = lay_out(up_blocks)
    latent_scale = lax.rsqrt(
        jnp.mean(latent_raw[:n, :LATENT] ** 2, axis=-1, keepdims=True) + EPSILON
    )
    grad_lat_raw, d_gain_latent = norm_back(
        latent_raw[:n, :LATENT], latent_scale, gain_lat, grad_latent_own[:, :LATENT]
    )
    grad_kv_raw = jnp.concatenate(
        [grad_lat_raw, rotate_back(grad_latent_own[:, LATENT:], cos_rel[:n], sin_rel[:n])], axis=1
    ).astype(bf16)
    grad_normed = summed[:, :width] + mm(grad_kv_raw, latent_t)
    kv_all = gather_plane(grad_kv_raw).reshape(length, -1)
    d_w_latent = mm_tn(
        lax.dynamic_slice_in_dim(kv_all, j * lat_cols, lat_cols, 1), normed_all
    ).astype(bf16)
    ex_part = d_w_expand.size // (fs * dpart)
    pack = jnp.concatenate(
        [d_attn, d_w_expand.reshape(fs, ex_part, dpart), split_cols(d_w_latent)], axis=1
    )
    bits = list(low_bits(fs))
    pack_sum = hops(pack, bits[:1])
    out_sum = hops(after(out_home, pack_sum), bits[:1])
    pack_sum = after(pack_sum, up_shards)
    pack_total = hops(pack_sum, bits[1:])[0]
    out_total = hops(after(out_sum, pack_total), bits[1:])[0]
    down_blocks = lax.all_gather(after(down_back, d_w_latent), "ctx", axis=0)
    grad_x_norm, d_gain_attn = norm_back(x_rel, attn_scale[:n], gain_norm, grad_normed)
    input_own = (grad_mid + grad_x_norm).astype(bf16)
    input_grad = rel_tp(spread_tp(input_own[None, None]).reshape(rows_dev, width)).astype(f32)

    out_own_rows = (middle + out_total).astype(bf16)
    layer_out = rel_tp(spread_tp(out_own_rows[None, None]).reshape(rows_dev, width))

    gate_cols = spread_tp(gate_cols[:, :EXPERTS][None, None]).reshape(rows_dev, EXPERTS)
    gate_cols = rel_tp(gate_cols)
    experts = jnp.arange(EXPERTS, dtype=jnp.int32)
    gates_grad = jnp.sum(
        jnp.where(routes[:, :, None] == experts, gate_cols[:, None, :], 0.0), axis=-1
    )

    blocks = over_ctx(pack_total.astype(bf16))
    gain_pin = blocks[1]
    at_q, at_e = hd * VHEAD, hd * VHEAD + q_cols
    by_group = [(j ^ m) // share for m in members]
    w_out_grad = place(
        w_out.shape, f32, [v[:at_q] for v in blocks], [g * hd * VHEAD for g in by_group], 0
    )
    w_query_grad = place(
        w_query.shape[::-1], f32, [v[at_q:at_e] for v in blocks], [g * q_cols for g in by_group], 0
    ).T
    w_expand_grad = place(
        w_expand.shape,
        f32,
        [
            v[at_e : at_e + ex_part].reshape(w_expand.shape[0], hd * kv_width) for v in blocks
        ],
        [g * hd * kv_width for g in by_group],
        1,
    )
    w_latent_grad = place(
        w_latent.shape[::-1],
        f32,
        [v[at_e + ex_part :] for v in blocks],
        [(j ^ m) * lat_cols for m in members],
        0,
    ).T

    gain_parts = jnp.concatenate(
        [
            d_gain_attn.reshape(fs, -1),
            d_gain_moe.reshape(fs, -1),
            d_gain_latent.reshape(fs, -1),
        ],
        axis=1,
    )
    gain_sum = jnp.sum(turn(after(gain_parts[:, None, :], gain_pin)), axis=0)
    for bit in low_bits(tp):
        gain_sum = gain_sum + exchange(gain_sum, "tp", bit)
    for bit in low_bits(cx):
        gain_sum = gain_sum + exchange(gain_sum, "ctx", bit)
    gain_sum = gain_sum[0]
    cut_a, cut_b = gain_attn.shape[0], gain_attn.shape[0] + gain_moe.shape[0]

    expert_gate_grad = gate_shards.transpose(0, 2, 1)
    expert_up_grad = up_shards.transpose(0, 2, 1)
    expert_down_grad = lay_out(down_blocks)
    shared_grads = down_blocks[:, :, ffn:].reshape(cx, fs, 3, sh, dpart).transpose(2, 0, 1, 3, 4)
    shared_grads = shared_grads.reshape(3, cx * fs * sh, dpart).astype(f32)
    shared_gate_grad = shared_grads[0].T
    shared_up_grad = shared_grads[1].T
    shared_down_grad = shared_grads[2]

    return (
        layer_out,
        input_grad,
        gates_grad,
        gain_sum[:cut_a],
        gain_sum[cut_b:],
        w_query_grad,
        w_latent_grad,
        w_expand_grad,
        w_out_grad,
        gain_sum[cut_a:cut_b],
        expert_gate_grad,
        expert_up_grad,
        expert_down_grad,
        shared_gate_grad,
        shared_up_grad,
        shared_down_grad,
    )


def solution(mesh):
    placed = (
        P(("fsdp", "ctx"), None),
        P(("fsdp", "ctx"), None),
        P(("fsdp", "ctx"), None),
        P(("fsdp", "ctx"), None),
        P("fsdp"),
        P("fsdp"),
        P("fsdp", "tp"),
        P("fsdp", None),
        P("fsdp", "tp"),
        P("tp", "fsdp"),
        P("fsdp"),
        P(None, "fsdp", "tp"),
        P(None, "fsdp", "tp"),
        P(None, "tp", "fsdp"),
        P("fsdp", "tp"),
        P("fsdp", "tp"),
        P("tp", "fsdp"),
    )
    return jax.shard_map(
        local,
        mesh=mesh,
        in_specs=placed,
        out_specs=(
            P(("fsdp", "ctx"), None),
            P(("fsdp", "ctx"), None),
            P(("fsdp", "ctx"), None),
            P("fsdp"),
            P("fsdp"),
            P("fsdp", "tp"),
            P("fsdp", None),
            P("fsdp", "tp"),
            P("tp", "fsdp"),
            P("fsdp"),
            P(None, "fsdp", "tp"),
            P(None, "fsdp", "tp"),
            P(None, "tp", "fsdp"),
            P("fsdp", "tp"),
            P("fsdp", "tp"),
            P("tp", "fsdp"),
        ),
        check_vma=False,
    )
```
